32 devices in a mesh: seq: 8 (over z, y), mp: 4 (over x, core).
Axes of the slice: x: 2, y: 2, z: 4, core: 2. Of those that a mesh axis runs over, the one named last changes fastest.
Arguments:
- inputs: bfloat16 [2048, 2560], P('seq'), may hold values from -6 to 6
- targets: bfloat16 [2048, 2560], P('seq'), may hold values from -6 to 6
- seq_ids: int32 [2048], P('seq'), may hold values from 0 to 1, as said below
- block_ids: int32 [2048], P('seq'), may hold values from 0 to 4, as said below
- attn_gain: bfloat16 [2560], P('seq'), may hold values from 0.5 to 1.5
- mlp_gain: bfloat16 [2560], P('seq'), may hold values from 0.5 to 1.5
- w_query: bfloat16 [2560, 2560], P('seq', 'mp'), may hold values from -0.125 to 0.125
- w_key: bfloat16 [2560, 640], P('seq', 'mp'), may hold values from -0.125 to 0.125
- w_value: bfloat16 [2560, 640], P('seq', 'mp'), may hold values from -0.125 to 0.125
- w_out: bfloat16 [2560, 2560], P('seq', 'mp'), may hold values from -2.5 to 2.5
- w_gate: bfloat16 [2560, 7168], P('seq', 'mp'), may hold values from -0.125 to 0.125
- w_up: bfloat16 [2560, 7168], P('seq', 'mp'), may hold values from -0.125 to 0.125
- w_down: bfloat16 [2560, 7168], P('seq', 'mp'), may hold values from -0.0625 to 0.0625
Outputs:
- layer_out: bfloat16 [2048, 2560], P('seq')
- input_grad: bfloat16 [2048, 2560], P('seq')
- grad_query: float32 [2560, 2560], P('seq', 'mp')
- grad_key: float32 [2560, 640], P('seq', 'mp')
- grad_value: float32 [2560, 640], P('seq', 'mp')
- grad_out: float32 [2560, 2560], P('seq', 'mp')
- grad_gate: float32 [2560, 7168], P('seq', 'mp')
- grad_up: float32 [2560, 7168], P('seq', 'mp')
- grad_down: float32 [2560, 7168], P('seq', 'mp')
- grad_attn_gain: float32 [2560], P('seq')
- grad_mlp_gain: float32 [2560], P('seq')
- rms_stream: float32 [], replicated
- rms_attn: float32 [], replicated
- rms_mlp: float32 [], replicated
The draws below stay inside these ranges and needn't reach their ends.
Inputs may be any that keep to these rules, and one draw needn't show every extreme that they name: `seq_ids`: every index of seq holds 2 runs of 128 rows, one run of each sequence, in an order drawn for each index; the run of a sequence on index i holds its positions i * 128 to i * 128 + 127. `block_ids`: along a sequence's positions the block never falls, and no block holds more than 256 positions.
All inputs are finite; a program needn't handle non-finite values.
Results may differ from the reference program's by a relative error of at most 0.017.
Values may be sent and summed in bfloat16 or wider, within the bound.
No kernel may reach another device: no remote copies, remote signals or barrier semaphores. Data moves between devices by JAX's collectives and lax.ppermute only.
A program may use at most 192 MiB of HBM per device.

```python
import jax
import jax.numpy as jnp
from jax import lax

D = 2560
KV_HEADS = 8
HEAD_DIM = 80
FF = 7168
TOK_DEV = 256
SPAN = 128
BLOCK = 256
GROUP = 4
QW = 2560
KW = 640
SEQS = 2
LENGTH = 1024
TOKENS = 2048


def sequence_labels(key):
    devices = TOKENS // TOK_DEV
    keys = jax.random.split(key, devices)
    orders = jax.vmap(lambda single: jax.random.permutation(single, SEQS))(keys)
    return jnp.repeat(orders, SPAN, axis=1).reshape(TOKENS).astype(jnp.int32)


def draw_seq_ids(key, part):
    labels = sequence_labels(key)
    return labels


def draw_block_ids(key, part):
    labels = sequence_labels(key)
    key = jax.random.fold_in(key, 7)
    offsets = jax.random.randint(key, (SEQS,), 1, BLOCK)
    token = jnp.arange(TOKENS, dtype=jnp.int32)
    place = token // TOK_DEV * SPAN + token % SPAN
    return ((place + offsets[labels]) // BLOCK).astype(jnp.int32)


def shard_levels(own_key, dims, shards, low, high):
    def one(position, parts):
        draws = jax.random.uniform(jax.random.fold_in(jax.random.fold_in(own_key, 6), position), (parts,), jnp.float32, low / len(shards), high / len(shards))
        return jnp.repeat(jnp.exp(draws), dims[position] // parts).reshape((-1,) + (1,) * (len(dims) - position - 1))

    factor_of = one(*shards[0])
    for cut in shards[1:]:
        factor_of = factor_of * one(*cut)
    return factor_of


def gaussian(stream_key, dims, scale, most, cuts=(), kind=jnp.bfloat16):
    values = jax.random.normal(stream_key, dims, jnp.float32) * scale
    if len(cuts) > 0:
        values = shard_levels(stream_key, dims, cuts, -0.22, 0.18) * values
    return jnp.clip(values, min=-most, max=most).astype(kind)


def setup_inputs(seed: int = 0) -> dict:
    streams_of = jax.random.split(jax.random.key(seed), 14)
    inputs = gaussian(streams_of[0], (TOKENS, D), 1.0, 6.0, ((0, 8),))
    targets = gaussian(streams_of[1], (TOKENS, D), 1.0, 6.0, ((0, 8),))
    seq_ids = draw_seq_ids(jax.random.fold_in(streams_of[13], 71), 0)
    block_ids = draw_block_ids(jax.random.fold_in(streams_of[13], 71), 0)
    attn_gain = jnp.clip(1.0 + 0.1 * jax.random.normal(streams_of[4], (D,), jnp.float32), 0.5, 1.5).astype(jnp.bfloat16)
    mlp_gain = jnp.clip(1.0 + 0.1 * jax.random.normal(streams_of[5], (D,), jnp.float32), 0.5, 1.5).astype(jnp.bfloat16)
    w_query = gaussian(streams_of[6], (D, QW), D ** -0.5, 0.125, ((0, 8), (1, 4)))
    w_key = gaussian(streams_of[7], (D, KW), D ** -0.5, 0.125, ((0, 8), (1, 4)))
    w_value = gaussian(streams_of[8], (D, KW), D ** -0.5, 0.125, ((0, 8), (1, 4)))
    w_out = gaussian(streams_of[9], (D, QW), 6 ** -0.5, 2.5, ((0, 8), (1, 4)))
    w_gate = gaussian(streams_of[10], (D, FF), D ** -0.5, 0.125, ((0, 8), (1, 4)))
    w_up = gaussian(streams_of[11], (D, FF), D ** -0.5, 0.125, ((0, 8), (1, 4)))
    w_down = gaussian(streams_of[12], (D, FF), FF ** -0.5, 0.0625, ((0, 8), (1, 4)))
    return dict(inputs=inputs, targets=targets, seq_ids=seq_ids, block_ids=block_ids, attn_gain=attn_gain, mlp_gain=mlp_gain, w_query=w_query, w_key=w_key, w_value=w_value, w_out=w_out, w_gate=w_gate, w_up=w_up, w_down=w_down)


EPS = 1e-05
THETA = 1000000.0

@jax.custom_vjp
def low(v):
    return lax.optimization_barrier(v.astype(jnp.bfloat16)).astype(jnp.float32)

@jax.custom_vjp
def low_back(v):
    return v

def low_keep(v):
    return (low(v), None)

def low_pass(kept, grad):
    return (grad,)

def back_keep(v):
    return (v, None)

def back_low(kept, grad):
    return (low(grad),)
low.defvjp(low_keep, low_pass)
low_back.defvjp(back_keep, back_low)

def matmul(left, right):
    return jnp.dot(left, right, precision=lax.Precision.HIGHEST)

def normed(value, gain):
    return value * lax.rsqrt(lax.optimization_barrier(jnp.mean(value * value, axis=-1, keepdims=True)) + EPS) * gain

def tables(place):
    half = HEAD_DIM // 2
    freq = THETA ** (-(jnp.arange(half, dtype=jnp.float32) * 2.0 / HEAD_DIM))
    angle = place[:, None] * freq[None, :]
    return (jnp.cos(angle), jnp.sin(angle))

def rotate(values, cosine, sine):
    count = values.shape[0]
    heads = values.reshape(count, -1, HEAD_DIM)
    half = HEAD_DIM // 2
    first = heads[..., :half]
    second = heads[..., half:]
    cosine = cosine[:, None, :]
    sine = sine[:, None, :]
    turned = jnp.concatenate([first * cosine - second * sine, second * cosine + first * sine], axis=-1)
    return turned.reshape(count, -1)

def attend_one(query, key, value, blocks):
    width = min(512, LENGTH)
    count = LENGTH // width
    query_blocks = query.reshape(count, width, KV_HEADS, GROUP, HEAD_DIM)
    block_rows = blocks.reshape(count, width)

    def step(pair):
        qblock, bblock = pair
        scores = jnp.einsum('qhgd,khd->qhgk', qblock, key, precision=lax.Precision.HIGHEST) * HEAD_DIM ** (-0.5)
        scores = low_back(scores)
        visible = bblock[:, None] >= blocks[None, :]
        scores = jnp.where(visible[:, None, None, :], scores, -1e+30)
        probs = low(jax.nn.softmax(scores, axis=-1))
        return jnp.einsum('qhgk,khd->qhgd', probs, value, precision=lax.Precision.HIGHEST)
    mixed = lax.map(jax.checkpoint(step), (query_blocks, block_rows))
    return mixed.reshape(LENGTH, QW)

def reference(inputs, targets, seq_ids, block_ids, attn_gain, mlp_gain, w_query, w_key, w_value, w_out, w_gate, w_up, w_down):
    token = jnp.arange(TOKENS, dtype=jnp.int32)
    place = (token // TOK_DEV * SPAN + token % SPAN).astype(jnp.float32)
    cosine, sine = tables(place)
    order = jnp.argsort(seq_ids * TOKENS + token).astype(jnp.int32)
    inverse = jnp.argsort(order).astype(jnp.int32)
    sorted_blocks = block_ids[order].reshape(SEQS, LENGTH)

    def layer(xin, gain_one, gain_two, wq, wk, wv, wo, wg, wu, wd):
        first = low(normed(xin, gain_one))
        query = low_back(matmul(first, wq))
        key = low_back(matmul(first, wk))
        value = low_back(matmul(first, wv))
        query_r = low(rotate(query, cosine, sine))
        key_r = low(rotate(key, cosine, sine))
        value_r = low(value)
        query_s = query_r[order].reshape(SEQS, LENGTH, KV_HEADS, GROUP, HEAD_DIM)
        key_s = key_r[order].reshape(SEQS, LENGTH, KV_HEADS, HEAD_DIM)
        value_s = value_r[order].reshape(SEQS, LENGTH, KV_HEADS, HEAD_DIM)
        mixed = lax.map(lambda group: attend_one(group[0], group[1], group[2], group[3]), (query_s, key_s, value_s, sorted_blocks))
        mixed = mixed.reshape(TOKENS, QW)[inverse]
        mixed = low(low_back(mixed))
        branch_attn = low_back(matmul(mixed, wo.T))
        middle = xin + branch_attn
        second = low(normed(middle, gain_two))
        gate = low_back(matmul(second, wg))
        upper = low_back(matmul(second, wu))
        hidden = low(jax.nn.silu(gate) * upper)
        branch_mlp = low_back(matmul(hidden, wd.T))
        stream = low_back(middle + branch_mlp)
        stats = (jnp.sqrt(jnp.mean(stream * stream) + EPS), jnp.sqrt(jnp.mean(branch_attn * branch_attn) + EPS), jnp.sqrt(jnp.mean(branch_mlp * branch_mlp) + EPS))
        return (stream, stats)
    values = (inputs, attn_gain, mlp_gain, w_query, w_key, w_value, w_out, w_gate, w_up, w_down)
    values = tuple((item.astype(jnp.float32) for item in values))
    stream, pullback, stats = jax.vjp(layer, *values, has_aux=True)
    grads = pullback(stream - targets.astype(jnp.float32))
    return (stream.astype(jnp.bfloat16), grads[0].astype(jnp.bfloat16), grads[3], grads[4], grads[5], grads[6], grads[7], grads[8], grads[9], grads[1], grads[2], stats[0], stats[1], stats[2])
```

```python
import jax
import jax.numpy as jnp
from jax import lax
from jax.sharding import PartitionSpec as P

HEAD_DIM = 80
SPAN = 128
EPS = 1e-05
THETA = 1000000.0
SEQS = 2
PARTS = 4
BF = jnp.bfloat16
F32 = jnp.float32

LAST = (((1,), (1,)), ((), ()))
ROWS = (((0,), (0,)), ((), ()))


def hop(value, axis, k):
    size = lax.axis_size(axis)
    return lax.ppermute(value, axis, [(i, i ^ k) for i in range(size)])


def dot(left, right, dims=(((1,), (0,)), ((), ()))):
    return lax.dot_general(left, right, dims, preferred_element_type=F32)


class Place:
    def __init__(self):
        self.inner = lax.axis_size("seq") // PARTS
        s = lax.axis_index("seq")
        m = lax.axis_index("mp")
        self.z = s // self.inner
        self.y = s % self.inner
        self.x = m // 2
        self.c = m % 2
        self.bits = []
        b = 1
        while b < self.inner:
            self.bits.append(b)
            b *= 2

    def hop_z(self, v, k):
        return hop(v, "seq", k * self.inner)

    def hop_y(self, v, b):
        return hop(v, "seq", b)

    def hop_x(self, v):
        return hop(v, "mp", 2)

    def hop_c(self, v):
        return hop(v, "mp", 1)

    def features_in(self, v):
        rows = v.shape[0]
        r = v.shape[1] // (PARTS * self.inner)
        v = v.reshape(rows, PARTS, self.inner, r).transpose(0, 2, 1, 3)
        return self.flip_y(v).reshape(rows, -1)

    def features_out(self, v):
        rows = v.shape[0]
        r = v.shape[1] // (PARTS * self.inner)
        v = self.flip_y(v.reshape(rows, self.inner, PARTS, r))
        return v.transpose(0, 2, 1, 3).reshape(rows, -1)

    def flip_y(self, v):
        for b in self.bits:
            w = v.reshape((v.shape[0], self.inner // (2 * b), 2, b) + v.shape[2:])
            w = w[:, :, ::-1].reshape(v.shape)
            v = jnp.where((self.y // b) % 2 == 1, w, v)
        return v

    def swap_z(self, pieces):
        got = []
        for k in range(PARTS):
            piece = lax.dynamic_index_in_dim(pieces, self.z ^ k, 0, keepdims=False)
            got.append(self.hop_z(piece, k) if k else piece)
        out = jnp.zeros(pieces.shape, pieces.dtype)
        for k in range(PARTS):
            out = lax.dynamic_update_index_in_dim(out, got[k], self.z ^ k, 0)
        return out

    def spread(self, buf):
        half = PARTS // 2

        def spread_y(v):
            for b in self.bits:
                v = jnp.concatenate([v, self.hop_y(v, b)], 0)
            return v

        first = spread_y(buf[None, :half])
        first = (first, self.hop_x(first))
        second = (buf[None, half:], self.hop_x(buf[None, half:]))
        second = tuple(spread_y(v) for v in second)
        return [
            jnp.concatenate([first[i], second[i]], 1).reshape(-1, buf.shape[-1]) for i in range(2)
        ]

    def collect(self, grads):
        half = PARTS // 2
        cols = grads[0].shape[-1]
        parts = [g.reshape(self.inner, PARTS, -1, cols) for g in grads]

        def collect_y(v):
            for b in reversed(self.bits):
                got = self.hop_y(v[b:], b)
                v = (v[:b].astype(F32) + got.astype(F32)).astype(BF)
            return v

        def collect_x(own, other):
            return (own.astype(F32) + self.hop_x(other).astype(F32)).astype(BF)

        first = collect_y(collect_x(parts[0][:, :half], parts[1][:, :half]))
        second = collect_x(collect_y(parts[0][:, half:]), collect_y(parts[1][:, half:]))
        return jnp.concatenate([first[0], second[0]], 0)

    def gather(self, own):
        one = self.hop_z(own, 1)
        two = self.hop_z(own, 2)
        three = self.hop_z(two, 1)
        mine = jnp.concatenate([own, one, two, three], 0)
        return mine, self.hop_c(mine)

    def scatter(self, mine, theirs):
        got = self.hop_c(theirs.astype(BF))
        both = mine + got.astype(F32)
        n = both.shape[0] // PARTS
        piece = [both[k * n : (k + 1) * n] for k in range(PARTS)]
        three = self.hop_z(piece[3].astype(BF), 1)
        two = self.hop_z((piece[2] + three.astype(F32)).astype(BF), 2)
        one = self.hop_z(piece[1].astype(BF), 1)
        return piece[0] + one.astype(F32) + two.astype(F32)


def tables(place):
    half = HEAD_DIM // 2
    freq = THETA ** (-(jnp.arange(half, dtype=F32) * 2.0 / HEAD_DIM))
    angle = place[:, None] * freq[None, :]
    return (jnp.cos(angle), jnp.sin(angle))


def rotate(values, cosine, sine, sign):
    count = values.shape[0]
    heads = values.reshape(count, -1, HEAD_DIM)
    half = HEAD_DIM // 2
    first = heads[..., :half]
    second = heads[..., half:]
    cosine = cosine[:, None, :]
    sine = sine[:, None, :] * sign
    turned = jnp.concatenate(
        [first * cosine - second * sine, second * cosine + first * sine], axis=-1
    )
    return turned.reshape(count, -1)


def scale_of(value):
    return lax.rsqrt(jnp.mean(value * value, axis=-1, keepdims=True) + EPS)


def norm_back(grad, value, scale, gain):
    unit = value * scale
    scaled = grad * gain
    back = scale * (scaled - unit * jnp.mean(scaled * unit, axis=-1, keepdims=True))
    return unit, back


def on_device(
    inputs,
    targets,
    seq_ids,
    block_ids,
    attn_gain,
    mlp_gain,
    w_query,
    w_key,
    w_value,
    w_out,
    w_gate,
    w_up,
    w_down,
):
    at = Place()
    inner = at.inner
    depth = w_query.shape[0]
    half_span = SPAN // 2
    kw = w_key.shape[1] // 2
    qw = w_query.shape[1] // PARTS
    fw = w_gate.shape[1] // PARTS

    def split(w):
        return w.reshape(depth, PARTS, -1).transpose(1, 0, 2)

    def split_kv(w):
        w = w.reshape(depth, 2, kw).transpose(1, 0, 2)
        return jnp.repeat(w, 2, axis=0)

    gains = jnp.broadcast_to(
        jnp.stack([attn_gain, mlp_gain], -1)[None], (PARTS, depth, 2)
    )
    pack_qkv = jnp.concatenate([split(w_query), split_kv(w_key), split_kv(w_value), gains], 2)
    pack_out = split(w_out)
    pack_up = jnp.concatenate([split(w_gate), split(w_up)], 2)
    pack_down = split(w_down)

    off = jnp.where(seq_ids[0] == at.x, 0, SPAN)
    row0 = off + at.c * half_span

    def own_rows(v):
        return at.features_in(lax.dynamic_slice_in_dim(v, row0, half_span, 0))

    x_own = own_rows(inputs)
    t_own = own_rows(targets).astype(F32)

    x_mine, x_theirs = at.gather(x_own)
    w_qkv = at.spread(at.swap_z(pack_qkv))
    ids = lax.dynamic_slice_in_dim(block_ids, off, SPAN, 0)
    ids = jnp.stack([ids] + [at.hop_z(ids, k) for k in range(1, PARTS)], 0)
    ids = ids.reshape(PARTS, 2, half_span).transpose(1, 0, 2)
    ids = jnp.where(at.c == 1, ids[::-1], ids).reshape(-1)
    key_ids = ids[None]
    for b in at.bits:
        key_ids = jnp.concatenate([key_ids, at.hop_y(key_ids, b)], 0)
    key_ids = key_ids.reshape(-1)

    w_o = at.spread(at.swap_z(pack_out))
    w_gu = at.spread(at.swap_z(pack_up))
    w_d = at.spread(at.swap_z(pack_down))

    gain = w_qkv[0][:, qw + 2 * kw :].astype(F32)
    gain_one = gain[:, 0][None]
    gain_two = gain[:, 1][None]

    x_all = jnp.concatenate([x_mine, x_theirs], 0).astype(F32)
    rows = x_all.shape[0]
    scale_one = scale_of(x_all)
    first = (x_all * scale_one * gain_one).astype(BF)
    count = jnp.arange(rows, dtype=jnp.int32)
    zz = at.z ^ ((count // half_span) % PARTS)
    cc = at.c ^ (count // (half_span * PARTS))
    place = ((zz * inner + at.y) * SPAN + cc * half_span + count % half_span).astype(F32)
    cosine, sine = tables(place)

    qkv = [dot(first, w[:, : qw + 2 * kw]) for w in w_qkv]
    query_r = [rotate(v[:, :qw], cosine, sine, 1.0).astype(BF) for v in qkv]
    key_r = [rotate(v[:, qw : qw + kw], cosine, sine, 1.0).astype(BF) for v in qkv]
    value_r = [v[:, qw + kw :].astype(BF) for v in qkv]
    kv = jnp.stack(key_r + value_r, 0)
    for b in at.bits:
        kv = jnp.concatenate([kv, at.hop_y(kv, b)], 1)
    keys = kv[:2]
    values = kv[2:]
    group = qw // HEAD_DIM
    queries = jnp.stack([v.reshape(rows, group, HEAD_DIM).transpose(1, 0, 2) for v in query_r], 0)
    factor = HEAD_DIM**-0.5
    visible = (key_ids[None, :] <= ids[:, None])[None, None]
    scores = jnp.einsum("xgqd,xkd->xgqk", queries, keys, preferred_element_type=F32) * factor
    masked = jnp.where(visible, scores, -1e30)
    top = masked.max(axis=-1, keepdims=True)
    weights = jnp.exp(masked - top)
    total = weights.sum(axis=-1, keepdims=True)
    lse = top + jnp.log(total)
    probs = jnp.where(visible, jnp.exp(scores - lse), 0.0)
    probs_b = probs.astype(BF)
    mixed_f = jnp.einsum("xgqk,xkd->xgqd", probs_b, values, preferred_element_type=F32)
    mixed = mixed_f.astype(BF).transpose(0, 2, 1, 3).reshape(2, rows, qw)

    def two_sides(v):
        n = rows // 2
        return v[:n], v[n:]

    partial = dot(mixed[0], w_o[0], LAST) + dot(mixed[1], w_o[1], LAST)
    branch_attn = at.scatter(*two_sides(partial))
    middle = x_own.astype(F32) + branch_attn
    scale_two = scale_of(middle)
    second_own = (middle * scale_two * gain_two).astype(BF)
    second = jnp.concatenate(at.gather(second_own), 0)
    gate_up = [dot(second, w) for w in w_gu]
    gate = [v[:, :fw] for v in gate_up]
    upper = [v[:, fw:] for v in gate_up]
    sigma = [jax.nn.sigmoid(g) for g in gate]
    silu = [g * s for g, s in zip(gate, sigma)]
    hidden = [(a * b).astype(BF) for a, b in zip(silu, upper)]
    partial = dot(hidden[0], w_d[0], LAST) + dot(hidden[1], w_d[1], LAST)
    branch_mlp = at.scatter(*two_sides(partial))
    stream = middle + branch_mlp

    sums = jnp.stack(
        [jnp.sum(stream * stream), jnp.sum(branch_attn * branch_attn), jnp.sum(branch_mlp * branch_mlp)]
    )
    sums = jnp.broadcast_to(sums[:, None], (3, 128))
    sums = sums + at.hop_c(sums)
    sums = sums + at.hop_x(sums)
    for b in at.bits:
        sums = sums + at.hop_y(sums, b)
    sums = sums + at.hop_z(sums, 1)
    sums = sums + at.hop_z(sums, 2)
    entries = inputs.shape[0] * lax.axis_size("seq") * inputs.shape[1]
    rms = jnp.sqrt(sums[:, 0] / entries + EPS)

    d_out_own = (stream - t_own).astype(BF)
    d_out = jnp.concatenate(at.gather(d_out_own), 0)
    grad_down = [dot(d_out, h, ROWS).astype(BF) for h in hidden]
    d_hidden = [dot(d_out, w) for w in w_d]
    d_gate_up = [
        jnp.concatenate(
            [
                (d * u * s * (1.0 + g * (1.0 - s))).astype(BF),
                (d * sg).astype(BF),
            ],
            1,
        )
        for d, u, s, g, sg in zip(d_hidden, upper, sigma, gate, silu)
    ]
    partial = dot(d_gate_up[0], w_gu[0], LAST) + dot(d_gate_up[1], w_gu[1], LAST)
    d_second = at.scatter(*two_sides(partial))
    grad_gu = [dot(second, d, ROWS).astype(BF) for d in d_gate_up]
    unit, back = norm_back(d_second, middle, scale_two, gain_two)
    grad_gain_two = jnp.sum(d_second * unit, axis=0)
    d_middle = d_out_own.astype(F32) + back
    d_attn = jnp.concatenate(at.gather(d_middle.astype(BF)), 0)
    grad_o = [dot(d_attn, mixed[i], ROWS).astype(BF) for i in range(2)]
    d_mix = [dot(d_attn, w).astype(BF) for w in w_o]
    d_heads = jnp.stack([v.reshape(rows, group, HEAD_DIM).transpose(1, 0, 2) for v in d_mix], 0)
    delta = jnp.sum(d_heads.astype(F32) * mixed_f, axis=-1, keepdims=True)
    d_probs = jnp.einsum("xgqd,xkd->xgqk", d_heads, values, preferred_element_type=F32)
    d_scores = (probs * (d_probs - delta)).astype(BF)
    d_query = jnp.einsum("xgqk,xkd->xgqd", d_scores, keys, preferred_element_type=F32) * factor
    d_keys = jnp.einsum("xgqk,xgqd->xkd", d_scores, queries, preferred_element_type=F32) * factor
    d_values = jnp.einsum("xgqk,xgqd->xkd", probs_b, d_heads, preferred_element_type=F32)
    d_kv = jnp.concatenate([d_keys, d_values], 0).reshape(4, inner, rows, HEAD_DIM)
    for b in reversed(at.bits):
        got = at.hop_y(d_kv[:, b:].astype(BF), b)
        d_kv = d_kv[:, :b] + got.astype(F32)
    d_kv = d_kv[:, 0]
    d_qkv = []
    for i in range(2):
        d_q = d_query[i].transpose(1, 0, 2).reshape(rows, qw)
        d_qkv.append(
            jnp.concatenate(
                [
                    rotate(d_q, cosine, sine, -1.0),
                    rotate(d_kv[i], cosine, sine, -1.0),
                    d_kv[2 + i],
                ],
                1,
            ).astype(BF)
        )
    partial = sum(dot(d, w[:, : qw + 2 * kw], LAST) for d, w in zip(d_qkv, w_qkv))
    d_first = at.scatter(*two_sides(partial))
    grad_gain_one = jnp.sum(partial * (x_all * scale_one), axis=0)
    grad_qkv = [dot(first, d, ROWS).astype(BF) for d in d_qkv]
    gain_grads = jnp.stack([grad_gain_one, grad_gain_two], -1).astype(BF)
    grad_qkv = [jnp.concatenate([g, gain_grads], 1) for g in grad_qkv]

    x_f = x_own.astype(F32)
    unit, back = norm_back(d_first, x_f, scale_of(x_f), gain_one)
    input_grad_own = (d_middle + back).astype(BF)

    def whole_rows(own):
        v = at.features_out(own)
        other = at.hop_c(v)
        v = jnp.where(at.c == 0, jnp.concatenate([v, other], 0), jnp.concatenate([other, v], 0))
        other = at.hop_x(v)
        return jnp.where(off == 0, jnp.concatenate([v, other], 0), jnp.concatenate([other, v], 0))

    layer_out = whole_rows(stream.astype(BF))
    input_grad = whole_rows(input_grad_own)

    def joined(pieces):
        return pieces.astype(F32).transpose(1, 0, 2).reshape(depth, -1)

    got_down = at.swap_z(at.collect(grad_down))
    got_gu = at.swap_z(at.collect(grad_gu))
    got_out = at.swap_z(at.collect(grad_o))
    got_qkv = at.swap_z(at.collect(grad_qkv))
    kv_got = got_qkv[:, :, qw:].astype(F32)
    kv_sum = kv_got.reshape(2, 2, depth, -1).sum(1)
    gains_sum = kv_sum[:, :, 2 * kw :].sum(0)
    gains_sum = gains_sum + at.hop_c(gains_sum)
    return (
        layer_out,
        input_grad,
        joined(got_qkv[:, :, :qw]),
        joined(kv_sum[:, :, :kw]),
        joined(kv_sum[:, :, kw : 2 * kw]),
        joined(got_out),
        joined(got_gu[:, :, :fw]),
        joined(got_gu[:, :, fw:]),
        joined(got_down),
        gains_sum[:, 0],
        gains_sum[:, 1],
        rms[0],
        rms[1],
        rms[2],
    )


def solution(mesh):
    return jax.shard_map(
        on_device,
        mesh=mesh,
        in_specs=(
            P("seq", None),
            P("seq", None),
            P("seq"),
            P("seq"),
            P("seq"),
            P("seq"),
            P("seq", "mp"),
            P("seq", "mp"),
            P("seq", "mp"),
            P("seq", "mp"),
            P("seq", "mp"),
            P("seq", "mp"),
            P("seq", "mp"),
        ),
        out_specs=(
            P("seq", None),
            P("seq", None),
            P("seq", "mp"),
            P("seq", "mp"),
            P("seq", "mp"),
            P("seq", "mp"),
            P("seq", "mp"),
            P("seq", "mp"),
            P("seq", "mp"),
            P("seq"),
            P("seq"),
            P(),
            P(),
            P(),
        ),
        check_vma=False,
    )
```

```python
import functools

import jax
import jax.numpy as jnp
from jax import lax
from jax.experimental import pallas as pl
from jax.experimental.pallas import tpu as pltpu
from jax.sharding import PartitionSpec as P

HEAD_DIM = 80
SPAN = 128
EPS = 1e-05
THETA = 1000000.0
PARTS = 4
BF = jnp.bfloat16
F32 = jnp.float32
FACTOR = HEAD_DIM**-0.5
LOG2E = 1.4426950408889634
LIMIT = 56 * 1024 * 1024

PLAIN = (((1,), (0,)), ((), ()))
LAST = (((1,), (1,)), ((), ()))
ROWS = (((0,), (0,)), ((), ()))

VM = pl.BlockSpec(memory_space=pltpu.VMEM)
SM = pl.BlockSpec(memory_space=pltpu.SMEM)
ANY = pl.BlockSpec(memory_space=pl.ANY)


def shape(dims, kind=BF):
    return jax.ShapeDtypeStruct(tuple(dims), kind)


def call(body, outs, in_specs, out_specs, scratch=(), flops=0, moved=0):
    return pl.pallas_call(
        body,
        out_shape=outs,
        in_specs=in_specs,
        out_specs=out_specs,
        scratch_shapes=list(scratch),
        compiler_params=pltpu.CompilerParams(vmem_limit_bytes=LIMIT),
        cost_estimate=pl.CostEstimate(flops=int(flops), bytes_accessed=int(moved), transcendentals=0),
    )


def hop(value, axis, k):
    size = lax.axis_size(axis)
    return lax.ppermute(value, axis, [(i, i ^ k) for i in range(size)])


def dot(left, right, dims=PLAIN):
    return lax.dot_general(left, right, dims, preferred_element_type=F32)


def put(refs, values):
    for ref, value in zip(refs, values):
        ref[...] = value.astype(ref.dtype)


def joined(values, width):
    values = [v.astype(F32) for v in values]
    have = sum(v.shape[1] for v in values)
    if have < width:
        values.append(jnp.zeros((values[0].shape[0], width - have), F32))
    return jnp.concatenate(values, axis=1).astype(BF)


def pack_body(takes, width, z_ref, *refs):
    count = len(takes)
    ins, outs = refs[:count], refs[count:]
    for k in range(PARTS):
        part = z_ref[0] ^ k
        for j in range(PARTS):

            @pl.when(part == j)
            def _():
                values = [ref[:, pl.ds(step * (j // share), step)] for ref, (step, share) in zip(ins, takes)]
                outs[k][...] = joined(values, width)


def pack(z, arrays, takes, width):
    depth = arrays[0].shape[0]
    return call(
        functools.partial(pack_body, takes, width),
        [shape((depth, width))] * PARTS,
        [SM] + [VM] * len(arrays),
        [VM] * PARTS,
        moved=depth * width * 2 * 8,
    )(z, *arrays)


def place_body(back, z_ref, *refs):
    pieces, halves = (refs[2:6], refs[:2]) if back else (refs[:4], refs[4:6])
    depth = pieces[0].shape[0]
    for k in range(PARTS):
        part = z_ref[0] ^ k
        for j in range(PARTS):

            @pl.when(part == j)
            def _():
                spot = pl.ds((j % 2) * depth, depth)
                if back:
                    pieces[k][...] = halves[j // 2][spot, :]
                else:
                    halves[j // 2][spot, :] = pieces[k][...]


def to_halves(z, pieces):
    depth, cols = pieces[0].shape
    return call(
        functools.partial(place_body, False),
        [shape((2 * depth, cols))] * 2,
        [SM] + [VM] * 4,
        [VM] * 2,
        moved=depth * cols * 16,
    )(z, *pieces)


def to_pieces(z, halves):
    depth, cols = halves[0].shape
    depth //= 2
    return call(
        functools.partial(place_body, True),
        [shape((depth, cols))] * 4,
        [SM] + [VM] * 2,
        [VM] * 4,
        moved=depth * cols * 16,
    )(z, *halves)


def unpack_body(takes, z_ref, *refs):
    ins, outs = refs[:PARTS], refs[PARTS:]
    for ref, (start, step, share) in zip(outs, takes):
        if share == 2:
            ref[...] = jnp.zeros_like(ref)
    for k in range(PARTS):
        part = z_ref[0] ^ k
        for j in range(PARTS):

            @pl.when(part == j)
            def _():
                for ref, (start, step, share) in zip(outs, takes):
                    value = ins[k][:, pl.ds(start, step)].astype(F32)
                    spot = pl.ds(step * (j // share), step)
                    if share == 1:
                        ref[:, spot] = value
                    else:
                        ref[:, spot] += value


def unpack(z, pieces, takes):
    depth = pieces[0].shape[0]
    return call(
        functools.partial(unpack_body, takes),
        [shape((depth, step * PARTS // share), F32) for start, step, share in takes],
        [SM] + [VM] * 4,
        [VM] * len(takes),
        moved=depth * pieces[0].shape[1] * 24,
    )(z, *pieces)


def fetch(pieces, store, sem, base=0):
    copies = []
    step = pieces[0].shape[0]
    for p, piece in enumerate(pieces):
        spot = store.at[pl.ds(p * step, step)]
        copies.append(pltpu.make_async_copy(piece, spot, sem.at[base + p]))
        copies[-1].start()

    def wait():
        for c in copies:
            c.wait()

    return wait


def rotated(value, cosine, sine):
    half = HEAD_DIM // 2
    a, b = value[:, :half], value[:, half:]
    return jnp.concatenate([a * cosine - b * sine, b * cosine + a * sine], axis=1)


def project_body(qw, x_mine, x_theirs, cosine, sine, *refs):
    w = refs[:8]
    first, q_ref, kv_ref, gains = refs[8:12]
    store, sem = refs[12:]
    waits = [fetch(w[4 * i : 4 * i + 4], store.at[i], sem, 4 * i) for i in range(2)]
    rows = x_mine.shape[0]
    waits[0]()
    step = w[0].shape[0]
    spot = 480 - 384
    for p in range(4):
        tail = store[0, pl.ds(p * step, step), 384:512].astype(F32).T
        gains[:, pl.ds(p * step, step)] = tail[spot : spot + 8]
    gain = gains[0:1, :]
    for i, ref in enumerate((x_mine, x_theirs)):
        x = ref[...].astype(F32)
        scale = lax.rsqrt(jnp.mean(x * x, axis=-1, keepdims=True) + EPS)
        first[pl.ds(i * rows, rows), :] = (x * scale * gain).astype(BF)
    cos, sin = cosine[...], sine[...]
    queries, keys, values = [], [], []
    for i in range(2):
        if i:
            waits[1]()
        out = dot(first[...], store[i])
        for start in range(0, qw, HEAD_DIM):
            queries.append(rotated(out[:, start : start + HEAD_DIM], cos, sin))
        keys.append(rotated(out[:, qw : qw + HEAD_DIM], cos, sin))
        values.append(out[:, qw + HEAD_DIM : qw + 2 * HEAD_DIM])
    q_ref[...] = jnp.concatenate(queries, axis=1).astype(BF)
    kv_ref[...] = jnp.concatenate(keys + values, axis=1).astype(BF)


def project(x_mine, x_theirs, cosine, sine, w, qw):
    rows, width = x_mine.shape
    return call(
        functools.partial(project_body, qw),
        [shape((2 * rows, width)), shape((2 * rows, 2 * qw)), shape((2 * rows, 4 * HEAD_DIM)), shape((8, width), F32)],
        [VM] * 4 + [ANY] * 8,
        [VM] * 4,
        [pltpu.VMEM((2, width, 512), BF), pltpu.SemaphoreType.DMA((8,))],
        flops=4 * 2 * rows * width * 512,
        moved=2 * width * 512 * 2 + 4 * rows * width * 2,
    )(x_mine, x_theirs, cosine, sine, *w)


def out_sides(partial, mine, theirs):
    n = mine.shape[0]
    mine[...] = partial[:n]
    theirs[...] = partial[n:].astype(theirs.dtype)


def each(count, step, start):
    if count <= 2:
        for s in range(count):
            start = step(s, start)
        return start
    return lax.fori_loop(0, count, step, start)


def reader(kvs, rows):
    def read(s, lane):
        spot = pl.ds(lane * HEAD_DIM, HEAD_DIM)
        if len(kvs) > 1:
            return kvs[s][:, spot]
        return kvs[0][pl.ds(pl.multiple_of(s * rows, rows), rows), spot]

    return read


def attend_body(sides, q_ref, key_ids, row_ids, *refs):
    arrays = sides if sides <= 2 else 1
    kvs, refs = refs[:arrays], refs[arrays:]
    w = refs[:8]
    mixed = refs[8:10]
    lse, mine, theirs = refs[10:13]
    store, sem = refs[13:]
    waits = [fetch(w[4 * i : 4 * i + 4], store.at[i], sem, 4 * i) for i in range(2)]
    rows = q_ref.shape[0]
    qw = q_ref.shape[1] // 2
    ids = row_ids[...]
    read = reader(kvs, rows)

    def look(s):
        return key_ids[pl.ds(s * rows, rows), :] <= ids

    looks = [look(s) for s in range(sides)] if sides <= 2 else None
    lse[...] = jnp.zeros_like(lse)
    head = 0
    c = FACTOR * LOG2E
    for i in range(2):
        outs = []
        for start in range(i * qw, (i + 1) * qw, HEAD_DIM):
            q = q_ref[:, start : start + HEAD_DIM]

            def score(s):
                seen = looks[s] if looks else look(s)
                return jnp.where(seen, dot(read(s, i), q, LAST), -1e30)

            scores = [score(s) for s in range(sides)] if sides <= 2 else None

            def highest(s, top):
                value = scores[s] if scores else score(s)
                return jnp.maximum(top, jnp.max(value, axis=0, keepdims=True))

            top = each(sides, highest, jnp.full((1, rows), -1e30, F32))

            def gathered(s, carry):
                total, out = carry
                value = scores[s] if scores else score(s)
                p = jnp.exp2(value * c - top * c)
                total = total + jnp.sum(p, axis=0, keepdims=True)
                return total, out + dot(read(s, 2 + i), p.astype(BF), ROWS)

            nothing = (jnp.zeros((1, rows), F32), jnp.zeros((HEAD_DIM, rows), F32))
            total, out = each(sides, gathered, nothing)
            outs.append(out / total)
            lse[head : head + 1, :] = top * c + jnp.log2(total)
            head += 1
        fill = jnp.zeros((512 - 320 - qw, rows), F32)
        tall = jnp.concatenate([jnp.zeros((320, rows), F32)] + outs + [fill], axis=0)
        mixed[i][...] = tall.T.astype(BF)
    for i in range(2):
        waits[i]()
    partial = dot(mixed[0][...], store[0], LAST) + dot(mixed[1][...], store[1], LAST)
    out_sides(partial, mine, theirs)


def attend(q, kvs, key_ids, row_ids, w):
    rows = q.shape[0]
    width = 4 * w[0].shape[0]
    sides = key_ids.shape[0] // rows
    return call(
        functools.partial(attend_body, sides),
        [shape((rows, 512))] * 2
        + [shape((8, rows), F32), shape((rows // 2, width), F32), shape((rows // 2, width))],
        [VM] * (3 + len(kvs)) + [ANY] * 8,
        [VM] * 5,
        [pltpu.VMEM((2, width, 512), BF), pltpu.SemaphoreType.DMA((8,))],
        flops=4 * rows * width * 512 + 16 * rows * rows * sides * HEAD_DIM,
        moved=2 * width * 512 * 2 + rows * width * 3,
    )(q, key_ids, row_ids, *kvs, *w)


def padded(value, width):
    return jnp.concatenate([value, jnp.zeros((value.shape[0], width - value.shape[1]), value.dtype)], axis=1)


def feed_body(fw, n_mine, n_theirs, *refs):
    gu, down = refs[:8], refs[8:16]
    hidden, slope, silu = refs[16:18], refs[18:20], refs[20:22]
    mine, theirs = refs[22:24]
    gu_store, down_store, sem = refs[24:]
    waits = [fetch(gu[4 * i : 4 * i + 4], gu_store.at[i], sem, 4 * i) for i in range(2)]
    waits += [fetch(down[4 * i : 4 * i + 4], down_store.at[i], sem, 8 + 4 * i) for i in range(2)]
    rows = n_mine.shape[0]
    for i in range(2):
        waits[i]()
        for side, ref in enumerate((n_mine, n_theirs)):
            out = dot(ref[...], gu_store[i])
            gate, upper = out[:, :fw], out[:, fw:]
            sigma = jax.nn.sigmoid(gate)
            act = gate * sigma
            spot = pl.ds(side * rows, rows)
            hidden[i][spot, :] = padded(act * upper, 512).astype(BF)
            slope[i][spot, :] = padded(upper * (sigma + act * (1.0 - sigma)), 512).astype(BF)
            silu[i][spot, :] = padded(act, 512).astype(BF)
    waits[2]()
    waits[3]()
    for side, ref in ((1, theirs), (0, mine)):
        spot = pl.ds(side * rows, rows)
        ref[...] = (
            dot(hidden[0][spot, :], down_store[0], LAST) + dot(hidden[1][spot, :], down_store[1], LAST)
        ).astype(ref.dtype)


def feed(n_mine, n_theirs, gu, down, fw):
    rows, width = n_mine.shape
    return call(
        functools.partial(feed_body, fw),
        [shape((2 * rows, 512))] * 6 + [shape((rows, width), F32), shape((rows, width))],
        [VM] * 2 + [ANY] * 16,
        [VM] * 8,
        [pltpu.VMEM((2, width, 2 * fw), BF), pltpu.VMEM((2, width, 512), BF), pltpu.SemaphoreType.DMA((16,))],
        flops=4 * rows * width * 2 * (2 * fw + 512),
        moved=2 * width * (2 * fw + 512) * 2,
    )(n_mine, n_theirs, *gu, *down)


def feed_back_body(fw, d_mine, d_theirs, *refs):
    slope, silu = refs[:2], refs[2:4]
    gu, down = refs[4:12], refs[12:20]
    d_gu = refs[20:22]
    mine, theirs = refs[22:24]
    gu_store, down_store, sem = refs[24:]
    waits = [fetch(down[4 * i : 4 * i + 4], down_store.at[i], sem, 8 + 4 * i) for i in range(2)]
    waits += [fetch(gu[4 * i : 4 * i + 4], gu_store.at[i], sem, 4 * i) for i in range(2)]
    rows = d_mine.shape[0]
    for i in range(2):
        waits[i]()
        for side, ref in enumerate((d_mine, d_theirs)):
            spot = pl.ds(side * rows, rows)
            out = dot(ref[...], down_store[i])
            a = (out * slope[i][spot, :].astype(F32))[:, :fw]
            b = (out * silu[i][spot, :].astype(F32))[:, :fw]
            d_gu[i][spot, :] = jnp.concatenate([a, b], axis=1).astype(BF)
    waits[2]()
    waits[3]()
    for side, ref in ((1, theirs), (0, mine)):
        spot = pl.ds(side * rows, rows)
        ref[...] = (
            dot(d_gu[0][spot, :], gu_store[0], LAST) + dot(d_gu[1][spot, :], gu_store[1], LAST)
        ).astype(ref.dtype)


def feed_back(d_mine, d_theirs, slope, silu, gu, down, fw):
    rows, width = d_mine.shape
    return call(
        functools.partial(feed_back_body, fw),
        [shape((2 * rows, 2 * fw))] * 2 + [shape((rows, width), F32), shape((rows, width))],
        [VM] * 6 + [ANY] * 16,
        [VM] * 4,
        [pltpu.VMEM((2, width, 2 * fw), BF), pltpu.VMEM((2, width, 512), BF), pltpu.SemaphoreType.DMA((16,))],
        flops=4 * rows * width * 2 * (2 * fw + 512),
        moved=2 * width * (2 * fw + 512) * 2,
    )(d_mine, d_theirs, *slope, *silu, *gu, *down)


def weight_grad_body(left_mine, left_theirs, *refs):
    right = refs[:2]
    outs = refs[2:10]
    store, sem = refs[10:]
    rows = left_mine.shape[0]
    step = outs[0].shape[0]
    copies = []
    for p in range(4):
        spot = pl.ds(p * step, step)
        for i in range(2):
            n = 4 * i + p
            value = dot(left_mine[:, spot], right[i][:rows, :], ROWS)
            value += dot(left_theirs[:, spot], right[i][rows:, :], ROWS)
            store[n] = value.astype(BF)
            copies.append(pltpu.make_async_copy(store.at[n], outs[n], sem.at[n]))
            copies[-1].start()
    for c in copies:
        c.wait()


def weight_grad(left_mine, left_theirs, right):
    rows, width = left_mine.shape
    cols = right[0].shape[1]
    step = width // 4
    return call(
        weight_grad_body,
        [shape((step, cols))] * 8,
        [VM] * 4,
        [ANY] * 8,
        [pltpu.VMEM((8, step, cols), BF), pltpu.SemaphoreType.DMA((8,))],
        flops=4 * 2 * rows * width * cols,
        moved=2 * width * cols * 2,
    )(left_mine, left_theirs, *right)


def attend_back_body(sides, d_mine, d_theirs, q_ref, key_ids, row_ids, lse, cosine, sine, *refs):
    arrays = sides if sides <= 2 else 1
    kvs, refs = refs[:arrays], refs[arrays:]
    w = refs[:8]
    dq_ref, own_ref, send_ref = refs[8:11]
    store, mix, d_kv, sem = refs[11:]
    waits = [fetch(w[4 * i : 4 * i + 4], store.at[i], sem, 4 * i) for i in range(2)]
    rows = q_ref.shape[0]
    half = rows // 2
    qw = q_ref.shape[1] // 2
    for i in range(2):
        waits[i]()
        for side, ref in enumerate((d_mine, d_theirs)):
            mix[i, pl.ds(side * half, half), :] = dot(ref[...], store[i])[:, 320 : 320 + qw].astype(BF)
    ids = row_ids[...]
    read = reader(kvs, rows)

    def look(s):
        return key_ids[pl.ds(s * rows, rows), :] <= ids

    looks = [look(s) for s in range(sides)] if sides <= 2 else None
    d_q = []
    c = FACTOR * LOG2E
    head = 0
    for i in range(2):
        for start in range(0, qw, HEAD_DIM):
            q = q_ref[:, i * qw + start : i * qw + start + HEAD_DIM]
            dm = mix[i, :, start : start + HEAD_DIM]
            level = lse[head : head + 1, :]
            head += 1

            def pair(s):
                seen = looks[s] if looks else look(s)
                p = jnp.where(seen, jnp.exp2(dot(read(s, i), q, LAST) * c - level), 0.0)
                return p, dot(read(s, 2 + i), dm, LAST)

            held = [pair(s) for s in range(sides)] if sides <= 2 else None

            def weigh(s, delta):
                p, dp = held[s] if held else pair(s)
                return delta + jnp.sum(p * dp, axis=0, keepdims=True)

            delta = each(sides, weigh, jnp.zeros((1, rows), F32))

            def grads(s, out):
                p, dp = held[s] if held else pair(s)
                ds = (p * (dp - delta)).astype(BF)
                d_value = dot(p.astype(BF), dm)
                d_key = dot(ds, q)
                if start == 0:
                    d_kv[2 + i, s] = d_value
                    d_kv[i, s] = d_key
                else:
                    d_kv[2 + i, s] += d_value
                    d_kv[i, s] += d_key
                return out + dot(read(s, i), ds, ROWS)

            d_q.append(each(sides, grads, jnp.zeros((HEAD_DIM, rows), F32)))
    tall = jnp.concatenate(d_q + [jnp.zeros((512 - 4 * HEAD_DIM, rows), F32)], axis=0).T * FACTOR
    cos, sin = cosine[...], sine[...]
    dq_ref[...] = jnp.concatenate(
        [rotated(tall[:, h * HEAD_DIM : (h + 1) * HEAD_DIM], cos, -sin) for h in range(4)], axis=1
    ).astype(BF)
    for s in range(sides):
        value = jnp.concatenate([d_kv[0, s] * FACTOR, d_kv[1, s] * FACTOR, d_kv[2, s], d_kv[3, s]], axis=1)
        if s == 0:
            own_ref[...] = value
        else:
            send_ref[pl.ds((s - 1) * rows, rows), :] = value.astype(BF)


def attend_back(d_mine, d_theirs, q, kvs, key_ids, row_ids, lse, cosine, sine, w):
    rows = q.shape[0]
    width = d_mine.shape[1]
    sides = key_ids.shape[0] // rows
    cols = kvs[0].shape[1]
    return call(
        functools.partial(attend_back_body, sides),
        [shape(q.shape), shape((rows, cols), F32), shape(((sides - 1) * rows, cols))],
        [VM] * (8 + len(kvs)) + [ANY] * 8,
        [VM] * 3,
        [
            pltpu.VMEM((2, width, 512), BF),
            pltpu.VMEM((2, rows, q.shape[1] // 2), BF),
            pltpu.VMEM((4, sides, rows, HEAD_DIM), F32),
            pltpu.SemaphoreType.DMA((8,)),
        ],
        flops=4 * rows * width * 512 + 40 * rows * rows * sides * HEAD_DIM,
        moved=2 * width * 512 * 2,
    )(d_mine, d_theirs, q, key_ids, row_ids, lse, cosine, sine, *kvs, *w)


def project_back_body(x_mine, x_theirs, dq_ref, own_ref, got_ref, cosine, sine, *refs):
    w = refs[:8]
    d_qkv = refs[8:10]
    mine, theirs, gain_ref = refs[10:13]
    store, sem = refs[13:]
    waits = [fetch(w[4 * i : 4 * i + 4], store.at[i], sem, 4 * i) for i in range(2)]
    qw = dq_ref.shape[1] // 2
    cos, sin = cosine[...], sine[...]
    d_kv = own_ref[...] + got_ref[...].astype(F32)
    d_q = dq_ref[...].astype(F32)
    rows = d_q.shape[0]
    for i in range(2):
        d_k = rotated(d_kv[:, i * HEAD_DIM : (i + 1) * HEAD_DIM], cos, -sin)
        d_v = d_kv[:, (2 + i) * HEAD_DIM : (3 + i) * HEAD_DIM]
        d_qkv[i][...] = padded(
            jnp.concatenate([d_q[:, i * qw : (i + 1) * qw], d_k, d_v], axis=1), 512
        ).astype(BF)
    for i in range(2):
        waits[i]()
    half = rows // 2
    total = 0.0
    for side, ref, x_ref in ((1, theirs, x_theirs), (0, mine, x_mine)):
        spot = pl.ds(side * half, half)
        part = dot(d_qkv[0][spot, :], store[0], LAST) + dot(d_qkv[1][spot, :], store[1], LAST)
        ref[...] = part.astype(ref.dtype)
        x = x_ref[...].astype(F32)
        scale = lax.rsqrt(jnp.mean(x * x, axis=-1, keepdims=True) + EPS)
        total = total + jnp.sum(part * (x * scale), axis=0, keepdims=True)
    gain_ref[...] = total


def project_back(x_mine, x_theirs, dq, own, got, cosine, sine, w):
    rows, width = x_mine.shape
    return call(
        project_back_body,
        [shape((2 * rows, 512))] * 2 + [shape((rows, width), F32), shape((rows, width)), shape((1, width), F32)],
        [VM] * 7 + [ANY] * 8,
        [VM] * 5,
        [pltpu.VMEM((2, width, 512), BF), pltpu.SemaphoreType.DMA((8,))],
        flops=8 * rows * width * 512,
        moved=2 * width * 512 * 2 + rows * width * 8,
    )(x_mine, x_theirs, dq, own, got, cosine, sine, *w)


def attn_grad_body(first, d_mine, d_theirs, gain_one, gain_two, *refs):
    d_qkv, mixed = refs[:2], refs[2:4]
    outs = refs[4:12]
    store, sem = refs[12:]
    half = d_mine.shape[0]
    step = outs[0].shape[0]
    copies = []
    for p in range(4):
        spot = pl.ds(p * step, step)
        tall = jnp.concatenate(
            [
                jnp.zeros((96, step), F32),
                gain_one[:, spot],
                gain_two[:, spot],
                jnp.zeros((30, step), F32),
            ],
            axis=0,
        ).T
        tall = jnp.concatenate([jnp.zeros((step, 384), F32), tall], axis=1)
        for i in range(2):
            n = 4 * i + p
            value = dot(first[:, spot], d_qkv[i][...], ROWS)
            value += dot(d_mine[:, spot], mixed[i][:half, :], ROWS)
            value += dot(d_theirs[:, spot], mixed[i][half:, :], ROWS)
            store[n] = (value + tall).astype(BF)
            copies.append(pltpu.make_async_copy(store.at[n], outs[n], sem.at[n]))
            copies[-1].start()
    for c in copies:
        c.wait()


def attn_grad(first, d_mine, d_theirs, gain_one, gain_two, d_qkv, mixed):
    rows, width = first.shape
    step = width // 4
    return call(
        attn_grad_body,
        [shape((step, 512))] * 8,
        [VM] * 9,
        [ANY] * 8,
        [pltpu.VMEM((8, step, 512), BF), pltpu.SemaphoreType.DMA((8,))],
        flops=8 * rows * width * 512,
        moved=2 * width * 512 * 2,
    )(first, d_mine, d_theirs, gain_one, gain_two, *d_qkv, *mixed)


class Place:
    def __init__(self):
        self.inner = lax.axis_size("seq") // PARTS
        s = lax.axis_index("seq")
        m = lax.axis_index("mp")
        self.z = s // self.inner
        self.y = s % self.inner
        self.x = m // 2
        self.c = m % 2
        self.zs = self.z.reshape(1).astype(jnp.int32)
        self.bits = []
        b = 1
        while b < self.inner:
            self.bits.append(b)
            b *= 2

    def hop_z(self, v, k):
        return hop(v, "seq", k * self.inner)

    def hop_y(self, v, b):
        return hop(v, "seq", b)

    def hop_x(self, v):
        return hop(v, "mp", 2)

    def hop_c(self, v):
        return hop(v, "mp", 1)

    def flip_y(self, v):
        for b in self.bits:
            w = v.reshape((v.shape[0], self.inner // (2 * b), 2, b) + v.shape[2:])
            w = w[:, :, ::-1].reshape(v.shape)
            v = jnp.where((self.y // b) % 2 == 1, w, v)
        return v

    def features_in(self, v):
        rows = v.shape[0]
        v = v.reshape(rows * 2, 2, self.inner, -1).transpose(0, 2, 1, 3)
        return self.flip_y(v).reshape(rows, -1)

    def features_out(self, v):
        rows = v.shape[0]
        v = self.flip_y(v.reshape(rows * 2, self.inner, 2, -1))
        return v.transpose(0, 2, 1, 3).reshape(rows, -1)

    def swap_z(self, pieces):
        return [pieces[0]] + [self.hop_z(pieces[k], k) for k in range(1, PARTS)]

    def spread_y(self, v):
        for b in self.bits[:-1]:
            v = jnp.concatenate([v, self.hop_y(v, b)], 0)
        return [v, self.hop_y(v, self.bits[-1])]

    def spread(self, halves):
        a = self.spread_y(halves[0])
        b_other = self.hop_x(halves[1])
        b = self.spread_y(halves[1])
        a_other = [self.hop_x(v) for v in a]
        b_other = self.spread_y(b_other)
        return a + b + a_other + b_other

    def collect(self, grads):
        def add(own, got):
            return (own.astype(F32) + got.astype(F32)).astype(BF)

        def collect_y(v):
            value = add(v[0], self.hop_y(v[1], self.bits[-1]))
            for b in reversed(self.bits[:-1]):
                n = value.shape[0] // 2
                value = add(value[:n], self.hop_y(value[n:], b))
            return value

        own, other = grads[:4], grads[4:]
        a = collect_y([add(own[i], self.hop_x(other[i])) for i in range(2)])
        b = add(collect_y(own[2:]), self.hop_x(collect_y(other[2:])))
        return [a, b]

    def gather(self, own):
        one = self.hop_z(own, 1)
        two = self.hop_z(own, 2)
        three = self.hop_z(two, 1)
        mine = jnp.concatenate([own, one, two, three], 0)
        return mine, self.hop_c(mine)

    def scatter(self, mine, theirs):
        got = self.hop_c(theirs)
        n = mine.shape[0] // PARTS

        def piece(k):
            spot = slice(k * n, (k + 1) * n)
            return mine[spot] + got[spot].astype(F32)

        three = self.hop_z(piece(3).astype(BF), 1)
        two = self.hop_z((piece(2) + three.astype(F32)).astype(BF), 2)
        one = self.hop_z(piece(1).astype(BF), 1)
        return piece(0) + one.astype(F32) + two.astype(F32)


def tables(place):
    half = HEAD_DIM // 2
    freq = THETA ** (-(jnp.arange(half, dtype=F32) * 2.0 / HEAD_DIM))
    angle = place[:, None] * freq[None, :]
    return (jnp.cos(angle), jnp.sin(angle))


def scale_of(value):
    return lax.rsqrt(jnp.mean(value * value, axis=-1, keepdims=True) + EPS)


def norm_back(grad, value, scale, gain):
    unit = value * scale
    scaled = grad * gain
    back = scale * (scaled - unit * jnp.mean(scaled * unit, axis=-1, keepdims=True))
    return unit, back


def on_device(
    inputs,
    targets,
    seq_ids,
    block_ids,
    attn_gain,
    mlp_gain,
    w_query,
    w_key,
    w_value,
    w_out,
    w_gate,
    w_up,
    w_down,
):
    at = Place()
    inner = at.inner
    half_span = SPAN // 2
    kw = w_key.shape[1] // 2
    qw = w_query.shape[1] // PARTS
    fw = w_gate.shape[1] // PARTS

    off = jnp.where(seq_ids[0] == at.x, 0, SPAN)
    row0 = off + at.c * half_span

    def own_rows(v):
        return at.features_in(lax.dynamic_slice_in_dim(v, row0, half_span, 0))

    gains = jnp.stack([attn_gain, mlp_gain], -1)
    takes = [(qw, 1), (kw, 2), (kw, 2), (qw, 1), (2, 4)]
    pieces_qo = pack(at.zs, [w_query, w_key, w_value, w_out, gains], takes, 512)
    x_own = own_rows(inputs)
    w_qo = at.spread(to_halves(at.zs, at.swap_z(pieces_qo)))
    x_mine, x_theirs = at.gather(x_own)

    ids = lax.dynamic_slice_in_dim(block_ids, off, SPAN, 0)
    ids = jnp.stack([ids] + [at.hop_z(ids, k) for k in range(1, PARTS)], 0)
    ids = ids.reshape(PARTS, 2, half_span).transpose(1, 0, 2)
    ids = jnp.where(at.c == 1, ids[::-1], ids).reshape(-1)
    key_ids = ids[None]
    for b in at.bits:
        key_ids = jnp.concatenate([key_ids, at.hop_y(key_ids, b)], 0)
    key_ids = key_ids.reshape(-1, 1)
    row_ids = ids.reshape(1, -1)

    pieces_gu = pack(at.zs, [w_gate, w_up], [(fw, 1), (fw, 1)], 2 * fw)
    w_gu = at.spread(to_halves(at.zs, at.swap_z(pieces_gu)))
    pieces_d = pack(at.zs, [w_down], [(fw, 1)], 512)
    w_d = at.spread(to_halves(at.zs, at.swap_z(pieces_d)))

    rows = 2 * PARTS * half_span
    count = jnp.arange(rows, dtype=jnp.int32)
    zz = at.z ^ ((count // half_span) % PARTS)
    cc = at.c ^ (count // (half_span * PARTS))
    place = ((zz * inner + at.y) * SPAN + cc * half_span + count % half_span).astype(F32)
    cosine, sine = tables(place)

    first, query, kv, gain = project(x_mine, x_theirs, cosine, sine, w_qo, qw)
    gain_one, gain_two = gain[0:1], gain[1:2]
    kvs = [kv]
    for b in at.bits:
        kvs = kvs + [at.hop_y(v, b) for v in kvs]
    if inner > 2:
        kvs = [jnp.concatenate(kvs, 0)]
    mixed_a, mixed_b, lse, mine, theirs = attend(query, kvs, key_ids, row_ids, w_qo)
    branch_attn = at.scatter(mine, theirs)
    middle = x_own.astype(F32) + branch_attn
    scale_two = scale_of(middle)
    n_mine, n_theirs = at.gather((middle * scale_two * gain_two).astype(BF))
    out = feed(n_mine, n_theirs, w_gu, w_d, fw)
    hidden, slope, silu, (mine, theirs) = out[:2], out[2:4], out[4:6], out[6:]
    branch_mlp = at.scatter(mine, theirs)
    stream = middle + branch_mlp

    t_own = own_rows(targets).astype(F32)
    d_own = (stream - t_own).astype(BF)
    d_mine, d_theirs = at.gather(d_own)
    out = feed_back(d_mine, d_theirs, slope, silu, w_gu, w_d, fw)
    d_gu, (mine, theirs) = out[:2], out[2:]
    grad_d = weight_grad(d_mine, d_theirs, hidden)
    d_second = at.scatter(mine, theirs)
    grad_gu = weight_grad(n_mine, n_theirs, d_gu)
    unit, back = norm_back(d_second, middle, scale_two, gain_two)
    grad_gain_two = jnp.sum(d_second * unit, axis=0, keepdims=True)
    d_middle = d_own.astype(F32) + back
    a_mine, a_theirs = at.gather(d_middle.astype(BF))
    out = attend_back(a_mine, a_theirs, query, kvs, key_ids, row_ids, lse, cosine, sine, w_qo)
    d_query, d_kv, sent = out
    if inner > 2:
        sent = jnp.concatenate([d_kv, sent.astype(F32)], 0)
        for b in reversed(at.bits[1:]):
            n = sent.shape[0] // 2
            sent = sent[:n] + at.hop_y(sent[n:].astype(BF), b).astype(F32)
        d_kv, sent = sent[:rows], sent[rows:].astype(BF)
    got = at.hop_y(sent, at.bits[0])
    out = project_back(x_mine, x_theirs, d_query, d_kv, got, cosine, sine, w_qo)
    d_qkv, mine, theirs, grad_gain_one = out[:2], out[2], out[3], out[4]
    d_first = at.scatter(mine, theirs)
    grad_qo = attn_grad(
        first, a_mine, a_theirs, grad_gain_one, grad_gain_two, d_qkv, (mixed_a, mixed_b)
    )

    x_f = x_own.astype(F32)
    unit, back = norm_back(d_first, x_f, scale_of(x_f), gain_one)
    input_grad_own = (d_middle + back).astype(BF)

    sums = jnp.stack(
        [jnp.sum(stream * stream), jnp.sum(branch_attn * branch_attn), jnp.sum(branch_mlp * branch_mlp)]
    )
    sums = jnp.broadcast_to(sums[:, None], (3, 128))
    sums = sums + at.hop_c(sums)
    sums = sums + at.hop_x(sums)
    for b in at.bits:
        sums = sums + at.hop_y(sums, b)
    sums = sums + at.hop_z(sums, 1)
    sums = sums + at.hop_z(sums, 2)
    entries = inputs.shape[0] * lax.axis_size("seq") * inputs.shape[1]
    rms = jnp.sqrt(sums[:, 0] / entries + EPS)

    def whole_rows(own):
        v = at.features_out(own)
        other = at.hop_c(v)
        v = jnp.where(at.c == 0, jnp.concatenate([v, other], 0), jnp.concatenate([other, v], 0))
        other = at.hop_x(v)
        return jnp.where(off == 0, jnp.concatenate([v, other], 0), jnp.concatenate([other, v], 0))

    layer_out = whole_rows(stream.astype(BF))
    input_grad = whole_rows(input_grad_own)

    def arrive(grads):
        return at.swap_z(to_pieces(at.zs, at.collect(grads)))

    (g_down,) = unpack(at.zs, arrive(grad_d), [(0, fw, 1)])
    g_gate, g_up = unpack(at.zs, arrive(grad_gu), [(0, fw, 1), (fw, fw, 1)])
    takes = [(0, qw, 1), (qw, kw, 2), (qw + kw, kw, 2), (qw + 2 * kw, qw, 1), (480, 2, 4)]
    got_qo = arrive(grad_qo)
    g_query, g_key, g_value, g_out = unpack(at.zs, got_qo, takes[:4])
    gains_sum = sum(p[:, 480:482].astype(F32) for p in got_qo)
    gains_sum = gains_sum + at.hop_c(gains_sum)
    return (
        layer_out,
        input_grad,
        g_query,
        g_key,
        g_value,
        g_out,
        g_gate,
        g_up,
        g_down,
        gains_sum[:, 0],
        gains_sum[:, 1],
        rms[0],
        rms[1],
        rms[2],
    )
def solution(mesh):
    return jax.shard_map(
        on_device,
        mesh=mesh,
        in_specs=(
            P("seq", None),
            P("seq", None),
            P("seq"),
            P("seq"),
            P("seq"),
            P("seq"),
            P("seq", "mp"),
            P("seq", "mp"),
            P("seq", "mp"),
            P("seq", "mp"),
            P("seq", "mp"),
            P("seq", "mp"),
            P("seq", "mp"),
        ),
        out_specs=(
            P("seq", None),
            P("seq", None),
            P("seq", "mp"),
            P("seq", "mp"),
            P("seq", "mp"),
            P("seq", "mp"),
            P("seq", "mp"),
            P("seq", "mp"),
            P("seq", "mp"),
            P("seq"),
            P("seq"),
            P(),
            P(),
            P(),
        ),
        check_vma=False,
    )
```

```python
import functools

import jax
import jax.numpy as jnp
from jax import lax
from jax.experimental import pallas as pl
from jax.experimental.pallas import tpu as pltpu
from jax.sharding import PartitionSpec as P

HEAD_DIM = 80
SPAN = 128
EPS = 1e-05
THETA = 1000000.0
PARTS = 4
BF = jnp.bfloat16
F32 = jnp.float32
FACTOR = HEAD_DIM**-0.5
LOG2E = 1.4426950408889634
LIMIT = 56 * 1024 * 1024

PLAIN = (((1,), (0,)), ((), ()))
LAST = (((1,), (1,)), ((), ()))
ROWS = (((0,), (0,)), ((), ()))

VM = pl.BlockSpec(memory_space=pltpu.VMEM)
SM = pl.BlockSpec(memory_space=pltpu.SMEM)
ANY = pl.BlockSpec(memory_space=pl.ANY)


def shape(dims, kind=BF):
    return jax.ShapeDtypeStruct(tuple(dims), kind)


def call(body, outs, in_specs, out_specs, scratch=()):
    return pl.pallas_call(
        body,
        out_shape=outs,
        in_specs=in_specs,
        out_specs=out_specs,
        scratch_shapes=list(scratch),
        compiler_params=pltpu.CompilerParams(vmem_limit_bytes=LIMIT),
    )


def hop(value, axis, k):
    size = lax.axis_size(axis)
    return lax.ppermute(value, axis, [(i, i ^ k) for i in range(size)])


def dot(left, right, dims=PLAIN):
    return lax.dot_general(left, right, dims, preferred_element_type=F32)


def joined(values, width):
    values = [v.astype(F32) for v in values]
    have = sum(v.shape[1] for v in values)
    if have < width:
        values.append(jnp.zeros((values[0].shape[0], width - have), F32))
    return jnp.concatenate(values, axis=1).astype(BF)


def pack_body(takes, width, z_ref, *refs):
    count = len(takes)
    ins, outs = refs[:count], refs[count:]
    for k in range(PARTS):
        part = z_ref[0] ^ k
        for j in range(PARTS):

            @pl.when(part == j)
            def _():
                values = [ref[:, pl.ds(step * (j // share), step)] for ref, (step, share) in zip(ins, takes)]
                outs[k][...] = joined(values, width)


def pack(z, arrays, takes, width):
    depth = arrays[0].shape[0]
    return call(
        functools.partial(pack_body, takes, width),
        [shape((depth, width))] * PARTS,
        [SM] + [VM] * len(arrays),
        [VM] * PARTS,
    )(z, *arrays)


def unpack_body(takes, z_ref, *refs):
    ins, outs = refs[:PARTS], refs[PARTS:]
    for ref, (start, step, share) in zip(outs, takes):
        if share == 2:
            ref[...] = jnp.zeros_like(ref)
    for k in range(PARTS):
        part = z_ref[0] ^ k
        for j in range(PARTS):

            @pl.when(part == j)
            def _():
                for ref, (start, step, share) in zip(outs, takes):
                    value = ins[k][:, pl.ds(start, step)].astype(F32)
                    spot = pl.ds(step * (j // share), step)
                    if share == 1:
                        ref[:, spot] = value
                    else:
                        ref[:, spot] += value


def unpack(z, pieces, takes):
    depth = pieces[0].shape[0]
    return call(
        functools.partial(unpack_body, takes),
        [shape((depth, step * PARTS // share), F32) for start, step, share in takes],
        [SM] + [VM] * 4,
        [VM] * len(takes),
    )(z, *pieces)


def fetch(pieces, store, sem, base=0):
    copies = []
    step = pieces[0].shape[0]
    for p, piece in enumerate(pieces):
        spot = store.at[pl.ds(p * step, step)]
        copies.append(pltpu.make_async_copy(piece, spot, sem.at[base + p]))
        copies[-1].start()

    def wait():
        for c in copies:
            c.wait()

    return wait


def swapped(value, width, k):
    count = value.shape[1] // width
    return jnp.concatenate([value[:, (i ^ k) * width : (i ^ k) * width + width] for i in range(count)], axis=1)


def relative(value, index, count):
    width = value.shape[1] // count
    b = 1
    while b < count:
        turned = swapped(value, width, b)
        value = jnp.where((index // b) % 2 == 1, turned, value)
        b *= 2
    return value


def own_rows_body(count, where_ref, ids, x_ref, t_ref, x_out, t_out):
    spot = pl.ds(pl.multiple_of(where_ref[0], 64), 64)
    width = x_ref.shape[1]
    x = relative(x_ref[spot, :].astype(F32), where_ref[1], count)
    x_out[:, :width] = x.astype(BF)
    x_out[:, width:] = jnp.broadcast_to(ids[spot, :].astype(F32), (64, 128)).astype(BF)
    t_out[...] = relative(t_ref[spot, :].astype(F32), where_ref[1], count).astype(BF)


def own_rows(where, ids, x, t, count):
    width = x.shape[1]
    return call(
        functools.partial(own_rows_body, count),
        [shape((64, width + 128)), shape((64, width))],
        [SM] + [VM] * 3,
        [VM] * 2,
    )(where, ids, x, t)


def stack_body(width, own, one, two, three, out):
    n = own.shape[0]
    for k, ref in enumerate((own, one, two, three)):
        spot = pl.ds(k * n, n)
        out[spot, : 4 * width] = swapped(ref[:, : 4 * width], width, k)
        if out.shape[1] > 4 * width:
            out[spot, 4 * width :] = ref[:, 4 * width :]


def stack(pieces, width):
    n, cols = pieces[0].shape
    return call(
        functools.partial(stack_body, width), shape((4 * n, cols)), [VM] * 4, VM
    )(*pieces)


def first_sum_body(mine, got, one, three, keep):
    n = one.shape[0]

    def piece(k):
        spot = pl.ds(k * n, n)
        return mine[spot, :] + got[spot, :].astype(F32)

    three[...] = piece(3).astype(BF)
    one[...] = piece(1).astype(BF)
    keep[:n, :] = piece(0)
    keep[n:, :] = piece(2)


def first_sum(mine, got):
    n, width = mine.shape
    n //= 4
    return call(
        first_sum_body, [shape((n, width))] * 2 + [shape((2 * n, width), F32)], [VM] * 2, [VM] * 3
    )(mine, got)


def second_sum_body(width, keep, three, out):
    n = out.shape[0]
    out[...] = (keep[n:, :] + swapped(three[...].astype(F32), width, 1)).astype(BF)


def second_sum(keep, three, width):
    return call(functools.partial(second_sum_body, width), shape(three.shape), [VM] * 2, VM)(keep, three)


def last_sum(width, keep, one, two):
    n = one.shape[0]
    return keep[:n, :] + swapped(one[...].astype(F32), width, 1) + swapped(two[...].astype(F32), width, 2)


def mean_scale(value):
    return lax.rsqrt(jnp.mean(value * value, axis=-1, keepdims=True) + EPS)


def back_norm(grad, value, gain):
    scale = mean_scale(value)
    unit = value * scale
    scaled = grad * gain
    return unit, scale * (scaled - unit * jnp.mean(scaled * unit, axis=-1, keepdims=True))


def after_attn_body(width, keep, one, two, x_own, gain, middle, n_own, total):
    branch = last_sum(width, keep, one, two)
    value = x_own[:, : 4 * width].astype(F32) + branch
    middle[...] = value
    n_own[...] = (value * mean_scale(value) * gain[1:2, :]).astype(BF)
    total[...] = jnp.full(total.shape, jnp.sum(branch * branch), F32)


def after_mlp_body(width, count, where_ref, keep, one, two, middle, target, d_own, out, total):
    branch = last_sum(width, keep, one, two)
    stream = middle[...] + branch
    d_own[...] = (stream - target[...].astype(F32)).astype(BF)
    out[...] = relative(stream, where_ref[1], count).astype(BF)
    total[0:8, :] = jnp.full((8, 128), jnp.sum(stream * stream), F32)
    total[8:16, :] = jnp.full((8, 128), jnp.sum(branch * branch), F32)


def after_feed_back_body(width, keep, one, two, middle, d_own, gain, d_middle, a_own, gain_grad):
    grad = last_sum(width, keep, one, two)
    unit, back = back_norm(grad, middle[...], gain[1:2, :])
    value = d_own[...].astype(F32) + back
    d_middle[...] = value
    a_own[...] = value.astype(BF)
    gain_grad[...] = jnp.sum(grad * unit, axis=0, keepdims=True)


def after_all_body(width, count, where_ref, keep, one, two, x_own, d_middle, gain, out):
    grad = last_sum(width, keep, one, two)
    unit, back = back_norm(grad, x_own[:, : 4 * width].astype(F32), gain[0:1, :])
    out[...] = relative(d_middle[...] + back, where_ref[1], count).astype(BF)


def spread_rows_body(spots, p0, p1, p2, p3, out):
    n = p0.shape[0]
    for i, ref in enumerate((p0, p1, p2, p3)):
        out[pl.ds(pl.multiple_of(spots[i], 64), n), :] = ref[...]


def spread_rows(spots, pieces):
    n, width = pieces[0].shape
    return call(spread_rows_body, shape((4 * n, width)), [SM] + [VM] * 4, VM)(spots, *pieces)


def rotated(value, cosine, sine):
    half = HEAD_DIM // 2
    a, b = value[:, :half], value[:, half:]
    return jnp.concatenate([a * cosine - b * sine, b * cosine + a * sine], axis=1)


def project_body(qw, x_mine, x_theirs, cosine, sine, *refs):
    w = refs[:16]
    first, q_ref, kv_ref, gains, row_ids = refs[16:21]
    store, sem = refs[21:]
    waits = [fetch(w[8 * i : 8 * i + 8], store.at[i], sem, 8 * i) for i in range(2)]
    rows = x_mine.shape[0]
    width = first.shape[1]
    step = width // 4
    ids = jnp.concatenate([x_mine[:, width:], x_theirs[:, width:]], axis=0).astype(F32)
    row_ids[...] = ids.T[0:8, :]
    waits[0]()
    spot = 480 - 384
    for p in range(4):
        tail = store[0, pl.ds(p * step, step), 384:512].astype(F32).T
        gains[:, pl.ds(p * step, step)] = tail[spot : spot + 8]
    gain = gains[0:1, :]
    for i, ref in enumerate((x_mine, x_theirs)):
        x = ref[:, :width].astype(F32)
        first[pl.ds(i * rows, rows), :] = (x * mean_scale(x) * gain).astype(BF)
    cos, sin = cosine[...], sine[...]
    queries, keys, values = [], [], []
    for i in range(2):
        if i:
            waits[1]()
        out = dot(first[...], store[i])
        for start in range(0, qw, HEAD_DIM):
            queries.append(rotated(out[:, start : start + HEAD_DIM], cos, sin))
        keys.append(rotated(out[:, qw : qw + HEAD_DIM], cos, sin))
        values.append(out[:, qw + HEAD_DIM : qw + 2 * HEAD_DIM])
    q_ref[...] = jnp.concatenate(queries, axis=1).astype(BF)
    kv_ref[...] = jnp.concatenate(keys + values + [ids[:, :64]], axis=1).astype(BF)


def project(x_mine, x_theirs, cosine, sine, w, qw):
    rows, width = x_mine.shape
    width -= 128
    return call(
        functools.partial(project_body, qw),
        [
            shape((2 * rows, width)),
            shape((2 * rows, 2 * qw)),
            shape((2 * rows, 384)),
            shape((8, width), F32),
            shape((8, 2 * rows), F32),
        ],
        [VM] * 4 + [ANY] * 16,
        [VM] * 5,
        [pltpu.VMEM((2, width, 512), BF), pltpu.SemaphoreType.DMA((16,))],
    )(x_mine, x_theirs, cosine, sine, *w)


def out_sides(partial, mine, theirs):
    n = mine.shape[0]
    mine[...] = partial[:n]
    theirs[...] = partial[n:].astype(theirs.dtype)


def each(count, step, start):
    if count <= 2:
        for s in range(count):
            start = step(s, start)
        return start
    return lax.fori_loop(0, count, step, start)


def reader(kvs, rows):
    def read(s, lane):
        if len(kvs) > 1:
            return kvs[s][:, lane]
        return kvs[0][pl.ds(pl.multiple_of(s * rows, rows), rows), lane]

    return read


def lanes(i):
    return pl.ds(i * HEAD_DIM, HEAD_DIM)


ID_LANE = pl.ds(4 * HEAD_DIM, 1)


def attend_body(sides, q_ref, row_ids, *refs):
    arrays = sides if sides <= 2 else 1
    kvs, refs = refs[:arrays], refs[arrays:]
    w = refs[:16]
    mixed = refs[16:18]
    lse, mine, theirs = refs[18:21]
    store, sem = refs[21:]
    waits = [fetch(w[8 * i : 8 * i + 8], store.at[i], sem, 8 * i) for i in range(2)]
    rows = q_ref.shape[0]
    qw = q_ref.shape[1] // 2
    ids = row_ids[0:1, :]
    read = reader(kvs, rows)

    def look(s):
        return read(s, ID_LANE).astype(F32) <= ids

    looks = [look(s) for s in range(sides)] if sides <= 2 else None
    lse[...] = jnp.zeros_like(lse)
    head = 0
    c = FACTOR * LOG2E
    for i in range(2):
        outs = []
        for start in range(i * qw, (i + 1) * qw, HEAD_DIM):
            q = q_ref[:, start : start + HEAD_DIM]

            def score(s):
                seen = looks[s] if looks else look(s)
                return jnp.where(seen, dot(read(s, lanes(i)), q, LAST), -1e30)

            scores = [score(s) for s in range(sides)] if sides <= 2 else None

            def highest(s, top):
                value = scores[s] if scores else score(s)
                return jnp.maximum(top, jnp.max(value, axis=0, keepdims=True))

            top = each(sides, highest, jnp.full((1, rows), -1e30, F32))

            def gathered(s, carry):
                total, out = carry
                value = scores[s] if scores else score(s)
                p = jnp.exp2(value * c - top * c)
                total = total + jnp.sum(p, axis=0, keepdims=True)
                return total, out + dot(read(s, lanes(2 + i)), p.astype(BF), ROWS)

            nothing = (jnp.zeros((1, rows), F32), jnp.zeros((HEAD_DIM, rows), F32))
            total, out = each(sides, gathered, nothing)
            outs.append(out / total)
            lse[head : head + 1, :] = top * c + jnp.log2(total)
            head += 1
        fill = jnp.zeros((512 - 320 - qw, rows), F32)
        tall = jnp.concatenate([jnp.zeros((320, rows), F32)] + outs + [fill], axis=0)
        mixed[i][...] = tall.T.astype(BF)
    for i in range(2):
        waits[i]()
    partial = dot(mixed[0][...], store[0], LAST) + dot(mixed[1][...], store[1], LAST)
    out_sides(partial, mine, theirs)


def attend(q, kvs, row_ids, w, sides):
    rows = q.shape[0]
    width = 8 * w[0].shape[0]
    return call(
        functools.partial(attend_body, sides),
        [shape((rows, 512))] * 2
        + [shape((8, rows), F32), shape((rows // 2, width), F32), shape((rows // 2, width))],
        [VM] * (2 + len(kvs)) + [ANY] * 16,
        [VM] * 5,
        [pltpu.VMEM((2, width, 512), BF), pltpu.SemaphoreType.DMA((16,))],
    )(q, row_ids, *kvs, *w)


def padded(value, width):
    return jnp.concatenate([value, jnp.zeros((value.shape[0], width - value.shape[1]), value.dtype)], axis=1)


def feed_body(fw, n_mine, n_theirs, *refs):
    w = refs[:16]
    hidden, slope, silu = refs[16:18], refs[18:20], refs[20:22]
    mine, theirs = refs[22:24]
    store, sem = refs[24:]
    waits = [fetch(w[8 * i : 8 * i + 8], store.at[i], sem, 8 * i) for i in range(2)]
    rows = n_mine.shape[0]
    for i in range(2):
        waits[i]()
        for side, ref in enumerate((n_mine, n_theirs)):
            out = dot(ref[...], store[i, :, : 2 * fw])
            gate, upper = out[:, :fw], out[:, fw:]
            sigma = jax.nn.sigmoid(gate)
            act = gate * sigma
            spot = pl.ds(side * rows, rows)
            hidden[i][spot, :] = padded(act * upper, 512).astype(BF)
            slope[i][spot, :] = padded(upper * (sigma + act * (1.0 - sigma)), 512).astype(BF)
            silu[i][spot, :] = padded(act, 512).astype(BF)
    for side, ref in ((1, theirs), (0, mine)):
        spot = pl.ds(side * rows, rows)
        ref[...] = (
            dot(hidden[0][spot, :], store[0, :, 2 * fw :], LAST)
            + dot(hidden[1][spot, :], store[1, :, 2 * fw :], LAST)
        ).astype(ref.dtype)


def feed(n_mine, n_theirs, w, fw):
    rows, width = n_mine.shape
    return call(
        functools.partial(feed_body, fw),
        [shape((2 * rows, 512))] * 6 + [shape((rows, width), F32), shape((rows, width))],
        [VM] * 2 + [ANY] * 16,
        [VM] * 8,
        [pltpu.VMEM((2, width, 2 * fw + 512), BF), pltpu.SemaphoreType.DMA((16,))],
    )(n_mine, n_theirs, *w)


def feed_back_body(fw, d_mine, d_theirs, *refs):
    slope, silu = refs[:2], refs[2:4]
    w = refs[4:20]
    d_gu = refs[20:22]
    mine, theirs = refs[22:24]
    store, sem = refs[24:]
    waits = [fetch(w[8 * i : 8 * i + 8], store.at[i], sem, 8 * i) for i in range(2)]
    rows = d_mine.shape[0]
    for i in range(2):
        waits[i]()
        for side, ref in enumerate((d_mine, d_theirs)):
            spot = pl.ds(side * rows, rows)
            out = dot(ref[...], store[i, :, 2 * fw :])
            a = (out * slope[i][spot, :].astype(F32))[:, :fw]
            b = (out * silu[i][spot, :].astype(F32))[:, :fw]
            d_gu[i][spot, :] = jnp.concatenate([a, b], axis=1).astype(BF)
    for side, ref in ((1, theirs), (0, mine)):
        spot = pl.ds(side * rows, rows)
        ref[...] = (
            dot(d_gu[0][spot, :], store[0, :, : 2 * fw], LAST)
            + dot(d_gu[1][spot, :], store[1, :, : 2 * fw], LAST)
        ).astype(ref.dtype)


def feed_back(d_mine, d_theirs, slope, silu, w, fw):
    rows, width = d_mine.shape
    return call(
        functools.partial(feed_back_body, fw),
        [shape((2 * rows, 2 * fw))] * 2 + [shape((rows, width), F32), shape((rows, width))],
        [VM] * 6 + [ANY] * 16,
        [VM] * 4,
        [pltpu.VMEM((2, width, 2 * fw + 512), BF), pltpu.SemaphoreType.DMA((16,))],
    )(d_mine, d_theirs, *slope, *silu, *w)


def send_out(store, outs, sem, p, i, copies):
    step = outs[0].shape[0]
    for side in range(2):
        n = 8 * i + 2 * p + side
        spot = store.at[4 * i + p, pl.ds(side * step, step)]
        copies.append(pltpu.make_async_copy(spot, outs[n], sem.at[n]))
        copies[-1].start()


def weight_grad_body(left_mine, left_theirs, *refs):
    right = refs[:2]
    outs = refs[2:18]
    store, sem = refs[18:]
    rows = left_mine.shape[0]
    step = 2 * outs[0].shape[0]
    copies = []
    for p in range(4):
        spot = pl.ds(p * step, step)
        for i in range(2):
            value = dot(left_mine[:, spot], right[i][:rows, :], ROWS)
            value += dot(left_theirs[:, spot], right[i][rows:, :], ROWS)
            store[4 * i + p] = value.astype(BF)
            send_out(store, outs, sem, p, i, copies)
    for c in copies:
        c.wait()


def weight_grad(left_mine, left_theirs, right):
    rows, width = left_mine.shape
    cols = right[0].shape[1]
    step = width // 8
    return call(
        weight_grad_body,
        [shape((step, cols))] * 16,
        [VM] * 4,
        [ANY] * 16,
        [pltpu.VMEM((8, 2 * step, cols), BF), pltpu.SemaphoreType.DMA((16,))],
    )(left_mine, left_theirs, *right)


def attend_back_body(sides, d_mine, d_theirs, q_ref, row_ids, lse, cosine, sine, *refs):
    arrays = sides if sides <= 2 else 1
    kvs, refs = refs[:arrays], refs[arrays:]
    w = refs[:16]
    dq_ref, own_ref, send_ref = refs[16:19]
    store, mix, d_kv, sem = refs[19:]
    waits = [fetch(w[8 * i : 8 * i + 8], store.at[i], sem, 8 * i) for i in range(2)]
    rows = q_ref.shape[0]
    half = rows // 2
    qw = q_ref.shape[1] // 2
    for i in range(2):
        waits[i]()
        for side, ref in enumerate((d_mine, d_theirs)):
            mix[i, pl.ds(side * half, half), :] = dot(ref[...], store[i])[:, 320 : 320 + qw].astype(BF)
    ids = row_ids[0:1, :]
    read = reader(kvs, rows)

    def look(s):
        return read(s, ID_LANE).astype(F32) <= ids

    looks = [look(s) for s in range(sides)] if sides <= 2 else None
    d_q = []
    c = FACTOR * LOG2E
    head = 0
    for i in range(2):
        for start in range(0, qw, HEAD_DIM):
            q = q_ref[:, i * qw + start : i * qw + start + HEAD_DIM]
            dm = mix[i, :, start : start + HEAD_DIM]
            level = lse[head : head + 1, :]
            head += 1

            def pair(s):
                seen = looks[s] if looks else look(s)
                p = jnp.where(seen, jnp.exp2(dot(read(s, lanes(i)), q, LAST) * c - level), 0.0)
                return p, dot(read(s, lanes(2 + i)), dm, LAST)

            held = [pair(s) for s in range(sides)] if sides <= 2 else None

            def weigh(s, delta):
                p, dp = held[s] if held else pair(s)
                return delta + jnp.sum(p * dp, axis=0, keepdims=True)

            delta = each(sides, weigh, jnp.zeros((1, rows), F32))

            def grads(s, out):
                p, dp = held[s] if held else pair(s)
                ds = (p * (dp - delta)).astype(BF)
                d_value = dot(p.astype(BF), dm)
                d_key = dot(ds, q)
                if start == 0:
                    d_kv[2 + i, s] = d_value
                    d_kv[i, s] = d_key
                else:
                    d_kv[2 + i, s] += d_value
                    d_kv[i, s] += d_key
                return out + dot(read(s, lanes(i)), ds, ROWS)

            d_q.append(each(sides, grads, jnp.zeros((HEAD_DIM, rows), F32)))
    tall = jnp.concatenate(d_q + [jnp.zeros((512 - 4 * HEAD_DIM, rows), F32)], axis=0).T * FACTOR
    cos, sin = cosine[...], sine[...]
    dq_ref[...] = jnp.concatenate(
        [rotated(tall[:, h * HEAD_DIM : (h + 1) * HEAD_DIM], cos, -sin) for h in range(4)], axis=1
    ).astype(BF)
    for s in range(sides):
        value = jnp.concatenate([d_kv[0, s] * FACTOR, d_kv[1, s] * FACTOR, d_kv[2, s], d_kv[3, s]], axis=1)
        if s == 0:
            own_ref[...] = value
        else:
            send_ref[pl.ds((s - 1) * rows, rows), :] = value.astype(BF)


def attend_back(d_mine, d_theirs, q, kvs, row_ids, lse, cosine, sine, w, sides):
    rows = q.shape[0]
    width = d_mine.shape[1]
    cols = 4 * HEAD_DIM
    return call(
        functools.partial(attend_back_body, sides),
        [shape(q.shape), shape((rows, cols), F32), shape(((sides - 1) * rows, cols))],
        [VM] * (7 + len(kvs)) + [ANY] * 16,
        [VM] * 3,
        [
            pltpu.VMEM((2, width, 512), BF),
            pltpu.VMEM((2, rows, q.shape[1] // 2), BF),
            pltpu.VMEM((4, sides, rows, HEAD_DIM), F32),
            pltpu.SemaphoreType.DMA((16,)),
        ],
    )(d_mine, d_theirs, q, row_ids, lse, cosine, sine, *kvs, *w)


def project_back_body(x_mine, x_theirs, dq_ref, own_ref, got_ref, cosine, sine, *refs):
    w = refs[:16]
    d_qkv = refs[16:18]
    mine, theirs, gain_ref = refs[18:21]
    store, sem = refs[21:]
    waits = [fetch(w[8 * i : 8 * i + 8], store.at[i], sem, 8 * i) for i in range(2)]
    qw = dq_ref.shape[1] // 2
    cos, sin = cosine[...], sine[...]
    d_kv = own_ref[...] + got_ref[...].astype(F32)
    d_q = dq_ref[...].astype(F32)
    rows = d_q.shape[0]
    for i in range(2):
        d_k = rotated(d_kv[:, i * HEAD_DIM : (i + 1) * HEAD_DIM], cos, -sin)
        d_v = d_kv[:, (2 + i) * HEAD_DIM : (3 + i) * HEAD_DIM]
        d_qkv[i][...] = padded(
            jnp.concatenate([d_q[:, i * qw : (i + 1) * qw], d_k, d_v], axis=1), 512
        ).astype(BF)
    for i in range(2):
        waits[i]()
    half = rows // 2
    width = mine.shape[1]
    total = 0.0
    for side, ref, x_ref in ((1, theirs, x_theirs), (0, mine, x_mine)):
        spot = pl.ds(side * half, half)
        part = dot(d_qkv[0][spot, :], store[0], LAST) + dot(d_qkv[1][spot, :], store[1], LAST)
        ref[...] = part.astype(ref.dtype)
        x = x_ref[:, :width].astype(F32)
        total = total + jnp.sum(part * (x * mean_scale(x)), axis=0, keepdims=True)
    gain_ref[...] = total


def project_back(x_mine, x_theirs, dq, own, got, cosine, sine, w):
    rows, width = x_mine.shape
    width -= 128
    return call(
        project_back_body,
        [shape((2 * rows, 512))] * 2 + [shape((rows, width), F32), shape((rows, width)), shape((1, width), F32)],
        [VM] * 7 + [ANY] * 16,
        [VM] * 5,
        [pltpu.VMEM((2, width, 512), BF), pltpu.SemaphoreType.DMA((16,))],
    )(x_mine, x_theirs, dq, own, got, cosine, sine, *w)


def attn_grad_body(first, d_mine, d_theirs, gain_one, gain_two, sum_attn, sums, *refs):
    d_qkv, mixed = refs[:2], refs[2:4]
    outs = refs[4:20]
    store, sem = refs[20:]
    half = d_mine.shape[0]
    step = 2 * outs[0].shape[0]
    copies = []
    lane = lax.broadcasted_iota(jnp.int32, (1, 128), 1)
    tail = jnp.where(lane == 98, sums[0:1, :], 0.0)
    tail = jnp.where(lane == 99, sum_attn[0:1, :], tail)
    tail = jnp.where(lane == 100, sums[8:9, :], tail)
    for p in range(4):
        spot = pl.ds(p * step, step)
        tall = jnp.concatenate(
            [
                jnp.zeros((96, step), F32),
                gain_one[:, spot],
                gain_two[:, spot],
                jnp.zeros((30, step), F32),
            ],
            axis=0,
        ).T
        for i in range(2):
            value = dot(first[:, spot], d_qkv[i][...], ROWS)
            value += dot(d_mine[:, spot], mixed[i][:half, :], ROWS)
            value += dot(d_theirs[:, spot], mixed[i][half:, :], ROWS)
            store[4 * i + p, :, :384] = value[:, :384].astype(BF)
            store[4 * i + p, :, 384:] = (value[:, 384:] + tall + tail).astype(BF)
            send_out(store, outs, sem, p, i, copies)
    for c in copies:
        c.wait()


def attn_grad(first, d_mine, d_theirs, gain_one, gain_two, sum_attn, sums, d_qkv, mixed):
    rows, width = first.shape
    step = width // 8
    return call(
        attn_grad_body,
        [shape((step, 512))] * 16,
        [VM] * 11,
        [ANY] * 16,
        [pltpu.VMEM((8, 2 * step, 512), BF), pltpu.SemaphoreType.DMA((16,))],
    )(first, d_mine, d_theirs, gain_one, gain_two, sum_attn, sums, *d_qkv, *mixed)


def hold(values, *others):
    values = list(values)
    got = lax.optimization_barrier(tuple(values) + tuple(others))
    return list(got[: len(values)])


class Place:
    def __init__(self):
        self.count = lax.axis_size("seq")
        self.inner = self.count // PARTS
        s = lax.axis_index("seq")
        m = lax.axis_index("mp")
        self.s = s
        self.z = s // self.inner
        self.y = s % self.inner
        self.x = m // 2
        self.c = m % 2
        self.zs = self.z.reshape(1).astype(jnp.int32)
        self.bits = []
        b = 1
        while b < self.inner:
            self.bits.append(b)
            b *= 2

    def hop_z(self, v, k):
        return hop(v, "seq", k * self.inner)

    def hop_y(self, v, b):
        return hop(v, "seq", b)

    def hop_x(self, v):
        return hop(v, "mp", 2)

    def hop_c(self, v):
        return hop(v, "mp", 1)

    def low_y(self, v):
        for b in self.bits[:-1]:
            v = jnp.concatenate([v, self.hop_y(v, b)], 0)
        return v

    def far_y(self, v):
        return self.hop_y(v, self.bits[-1])

    def spread(self, k, v):
        if k % 2 == 0:
            v = self.low_y(v)
            w = self.far_y(v)
            return (v, w), (self.hop_x(v), self.hop_x(w))
        u = self.low_y(self.hop_x(v))
        v = self.low_y(v)
        return (v, self.far_y(v)), (u, self.far_y(u))

    def add(self, own, got):
        return (own.astype(F32) + got.astype(F32)).astype(BF)

    def collect_y(self, own, far):
        value = self.add(own, self.far_y(far))
        for b in reversed(self.bits[:-1]):
            n = value.shape[0] // 2
            value = self.add(value[:n], self.hop_y(value[n:], b))
        return value

    def collect(self, k, own, other):
        if k % 2 == 0:
            v, w = [self.add(a, self.hop_x(b)) for a, b in zip(own, other)]
            return self.collect_y(v, w)
        u = self.collect_y(*other)
        return self.add(self.collect_y(*own), self.hop_x(u))

    def gather(self, own, width):
        one = self.hop_z(own, 1)
        two = self.hop_z(own, 2)
        three = self.hop_z(two, 1)
        mine = stack([own, one, two, three], width)
        return mine, self.hop_c(mine)

    def scatter(self, mine, theirs, width):
        one, three, keep = first_sum(mine, self.hop_c(theirs))
        three = self.hop_z(three, 1)
        two = self.hop_z(second_sum(keep, three, width), 2)
        one = self.hop_z(one, 1)
        return keep, one, two


def tables(place):
    half = HEAD_DIM // 2
    freq = THETA ** (-(jnp.arange(half, dtype=F32) * 2.0 / HEAD_DIM))
    angle = place[:, None] * freq[None, :]
    return (jnp.cos(angle), jnp.sin(angle))


def on_device(
    inputs,
    targets,
    seq_ids,
    block_ids,
    attn_gain,
    mlp_gain,
    w_query,
    w_key,
    w_value,
    w_out,
    w_gate,
    w_up,
    w_down,
):
    at = Place()
    inner = at.inner
    full = inputs.shape[1]
    width = full // PARTS
    half_span = SPAN // 2
    kw = w_key.shape[1] // 2
    qw = w_query.shape[1] // PARTS
    fw = w_gate.shape[1] // PARTS
    row_f32 = shape((half_span, full), F32)
    row_bf = shape((half_span, full))

    off = jnp.where(seq_ids[0] == at.x, 0, SPAN)
    where = jnp.stack([off + at.c * half_span, at.s]).astype(jnp.int32)
    spots = [
        (off if xr == 0 else SPAN - off) + (at.c ^ cr) * half_span for xr in range(2) for cr in range(2)
    ]
    spots = jnp.stack(spots).astype(jnp.int32)

    def all_rows(own):
        across = at.hop_x(own)
        return spread_rows(spots, [own, at.hop_c(own), across, at.hop_c(across)])

    rows = 2 * PARTS * half_span
    count = jnp.arange(rows, dtype=jnp.int32)
    zz = at.z ^ ((count // half_span) % PARTS)
    cc = at.c ^ (count // (half_span * PARTS))
    place = ((zz * inner + at.y) * SPAN + cc * half_span + count % half_span).astype(F32)
    cosine, sine = tables(place)

    gains = jnp.stack([attn_gain, mlp_gain], -1)
    takes = [(qw, 1), (kw, 2), (kw, 2), (qw, 1), (2, 4)]
    piece = pack(at.zs, [w_query, w_key, w_value, w_out, gains], takes, 512)
    x_own, t_own = own_rows(where, block_ids.reshape(-1, 1), inputs, targets, at.count)

    def spread_all(got):
        w = [at.spread(k, got[k]) for k in range(PARTS)]
        return [v for i in range(2) for k in range(PARTS) for v in w[k][i]]

    got_qo = [piece[0]] + [at.hop_z(piece[k], k) for k in range(1, PARTS)]
    w_qo = spread_all(got_qo)
    x_mine, x_theirs = at.gather(x_own, width)

    piece = pack(at.zs, [w_gate, w_up, w_down], [(fw, 1)] * 3, 2 * fw + 512)
    piece = hold(piece, *got_qo, x_mine)
    got = [piece[0]] + [at.hop_z(piece[k], k) for k in range(1, PARTS)]
    w_ff = spread_all(got)

    first, query, kv, gain, row_ids = project(x_mine, x_theirs, cosine, sine, w_qo, qw)
    kvs = [kv]
    for b in at.bits:
        kvs = kvs + [at.hop_y(v, b) for v in kvs]
    if inner > 2:
        kvs = [jnp.concatenate(kvs, 0)]
    mixed_a, mixed_b, lse, mine, theirs = attend(query, kvs, row_ids, w_qo, inner)
    left = at.scatter(mine, theirs, width)
    middle, n_own, sum_attn = call(
        functools.partial(after_attn_body, width),
        [row_f32, row_bf, shape((8, 128), F32)],
        [VM] * 5,
        [VM] * 3,
    )(*left, x_own, gain)
    n_mine, n_theirs = at.gather(n_own, width)
    out = feed(n_mine, n_theirs, w_ff, fw)
    hidden, slope, silu, (mine, theirs) = out[:2], out[2:4], out[4:6], out[6:]
    left = at.scatter(mine, theirs, width)
    d_own, layer_own, sums = call(
        functools.partial(after_mlp_body, width, at.count),
        [row_bf, row_bf, shape((16, 128), F32)],
        [SM] + [VM] * 5,
        [VM] * 3,
    )(where, *left, middle, t_own)

    d_mine, d_theirs = at.gather(d_own, width)
    grad_d = weight_grad(d_mine, d_theirs, hidden)
    d_mine, d_theirs, *_ = hold([d_mine, d_theirs], grad_d[0])
    out = feed_back(d_mine, d_theirs, slope, silu, w_ff, fw)
    d_gu, (mine, theirs) = out[:2], out[2:]
    left = at.scatter(mine, theirs, width)
    grad_gu = weight_grad(n_mine, n_theirs, d_gu)
    d_middle, a_own, grad_gain_two = call(
        functools.partial(after_feed_back_body, width),
        [row_f32, row_bf, shape((1, full), F32)],
        [VM] * 6,
        [VM] * 3,
    )(*left, middle, d_own, gain)
    a_mine, a_theirs = at.gather(a_own, width)
    d_query, d_kv, sent = attend_back(
        a_mine, a_theirs, query, kvs, row_ids, lse, cosine, sine, w_qo, inner
    )
    if inner > 2:
        sent = jnp.concatenate([d_kv, sent.astype(F32)], 0)
        for b in reversed(at.bits[1:]):
            n = sent.shape[0] // 2
            sent = sent[:n] + at.hop_y(sent[n:].astype(BF), b).astype(F32)
        d_kv, sent = sent[:rows], sent[rows:].astype(BF)
    sent = at.hop_y(sent, at.bits[0])
    out = project_back(x_mine, x_theirs, d_query, d_kv, sent, cosine, sine, w_qo)
    d_qkv, mine, theirs, grad_gain_one = out[:2], out[2], out[3], out[4]
    left = at.scatter(mine, theirs, width)
    grad_qo = attn_grad(
        first, a_mine, a_theirs, grad_gain_one, grad_gain_two, sum_attn, sums, d_qkv, (mixed_a, mixed_b)
    )
    (input_own,) = call(
        functools.partial(after_all_body, width, at.count),
        [row_bf],
        [SM] + [VM] * 6,
        [VM],
    )(where, *left, x_own, d_middle, gain)

    layer_out = all_rows(layer_own)
    input_grad = all_rows(input_own)

    def arrive(grads):
        got = []
        for k in reversed(range(PARTS)):
            own, other = grads[2 * k : 2 * k + 2], grads[8 + 2 * k : 10 + 2 * k]
            v = at.collect(k, own, other)
            got.append(at.hop_z(v, k) if k else v)
        return got[::-1]

    (g_down,) = unpack(at.zs, arrive(grad_d), [(0, fw, 1)])
    g_gate, g_up = unpack(at.zs, arrive(grad_gu), [(0, fw, 1), (fw, fw, 1)])
    takes = [(0, qw, 1), (qw, kw, 2), (qw + kw, kw, 2), (qw + 2 * kw, qw, 1)]
    got_qo = arrive(grad_qo)
    g_query, g_key, g_value, g_out = unpack(at.zs, got_qo, takes)
    tails = sum(p[:, 384:512].astype(F32) for p in got_qo)
    tails = tails + at.hop_c(tails)
    entries = inputs.shape[0] * lax.axis_size("seq") * inputs.shape[1]
    rms = jnp.sqrt(tails[0, 98:101] / entries + EPS)
    return (
        layer_out,
        input_grad,
        g_query,
        g_key,
        g_value,
        g_out,
        g_gate,
        g_up,
        g_down,
        tails[:, 96],
        tails[:, 97],
        rms[0],
        rms[1],
        rms[2],
    )


def solution(mesh):
    return jax.shard_map(
        on_device,
        mesh=mesh,
        in_specs=(
            P("seq", None),
            P("seq", None),
            P("seq"),
            P("seq"),
            P("seq"),
            P("seq"),
            P("seq", "mp"),
            P("seq", "mp"),
            P("seq", "mp"),
            P("seq", "mp"),
            P("seq", "mp"),
            P("seq", "mp"),
            P("seq", "mp"),
        ),
        out_specs=(
            P("seq", None),
            P("seq", None),
            P("seq", "mp"),
            P("seq", "mp"),
            P("seq", "mp"),
            P("seq", "mp"),
            P("seq", "mp"),
            P("seq", "mp"),
            P("seq", "mp"),
            P("seq"),
            P("seq"),
            P(),
            P(),
            P(),
        ),
        check_vma=False,
    )
```

```python
import functools

import jax
import jax.numpy as jnp
from jax import lax
from jax.experimental import pallas as pl
from jax.experimental.pallas import tpu as pltpu
from jax.sharding import Mesh
from jax.sharding import PartitionSpec as P

HEAD_DIM = 80
SPAN = 128
EPS = 1e-05
THETA = 1000000.0
PARTS = 4
BF = jnp.bfloat16
F32 = jnp.float32
FACTOR = HEAD_DIM**-0.5
LOG2E = 1.4426950408889634
LIMIT = 56 * 1024 * 1024

PLAIN = (((1,), (0,)), ((), ()))
LAST = (((1,), (1,)), ((), ()))
ROWS = (((0,), (0,)), ((), ()))

VM = pl.BlockSpec(memory_space=pltpu.VMEM)
SM = pl.BlockSpec(memory_space=pltpu.SMEM)
ANY = pl.BlockSpec(memory_space=pl.ANY)


def shape(dims, kind=BF):
    return jax.ShapeDtypeStruct(tuple(dims), kind)


def call(body, outs, in_specs, out_specs, scratch=(), cost=2):
    return pl.pallas_call(
        body,
        out_shape=outs,
        in_specs=in_specs,
        out_specs=out_specs,
        scratch_shapes=list(scratch),
        compiler_params=pltpu.CompilerParams(vmem_limit_bytes=LIMIT),
        cost_estimate=pl.CostEstimate(flops=cost * 10**9, bytes_accessed=0, transcendentals=0),
    )


AXES = ("z", "y", "x", "c")


def hop(value, axis, k):
    size = lax.axis_size(axis)
    return lax.ppermute(value, axis, [(i, i ^ k) for i in range(size)])


def dot(left, right, dims=PLAIN):
    return lax.dot_general(left, right, dims, preferred_element_type=F32)


def joined(values, width):
    values = [v.astype(F32) for v in values]
    have = sum(v.shape[1] for v in values)
    if have < width:
        values.append(jnp.zeros((values[0].shape[0], width - have), F32))
    return jnp.concatenate(values, axis=1).astype(BF)


def pack_body(takes, width, cut, z_ref, *refs):
    count = len(takes)
    ins, outs = refs[:count], refs[count:]
    for k in range(PARTS):
        part = z_ref[0] ^ k
        for j in range(PARTS):

            @pl.when(part == j)
            def _():
                values = [ref[:, pl.ds(step * (j // share), step)] for ref, (step, share) in zip(ins, takes)]
                value = joined(values, width)
                if cut and k >= 2:
                    outs[k][...] = value[:, :cut]
                    outs[k + 2][...] = value[:, cut:]
                else:
                    outs[k][...] = value


def pack(z, arrays, takes, width, cut=None):
    depth = arrays[0].shape[0]
    outs = [shape((depth, width))] * PARTS
    if cut:
        outs = outs[:2] + [shape((depth, cut))] * 2 + [shape((depth, width - cut))] * 2
    return call(
        functools.partial(pack_body, takes, width, cut),
        outs,
        [SM] + [VM] * len(arrays),
        [VM] * len(outs),
    )(z, *arrays)


def pack_attn_body(z_ref, wq, wk, wv, wo, gain_one, gain_two, *outs):
    depth, width = outs[0].shape
    kw = wk.shape[0] // 2
    qw = wq.shape[1] // PARTS
    narrow = jnp.concatenate([wk[...].astype(F32), wv[...].astype(F32)], axis=0)
    gains = jnp.concatenate([gain_one[...], gain_two[...]], axis=0).astype(F32)
    fill = jnp.zeros((128 - (4 * kw + 2) % 128, depth), F32)
    tall = jnp.concatenate([narrow, gains, fill], axis=0).T
    for k in range(PARTS):
        part = z_ref[0] ^ k
        for j in range(PARTS):

            @pl.when(part == j)
            def _():
                spot = pl.ds(qw * j, qw)
                h = j // 2
                values = [
                    wq[:, spot],
                    tall[:, kw * h : kw * h + kw],
                    tall[:, kw * (h + 2) : kw * (h + 3)],
                    wo[:, spot],
                    tall[:, 4 * kw : 4 * kw + 2],
                ]
                outs[k][...] = joined(values, width)


def pack_attn(z, wq, wk, wv, wo, gain_one, gain_two, width):
    depth = wq.shape[0]
    return call(
        pack_attn_body, [shape((depth, width))] * PARTS, [SM] + [VM] * 6, [VM] * PARTS
    )(z, wq, wk.T, wv.T, wo, gain_one.reshape(1, -1), gain_two.reshape(1, -1))


def unpack_body(takes, cut, z_ref, *refs):
    count = PARTS + 2 if cut else PARTS
    ins, outs = refs[:count], refs[count:]
    for ref, (start, step, share) in zip(outs, takes):
        if share == 2:
            ref[...] = jnp.zeros_like(ref)
    for k in range(PARTS):
        part = z_ref[0] ^ k
        for j in range(PARTS):

            @pl.when(part == j)
            def _():
                for ref, (start, step, share) in zip(outs, takes):
                    late = cut and k >= 2 and start >= cut
                    piece = ins[k + 2] if late else ins[k]
                    value = piece[:, pl.ds(start - cut if late else start, step)].astype(F32)
                    spot = pl.ds(step * (j // share), step)
                    if share == 1:
                        ref[:, spot] = value
                    else:
                        ref[:, spot] += value


def unpack(z, pieces, takes, cut=None):
    depth = pieces[0].shape[0]
    return call(
        functools.partial(unpack_body, takes, cut),
        [shape((depth, step * PARTS // share), F32) for start, step, share in takes],
        [SM] + [VM] * len(pieces),
        [VM] * len(takes),
        cost=4,
    )(z, *pieces)


def spot_of(pos, k, j, inner, depth):
    return pl.ds(pl.multiple_of(((pos[1] ^ k) * inner + (pos[2] ^ j)) * depth, 16), depth)


def piece_copies(pos, inner, pieces, store, sem, i, back=False):
    half = inner // 2
    depth = store.shape[1] // (PARTS * inner)
    copies = []
    for k in range(PARTS):
        for j in range(inner):
            ends = (
                pieces[2 * k + j // half].at[pl.ds((j % half) * depth, depth)],
                store.at[i, spot_of(pos, k, j, inner, depth)],
            )
            n = (i * PARTS + k) * inner + j
            copies.append(pltpu.make_async_copy(*(ends[::-1] if back else ends), sem.at[n]))
    return copies


def fetch(pos, inner, pieces, store, sem):
    copies = [piece_copies(pos, inner, pieces[8 * i : 8 * i + 8], store, sem, i) for i in range(2)]
    return start_all(copies)


def start_all(copies):
    for half in copies:
        for c in half:
            c.start()

    def wait(i):
        for c in copies[i]:
            c.wait()

    return wait


def own_rows_body(pos, ids, x_ref, t_ref, x_out, t_out, tall):
    spot = pl.ds(pl.multiple_of(pos[0], 64), 64)
    width = x_ref.shape[1]
    tall[...] = jnp.broadcast_to(ids[...].astype(F32), tall.shape[::-1]).T
    x_out[:, :width] = x_ref[spot, :]
    x_out[:, width:] = tall[spot, :].astype(BF)
    t_out[...] = t_ref[spot, :]


def own_rows(pos, ids, x, t):
    rows, width = x.shape
    return call(
        own_rows_body,
        [shape((64, width + 128)), shape((64, width))],
        [SM] + [VM] * 3,
        [VM] * 2,
        [pltpu.VMEM((rows, 128), F32)],
    )(pos, ids, x, t)


def stack_body(own, one, two, three, out):
    n = own.shape[0]
    for k, ref in enumerate((own, one, two, three)):
        out[pl.ds(k * n, n), :] = ref[...]


def stack(pieces):
    n, cols = pieces[0].shape
    return call(stack_body, shape((4 * n, cols)), [VM] * 4, VM)(*pieces)


def first_sum_body(mine, got, one, three, keep):
    n = one.shape[0]

    def piece(k):
        spot = pl.ds(k * n, n)
        return mine[spot, :] + got[spot, :].astype(F32)

    three[...] = piece(3).astype(BF)
    one[...] = piece(1).astype(BF)
    keep[:n, :] = piece(0)
    keep[n:, :] = piece(2)


def first_sum(mine, got):
    n, width = mine.shape
    n //= 4
    return call(
        first_sum_body, [shape((n, width))] * 2 + [shape((2 * n, width), F32)], [VM] * 2, [VM] * 3
    )(mine, got)


def second_sum_body(keep, three, out):
    n = out.shape[0]
    out[...] = (keep[n:, :] + three[...].astype(F32)).astype(BF)


def second_sum(keep, three):
    return call(second_sum_body, shape(three.shape), [VM] * 2, VM)(keep, three)


def last_sum(keep, one, two):
    n = one.shape[0]
    return keep[:n, :] + one[...].astype(F32) + two[...].astype(F32)


def mean_scale(value):
    return lax.rsqrt(jnp.mean(value * value, axis=-1, keepdims=True) + EPS)


def back_norm(grad, value, gain):
    scale = mean_scale(value)
    unit = value * scale
    scaled = grad * gain
    return unit, scale * (scaled - unit * jnp.mean(scaled * unit, axis=-1, keepdims=True))


def after_attn_body(keep, one, two, x_own, gain, middle, n_own, total):
    branch = last_sum(keep, one, two)
    value = x_own[:, : branch.shape[1]].astype(F32) + branch
    middle[...] = value
    n_own[...] = (value * mean_scale(value) * gain[1:2, :]).astype(BF)
    total[...] = jnp.full(total.shape, jnp.sum(branch * branch), F32)


def after_mlp_body(keep, one, two, middle, target, d_own, out, total):
    branch = last_sum(keep, one, two)
    stream = middle[...] + branch
    d_own[...] = (stream - target[...].astype(F32)).astype(BF)
    out[...] = stream.astype(BF)
    total[0:8, :] = jnp.full((8, 128), jnp.sum(stream * stream), F32)
    total[8:16, :] = jnp.full((8, 128), jnp.sum(branch * branch), F32)


def after_feed_back_body(keep, one, two, middle, d_own, gain, d_middle, a_own, gain_grad):
    grad = last_sum(keep, one, two)
    unit, back = back_norm(grad, middle[...], gain[1:2, :])
    value = d_own[...].astype(F32) + back
    d_middle[...] = value
    a_own[...] = value.astype(BF)
    gain_grad[...] = jnp.sum(grad * unit, axis=0, keepdims=True)


def after_all_body(keep, one, two, x_own, d_middle, gain, out):
    grad = last_sum(keep, one, two)
    unit, back = back_norm(grad, x_own[:, : grad.shape[1]].astype(F32), gain[0:1, :])
    out[...] = (d_middle[...] + back).astype(BF)


def spread_rows_body(spots, p0, p1, p2, p3, out):
    n = p0.shape[0]
    for i, ref in enumerate((p0, p1, p2, p3)):
        out[pl.ds(pl.multiple_of(spots[i], 64), n), :] = ref[...]


def spread_rows(spots, pieces):
    n, width = pieces[0].shape
    return call(spread_rows_body, shape((4 * n, width)), [SM] + [VM] * 4, VM)(spots, *pieces)


def rotated(value, cosine, sine):
    half = HEAD_DIM // 2
    a, b = value[:, :half], value[:, half:]
    return jnp.concatenate([a * cosine - b * sine, b * cosine + a * sine], axis=1)


def project_body(qw, inner, pos, x_mine, x_theirs, cosine, sine, *refs):
    w = refs[:16]
    first, q_ref, kv_ref, gains, row_ids = refs[16:21]
    store, sem = refs[21:]
    wait = fetch(pos, inner, w, store, sem)
    width = first.shape[1]
    step = width // 4
    ids = jnp.concatenate([x_mine[:, width:], x_theirs[:, width:]], axis=0).astype(F32)
    row_ids[...] = ids.T[0:8, :]
    wait(0)
    spot = 480 - 384
    for p in range(4):
        tail = store[0, pl.ds(p * step, step), 384:512].astype(F32).T
        gains[:, pl.ds(p * step, step)] = tail[spot : spot + 8]
    gain = gains[0:1, :]
    rows = x_mine.shape[0]
    for i, ref in enumerate((x_mine, x_theirs)):
        value = ref[:, :width].astype(F32)
        first[pl.ds(i * rows, rows), :] = (value * mean_scale(value) * gain).astype(BF)
    cos, sin = cosine[...], sine[...]
    queries, keys, values = [], [], []
    for i in range(2):
        if i:
            wait(1)
        out = dot(first[...], store[i])
        for start in range(0, qw, HEAD_DIM):
            queries.append(rotated(out[:, start : start + HEAD_DIM], cos, sin))
        keys.append(rotated(out[:, qw : qw + HEAD_DIM], cos, sin))
        values.append(out[:, qw + HEAD_DIM : qw + 2 * HEAD_DIM])
    q_ref[...] = jnp.concatenate(queries, axis=1).astype(BF)
    kv_ref[...] = jnp.concatenate(keys + values + [ids[:, :64]], axis=1).astype(BF)


def sems(inner):
    return pltpu.SemaphoreType.DMA((2 * PARTS * inner,))


def project(pos, x_mine, x_theirs, cosine, sine, w, qw, inner):
    rows, width = x_mine.shape
    rows *= 2
    width -= 128
    return call(
        functools.partial(project_body, qw, inner),
        [
            shape((rows, width)),
            shape((rows, 2 * qw)),
            shape((rows, 384)),
            shape((8, width), F32),
            shape((8, rows), F32),
        ],
        [SM] + [VM] * 4 + [ANY] * 16,
        [VM] * 5,
        [pltpu.VMEM((2, width, 512), BF), sems(inner)],
        cost=12,
    )(pos, x_mine, x_theirs, cosine, sine, *w)


def out_sides(partial, mine, theirs):
    n = mine.shape[0]
    mine[...] = partial[:n]
    theirs[...] = partial[n:].astype(theirs.dtype)


def each(count, step, start):
    if count <= 2:
        for s in range(count):
            start = step(s, start)
        return start
    return lax.fori_loop(0, count, step, start)


def reader(kvs, rows):
    def read(s, lane):
        if len(kvs) > 1:
            return kvs[s][:, lane]
        return kvs[0][pl.ds(pl.multiple_of(s * rows, rows), rows), lane]

    return read


def lanes(i):
    return pl.ds(i * HEAD_DIM, HEAD_DIM)


ID_LANE = pl.ds(4 * HEAD_DIM, 1)


def attend_body(sides, pos, q_ref, row_ids, *refs):
    arrays = sides if sides <= 2 else 1
    kvs, refs = refs[:arrays], refs[arrays:]
    w = refs[:16]
    mixed = refs[16:18]
    lse, mine, theirs = refs[18:21]
    store, sem = refs[21:]
    wait = fetch(pos, sides, w, store, sem)
    rows = q_ref.shape[0]
    qw = q_ref.shape[1] // 2
    ids = row_ids[0:1, :]
    read = reader(kvs, rows)

    def look(s):
        return read(s, ID_LANE).astype(F32) <= ids

    looks = [look(s) for s in range(sides)] if sides <= 2 else None
    lse[...] = jnp.zeros_like(lse)
    head = 0
    c = FACTOR * LOG2E
    for i in range(2):
        outs = []
        for start in range(i * qw, (i + 1) * qw, HEAD_DIM):
            q = q_ref[:, start : start + HEAD_DIM]

            def score(s):
                seen = looks[s] if looks else look(s)
                return jnp.where(seen, dot(read(s, lanes(i)), q, LAST), -1e30)

            scores = [score(s) for s in range(sides)] if sides <= 2 else None

            def highest(s, top):
                value = scores[s] if scores else score(s)
                return jnp.maximum(top, jnp.max(value, axis=0, keepdims=True))

            top = each(sides, highest, jnp.full((1, rows), -1e30, F32))

            def gathered(s, carry):
                total, out = carry
                value = scores[s] if scores else score(s)
                p = jnp.exp2(value * c - top * c)
                total = total + jnp.sum(p, axis=0, keepdims=True)
                return total, out + dot(read(s, lanes(2 + i)), p.astype(BF), ROWS)

            nothing = (jnp.zeros((1, rows), F32), jnp.zeros((HEAD_DIM, rows), F32))
            total, out = each(sides, gathered, nothing)
            outs.append(out / total)
            lse[head : head + 1, :] = top * c + jnp.log2(total)
            head += 1
        fill = jnp.zeros((512 - 320 - qw, rows), F32)
        tall = jnp.concatenate([jnp.zeros((320, rows), F32)] + outs + [fill], axis=0)
        mixed[i][...] = tall.T.astype(BF)
    for i in range(2):
        wait(i)
    partial = dot(mixed[0][...], store[0], LAST) + dot(mixed[1][...], store[1], LAST)
    out_sides(partial, mine, theirs)


def attend(pos, q, kvs, row_ids, w, sides):
    rows = q.shape[0]
    width = 8 * w[0].shape[0]
    return call(
        functools.partial(attend_body, sides),
        [shape((rows, 512))] * 2
        + [shape((8, rows), F32), shape((rows // 2, width), F32), shape((rows // 2, width))],
        [SM] + [VM] * (2 + len(kvs)) + [ANY] * 16,
        [VM] * 5,
        [pltpu.VMEM((2, width, 512), BF), sems(sides)],
        cost=12,
    )(pos, q, row_ids, *kvs, *w)


def padded(value, width):
    return jnp.concatenate([value, jnp.zeros((value.shape[0], width - value.shape[1]), value.dtype)], axis=1)


def block_copies(pos, inner, arrays, store, sem, i):
    depth = arrays[0].shape[1] // 2
    copies = []
    for k in range(PARTS):
        for j in range(inner):
            n = k * inner + j
            spot = arrays[k // 2].at[j * 2 + (pos[3] ^ i), pl.ds((k % 2) * depth, depth)]
            to = store.at[i, pl.ds(pl.multiple_of(((pos[1] ^ k) * inner + j) * depth, 16), depth)]
            copies.append(pltpu.make_async_copy(spot, to, sem.at[i * PARTS * inner + n]))
    return copies


def feed_body(fw, inner, pos, n_mine, n_theirs, near, far, *refs):
    hidden, slope, silu = refs[0:2], refs[2:4], refs[4:6]
    mine, theirs = refs[6:8]
    rows_in, store, sem = refs[8:]
    wait = start_all([block_copies(pos, inner, (near, far), store, sem, i) for i in range(2)])
    rows = n_mine.shape[0]
    rows_in[:rows, :] = n_mine[...]
    rows_in[rows:, :] = n_theirs[...]
    for i in range(2):
        wait(i)
        out = dot(rows_in[...], store[i, :, : 2 * fw])
        gate, upper = out[:, :fw], out[:, fw:]
        sigma = jax.nn.sigmoid(gate)
        act = gate * sigma
        hidden[i][...] = padded(act * upper, 512).astype(BF)
        slope[i][...] = padded(upper * (sigma + act * (1.0 - sigma)), 512).astype(BF)
        silu[i][...] = padded(act, 512).astype(BF)
    out_sides(
        dot(hidden[0][...], store[0, :, 2 * fw :], LAST)
        + dot(hidden[1][...], store[1, :, 2 * fw :], LAST),
        mine,
        theirs,
    )


def feed(pos, n_mine, n_theirs, w, fw, inner):
    rows, width = n_mine.shape
    return call(
        functools.partial(feed_body, fw, inner),
        [shape((2 * rows, 512))] * 6 + [shape((rows, width), F32), shape((rows, width))],
        [SM] + [VM] * 2 + [ANY] * 2,
        [VM] * 8,
        [pltpu.VMEM((2 * rows, width), BF), pltpu.VMEM((2, width, 2 * fw + 512), BF), sems(inner)],
        cost=18,
    )(pos, n_mine, n_theirs, *w)


def feed_back_body(fw, inner, pos, d_mine, d_theirs, *refs):
    slope, silu = refs[:2], refs[2:4]
    blocks = refs[4:6]
    d_gu = refs[6:8]
    mine, theirs = refs[8:10]
    rows_in, store, sem = refs[10:]
    wait = start_all([block_copies(pos, inner, blocks, store, sem, i) for i in range(2)])
    rows = d_mine.shape[0]
    rows_in[:rows, :] = d_mine[...]
    rows_in[rows:, :] = d_theirs[...]
    for i in range(2):
        wait(i)
        out = dot(rows_in[...], store[i, :, 2 * fw :])
        a = (out * slope[i][...].astype(F32))[:, :fw]
        b = (out * silu[i][...].astype(F32))[:, :fw]
        d_gu[i][...] = jnp.concatenate([a, b], axis=1).astype(BF)
    out_sides(
        dot(d_gu[0][...], store[0, :, : 2 * fw], LAST)
        + dot(d_gu[1][...], store[1, :, : 2 * fw], LAST),
        mine,
        theirs,
    )


def feed_back(pos, d_mine, d_theirs, slope, silu, w, fw, inner):
    rows, width = d_mine.shape
    return call(
        functools.partial(feed_back_body, fw, inner),
        [shape((2 * rows, 2 * fw))] * 2 + [shape((rows, width), F32), shape((rows, width))],
        [SM] + [VM] * 6 + [ANY] * 2,
        [VM] * 4,
        [pltpu.VMEM((2 * rows, width), BF), pltpu.VMEM((2, width, 2 * fw + 512), BF), sems(inner)],
        cost=16,
    )(pos, d_mine, d_theirs, *slope, *silu, *w)


def features(pos, k, step):
    return pl.ds(pl.multiple_of((pos[1] ^ k) * step, 128), step)


def feed_grad_body(inner, pair, pos, n_mine, n_theirs, d_mine, d_theirs, *refs):
    d_gu, hidden = refs[:2], refs[2:4]
    out, store, sem = refs[4:]
    rows = n_mine.shape[0]
    step = store.shape[1] // 2
    depth = step // inner
    cut = d_gu[0].shape[1]
    copies = []
    for p in range(2):
        spot = features(pos, 2 * pair + p, step)
        to = pl.ds(p * step, step)
        for i in range(2):
            value = dot(n_mine[:, spot], d_gu[i][:rows, :], ROWS)
            value += dot(n_theirs[:, spot], d_gu[i][rows:, :], ROWS)
            store[i, to, :cut] = value.astype(BF)
            value = dot(d_mine[:, spot], hidden[i][:rows, :], ROWS)
            value += dot(d_theirs[:, spot], hidden[i][rows:, :], ROWS)
            store[i, to, cut:] = value.astype(BF)
            for j in range(inner):
                n = p * inner + j
                copies.append(
                    pltpu.make_async_copy(
                        store.at[i, pl.ds(n * depth, depth)],
                        out.at[j * 2 + (pos[3] ^ i), pl.ds(p * depth, depth)],
                        sem.at[i * 2 * inner + n],
                    )
                )
                copies[-1].start()
    for c in copies:
        c.wait()


def feed_grad(pos, n_all, d_all, d_gu, hidden, inner, pair):
    rows, width = n_all[0].shape
    cols = d_gu[0].shape[1] + hidden[0].shape[1]
    return call(
        functools.partial(feed_grad_body, inner, pair),
        shape((inner * 2, width // (2 * inner), cols)),
        [SM] + [VM] * 8,
        ANY,
        [pltpu.VMEM((2, width // 2, cols), BF), pltpu.SemaphoreType.DMA((4 * inner,))],
        cost=9,
    )(pos, *n_all, *d_all, *d_gu, *hidden)


def attend_back_body(sides, pos, d_mine, d_theirs, q_ref, row_ids, lse, cosine, sine, *refs):
    arrays = sides if sides <= 2 else 1
    kvs, refs = refs[:arrays], refs[arrays:]
    w = refs[:16]
    dq_ref, own_ref, send_ref = refs[16:19]
    store, mix, d_kv, sem = refs[19:]
    wait = fetch(pos, sides, w, store, sem)
    rows = q_ref.shape[0]
    half = rows // 2
    qw = q_ref.shape[1] // 2
    for i in range(2):
        wait(i)
        for side, ref in enumerate((d_mine, d_theirs)):
            mix[i, pl.ds(side * half, half), :] = dot(ref[...], store[i])[:, 320 : 320 + qw].astype(BF)
    ids = row_ids[0:1, :]
    read = reader(kvs, rows)

    def look(s):
        return read(s, ID_LANE).astype(F32) <= ids

    looks = [look(s) for s in range(sides)] if sides <= 2 else None
    d_q = []
    c = FACTOR * LOG2E
    head = 0
    for i in range(2):
        for start in range(0, qw, HEAD_DIM):
            q = q_ref[:, i * qw + start : i * qw + start + HEAD_DIM]
            dm = mix[i, :, start : start + HEAD_DIM]
            level = lse[head : head + 1, :]
            head += 1

            def pair(s):
                seen = looks[s] if looks else look(s)
                p = jnp.where(seen, jnp.exp2(dot(read(s, lanes(i)), q, LAST) * c - level), 0.0)
                return p, dot(read(s, lanes(2 + i)), dm, LAST)

            held = [pair(s) for s in range(sides)] if sides <= 2 else None

            def weigh(s, delta):
                p, dp = held[s] if held else pair(s)
                return delta + jnp.sum(p * dp, axis=0, keepdims=True)

            delta = each(sides, weigh, jnp.zeros((1, rows), F32))

            def grads(s, out):
                p, dp = held[s] if held else pair(s)
                ds = (p * (dp - delta)).astype(BF)
                d_value = dot(p.astype(BF), dm)
                d_key = dot(ds, q)
                if start == 0:
                    d_kv[2 + i, s] = d_value
                    d_kv[i, s] = d_key
                else:
                    d_kv[2 + i, s] += d_value
                    d_kv[i, s] += d_key
                return out + dot(read(s, lanes(i)), ds, ROWS)

            d_q.append(each(sides, grads, jnp.zeros((HEAD_DIM, rows), F32)))
    tall = jnp.concatenate(d_q + [jnp.zeros((512 - 4 * HEAD_DIM, rows), F32)], axis=0).T * FACTOR
    cos, sin = cosine[...], sine[...]
    dq_ref[...] = jnp.concatenate(
        [rotated(tall[:, h * HEAD_DIM : (h + 1) * HEAD_DIM], cos, -sin) for h in range(4)], axis=1
    ).astype(BF)
    for s in range(sides):
        value = jnp.concatenate([d_kv[0, s] * FACTOR, d_kv[1, s] * FACTOR, d_kv[2, s], d_kv[3, s]], axis=1)
        if s == 0:
            own_ref[...] = value
        else:
            send_ref[pl.ds((s - 1) * rows, rows), :] = value.astype(BF)


def attend_back(pos, d_mine, d_theirs, q, kvs, row_ids, lse, cosine, sine, w, sides):
    rows = q.shape[0]
    width = d_mine.shape[1]
    cols = 4 * HEAD_DIM
    return call(
        functools.partial(attend_back_body, sides),
        [shape(q.shape), shape((rows, cols), F32), shape(((sides - 1) * rows, cols))],
        [SM] + [VM] * (7 + len(kvs)) + [ANY] * 16,
        [VM] * 3,
        [
            pltpu.VMEM((2, width, 512), BF),
            pltpu.VMEM((2, rows, q.shape[1] // 2), BF),
            pltpu.VMEM((4, sides, rows, HEAD_DIM), F32),
            sems(sides),
        ],
        cost=18,
    )(pos, d_mine, d_theirs, q, row_ids, lse, cosine, sine, *kvs, *w)


def split_body(dq_ref, own_ref, got_ref, cosine, sine, *d_qkv):
    qw = dq_ref.shape[1] // 2
    cos, sin = cosine[...], sine[...]
    d_kv = own_ref[...] + got_ref[...].astype(F32)
    d_q = dq_ref[...].astype(F32)
    for i in range(2):
        d_k = rotated(d_kv[:, i * HEAD_DIM : (i + 1) * HEAD_DIM], cos, -sin)
        d_v = d_kv[:, (2 + i) * HEAD_DIM : (3 + i) * HEAD_DIM]
        d_qkv[i][...] = padded(
            jnp.concatenate([d_q[:, i * qw : (i + 1) * qw], d_k, d_v], axis=1), 512
        ).astype(BF)


def split_grads(dq, own, got, cosine, sine):
    rows = dq.shape[0]
    return call(split_body, [shape((rows, 512))] * 2, [VM] * 5, [VM] * 2)(dq, own, got, cosine, sine)


def project_back_body(inner, pos, x_mine, x_theirs, d_a, d_b, *refs):
    w = refs[:16]
    mine, theirs, gain_ref = refs[16:19]
    store, sem = refs[19:]
    wait = fetch(pos, inner, w, store, sem)
    for i in range(2):
        wait(i)
    half, width = mine.shape
    total = 0.0
    for side, ref, x_ref in ((1, theirs, x_theirs), (0, mine, x_mine)):
        spot = pl.ds(side * half, half)
        part = dot(d_a[spot, :], store[0], LAST) + dot(d_b[spot, :], store[1], LAST)
        ref[...] = part.astype(ref.dtype)
        x = x_ref[:, :width].astype(F32)
        total = total + jnp.sum(part * (x * mean_scale(x)), axis=0, keepdims=True)
    gain_ref[...] = jnp.broadcast_to(total, gain_ref.shape)


def project_back(pos, x_mine, x_theirs, d_qkv, w, inner):
    rows, width = x_mine.shape
    width -= 128
    return call(
        functools.partial(project_back_body, inner),
        [shape((rows, width), F32), shape((rows, width)), shape((8, width), F32)],
        [SM] + [VM] * 4 + [ANY] * 16,
        [VM] * 3,
        [pltpu.VMEM((2, width, 512), BF), sems(inner)],
        cost=10,
    )(pos, x_mine, x_theirs, *d_qkv, *w)


def attn_grad_body(inner, pos, first, d_mine, d_theirs, *refs):
    d_qkv, mixed = refs[:2], refs[2:4]
    outs = refs[4:20]
    store, sem = refs[20:]
    half = d_mine.shape[0]
    step = store.shape[1] // PARTS
    copies = [piece_copies(pos, inner, outs[8 * i : 8 * i + 8], store, sem, i, True) for i in range(2)]
    for k in (3, 2, 1, 0):
        spot = features(pos, k, step)
        for i in range(2):
            value = dot(first[:, spot], d_qkv[i][...], ROWS)
            value += dot(d_mine[:, spot], mixed[i][:half, :], ROWS)
            value += dot(d_theirs[:, spot], mixed[i][half:, :], ROWS)
            store[i, spot, :] = value.astype(BF)
            for c in copies[i][k * inner : (k + 1) * inner]:
                c.start()
    for i in range(2):
        for c in copies[i]:
            c.wait()


def attn_grad(pos, first, d_mine, d_theirs, d_qkv, mixed, inner):
    rows, width = first.shape
    return call(
        functools.partial(attn_grad_body, inner),
        [shape((width // 8, 512))] * 16,
        [SM] + [VM] * 7,
        [ANY] * 16,
        [pltpu.VMEM((2, width, 512), BF), sems(inner)],
        cost=10,
    )(pos, first, d_mine, d_theirs, *d_qkv, *mixed)


def tail_body(gain_one, gain_two, sum_attn, sums, out):
    width = gain_two.shape[1]
    out[:, :width] = jnp.concatenate(
        [gain_one[0:1, :], gain_two[...], jnp.zeros((6, width), F32)], axis=0
    )
    lane = lax.broadcasted_iota(jnp.int32, (8, 128), 1)
    tail = jnp.where(lane == 0, sums[0:8, :], 0.0)
    tail = jnp.where(lane == 1, sum_attn[...], tail)
    out[:, width:] = jnp.where(lane == 2, sums[8:16, :], tail)


def tail_rows(gain_one, gain_two, sum_attn, sums):
    width = gain_two.shape[1]
    return call(tail_body, shape((8, width + 128), F32), [VM] * 4, VM)(gain_one, gain_two, sum_attn, sums)


class Live:
    def fence(self):
        names = sorted(self.__dict__)
        leaves, tree = jax.tree.flatten([self.__dict__[n] for n in names])
        leaves = lax.optimization_barrier(tuple(leaves))
        self.__dict__.update(zip(names, jax.tree.unflatten(tree, leaves)))


class Place:
    def __init__(self):
        self.inner = lax.axis_size("y")
        self.count = PARTS * self.inner
        self.z, self.y, self.x, self.c = [lax.axis_index(name) for name in AXES]
        self.s = self.z * self.inner + self.y
        self.zs = self.z.reshape(1).astype(jnp.int32)
        self.bits = []
        b = 1
        while b < self.inner:
            self.bits.append(b)
            b *= 2

    def hop_z(self, v, k):
        return hop(v, "z", k)

    def hop_y(self, v, b):
        return hop(v, "y", b)

    def hop_x(self, v):
        return hop(v, "x", 1)

    def hop_c(self, v):
        return hop(v, "c", 1)

    def low_y(self, v):
        for b in self.bits[:-1]:
            v = jnp.concatenate([v, self.hop_y(v, b)], 0)
        return v

    def far_y(self, v):
        return self.hop_y(v, self.bits[-1])

    def add(self, own, got):
        return (own.astype(F32) + got.astype(F32)).astype(BF)

    def sum_y(self, own, far):
        value = self.add(own, self.far_y(far))
        for b in reversed(self.bits[:-1]):
            n = value.shape[0] // 2
            value = self.add(value[:n], self.hop_y(value[n:], b))
        return value

    def sum_x(self, own, other):
        return self.add(own, self.hop_x(other))

    def gather(self, own):
        one = self.hop_z(own, 1)
        two = self.hop_z(own, 2)
        three = self.hop_z(two, 1)
        mine = stack([own, one, two, three])
        return [mine, self.hop_c(mine)]

    def scatter(self, mine, theirs):
        one, three, keep = first_sum(mine, self.hop_c(theirs))
        two = second_sum(keep, self.hop_z(three, 1))
        return keep, self.hop_z(one, 1), self.hop_z(two, 2)


def tables(place):
    half = HEAD_DIM // 2
    freq = THETA ** (-(jnp.arange(half, dtype=F32) * 2.0 / HEAD_DIM))
    angle = place[:, None] * freq[None, :]
    return (jnp.cos(angle), jnp.sin(angle))


def on_device(
    inputs,
    targets,
    seq_ids,
    block_ids,
    attn_gain,
    mlp_gain,
    w_query,
    w_key,
    w_value,
    w_out,
    w_gate,
    w_up,
    w_down,
):
    at = Place()
    inner = at.inner
    full = inputs.shape[1]
    half_span = SPAN // 2
    kw = w_key.shape[1] // 2
    qw = w_query.shape[1] // PARTS
    fw = w_gate.shape[1] // PARTS
    row_f32 = shape((half_span, full), F32)
    row_bf = shape((half_span, full))

    off = jnp.where(seq_ids[0] == at.x, 0, SPAN)
    pos = jnp.stack([off + at.c * half_span, at.z, at.y, at.x, at.c]).astype(jnp.int32)
    spots = [
        (off if xr == 0 else SPAN - off) + (at.c ^ cr) * half_span for xr in range(2) for cr in range(2)
    ]
    spots = jnp.stack(spots).astype(jnp.int32)

    def all_rows(own):
        across = at.hop_x(own)
        return spread_rows(spots, [own, at.hop_c(own), across, at.hop_c(across)])

    rows = 2 * PARTS * half_span
    count = jnp.arange(rows, dtype=jnp.int32)
    zz = at.z ^ ((count // half_span) % PARTS)
    cc = at.c ^ (count // (half_span * PARTS))
    place = ((zz * inner + at.y) * SPAN + cc * half_span + count % half_span).astype(F32)
    cosine, sine = tables(place)

    def listed(w):
        return [v for i in range(2) for k in range(PARTS) for v in w[k][i]]

    def pieces(grads):
        return [(grads[2 * k : 2 * k + 2], grads[8 + 2 * k : 10 + 2 * k]) for k in range(PARTS)]

    def first_x(g):
        return [at.sum_x(a, b) for a, b in zip(*g)]

    def first_y(g):
        return [at.sum_y(*side) for side in g]

    def gather_blocks(pair):
        return lax.all_gather(pair, ("y", "x"), axis=0)

    def scatter_blocks(blocks):
        blocks = blocks.reshape(-1, blocks.shape[-1])
        got = lax.psum_scatter(blocks, ("y", "x"), scatter_dimension=0, tiled=True)
        n = got.shape[0] // 2
        return [got[:n], got[n:]]

    hop_x, hop_z, low_y, far_y = at.hop_x, at.hop_z, at.low_y, at.far_y
    live = Live()
    live.w = [w_gate, w_up, w_down]
    live.rows = [inputs, targets]
    live.qo = pack_attn(at.zs, w_query, w_key, w_value, w_out, attn_gain, mlp_gain, 512)
    live.fence()

    q = live.qo
    z = [q[0]] + [hop_z(q[k], k) for k in range(1, PARTS)]
    live.x_own, live.t_own = own_rows(pos, block_ids.reshape(1, -1), *live.rows)
    live.g = list(pack(at.zs, live.w, [(fw, 1)] * 3, 2 * fw + 512, 2 * fw))
    del live.w, live.rows
    live.g[1] = hop_z(live.g[1], 1)
    v = low_y(z[0])
    w = far_y(v)
    q0 = ((v, w), (hop_x(v), hop_x(w)))
    u, v = low_y(hop_x(z[1])), low_y(z[1])
    q1 = ((v, far_y(v)), (u, far_y(u)))
    live.qo, live.z = [q0, q1], z[2:]
    live.fence()

    near = gather_blocks(jnp.concatenate(live.g[:2], 0))
    v = low_y(live.z[0])
    w = far_y(v)
    q2 = ((v, w), (hop_x(v), hop_x(w)))
    u, v = low_y(hop_x(live.z[1])), low_y(live.z[1])
    q3 = ((v, far_y(v)), (u, far_y(u)))
    one, two = hop_z(live.x_own, 1), hop_z(live.x_own, 2)
    live.x_all = [stack([live.x_own, one, two, hop_z(two, 1)])]
    live.w_qo = listed(live.qo + [q2, q3])
    live.g[2] = hop_z(live.g[2], 2)
    del live.z, live.qo
    live.fence()

    live.x_all = [live.x_all[0], at.hop_c(live.x_all[0])]
    live.first, live.query, kv, live.gain, live.row_ids = project(
        pos, *live.x_all, cosine, sine, live.w_qo, qw, inner
    )
    live.kvs = [kv]
    live.g[4], live.g[5] = hop_z(live.g[4], 2), hop_z(live.g[5], 3)
    live.fence()

    kvs = live.kvs
    for b in at.bits:
        kvs = kvs + [at.hop_y(v, b) for v in kvs]
    if inner > 2:
        kvs = [jnp.concatenate(kvs, 0)]
    live.kvs = kvs
    mixed_a, mixed_b, live.lse, live.mine, live.theirs = attend(
        pos, live.query, kvs, live.row_ids, live.w_qo, inner
    )
    live.mixed = (mixed_a, mixed_b)
    live.g[3] = hop_z(live.g[3], 3)
    live.fence()

    two = [jnp.concatenate([live.g[k], live.g[k + 2]], 1) for k in (2, 3)]
    far = gather_blocks(jnp.concatenate(two, 0))
    del live.g
    live.middle, n_own, live.sum_attn = call(
        after_attn_body,
        [row_f32, row_bf, shape((8, 128), F32)],
        [VM] * 5,
        [VM] * 3,
    )(*at.scatter(live.mine, live.theirs), live.x_own, live.gain)
    live.n_all = at.gather(n_own)
    del live.mine, live.theirs
    live.fence()

    live.w_ff = [near, far]
    out = feed(pos, *live.n_all, live.w_ff, fw, inner)
    live.hidden, live.slope, live.silu, (mine, theirs) = out[:2], out[2:4], out[4:6], out[6:]
    live.d_own, live.layer_own, live.sums = call(
        after_mlp_body,
        [row_bf, row_bf, shape((16, 128), F32)],
        [VM] * 5,
        [VM] * 3,
    )(*at.scatter(mine, theirs), live.middle, live.t_own)
    del live.t_own
    live.d_all = at.gather(live.d_own)
    live.fence()


    out = feed_back(pos, *live.d_all, live.slope, live.silu, live.w_ff, fw, inner)
    live.d_gu, live.mine, live.theirs = out[:2], out[2], out[3]
    del live.slope, live.silu, live.w_ff
    live.fence()

    one, three, keep = first_sum(live.mine, at.hop_c(live.theirs))
    live.left = [keep, one, second_sum(keep, hop_z(three, 1))]
    del live.mine, live.theirs
    live.far = feed_grad(pos, live.n_all, live.d_all, live.d_gu, live.hidden, inner, 1)
    live.fence()

    far = scatter_blocks(live.far)
    keep, one, two = live.left
    live.d_middle, live.a_own, live.grad_gain_two = call(
        after_feed_back_body,
        [row_f32, row_bf, shape((1, full), F32)],
        [VM] * 6,
        [VM] * 3,
    )(keep, hop_z(one, 1), hop_z(two, 2), live.middle, live.d_own, live.gain)
    del live.middle, live.d_own, live.left, live.far
    live.near = feed_grad(pos, live.n_all, live.d_all, live.d_gu, live.hidden, inner, 0)
    del live.n_all, live.d_all, live.d_gu, live.hidden
    live.fence()

    near = scatter_blocks(live.near)
    del live.near
    live.a_all = at.gather(live.a_own)
    del live.a_own
    live.fence()

    live.d_query, live.d_kv, live.sent = attend_back(
        pos, *live.a_all, live.query, live.kvs, live.row_ids, live.lse, cosine, sine, live.w_qo, inner
    )
    del live.query, live.kvs, live.row_ids, live.lse
    live.fence()

    d_kv, sent = live.d_kv, live.sent
    if inner > 2:
        sent = jnp.concatenate([d_kv, sent.astype(F32)], 0)
        for b in reversed(at.bits[1:]):
            n = sent.shape[0] // 2
            sent = sent[:n] + at.hop_y(sent[n:].astype(BF), b).astype(F32)
        d_kv, sent = sent[:rows], sent[rows:].astype(BF)
    sent = at.hop_y(sent, at.bits[0])
    live.d_qkv = split_grads(live.d_query, d_kv, sent, cosine, sine)
    live.mine, live.theirs, live.gain_one = project_back(pos, *live.x_all, live.d_qkv, live.w_qo, inner)
    del live.d_kv, live.sent, live.d_query, live.w_qo, live.x_all
    live.far3 = [far[1][:, : 2 * fw], hop_z(far[1][:, 2 * fw :], 3)]
    live.fence()

    one, three, keep = first_sum(live.mine, at.hop_c(live.theirs))
    live.left = [keep, one, second_sum(keep, hop_z(three, 1))]
    live.grad_qo = pieces(attn_grad(pos, live.first, *live.a_all, live.d_qkv, live.mixed, inner))
    del live.first, live.a_all, live.mixed, live.mine, live.theirs, live.d_qkv
    live.far3[0] = hop_z(live.far3[0], 3)
    live.fence()

    q = live.grad_qo
    live.tails = tail_rows(live.gain_one, live.grad_gain_two, live.sum_attn, live.sums)
    del live.gain_one, live.grad_gain_two, live.sum_attn, live.sums
    keep, one, two = live.left
    (live.input_own,) = call(
        after_all_body,
        [row_bf],
        [VM] * 6,
        [VM],
    )(keep, hop_z(one, 1), hop_z(two, 2), live.x_own, live.d_middle, live.gain)
    del live.left, live.x_own, live.d_middle
    q[3], q[2] = first_y(q[3]), first_x(q[2])
    live.fence()

    q = live.grad_qo
    live.far2 = [hop_z(far[0][:, : 2 * fw], 2), far[0][:, 2 * fw :]]
    q[3], q[2] = at.sum_x(*q[3]), at.sum_y(*q[2])
    q[1], q[0] = first_y(q[1]), first_x(q[0])
    live.input_grad = all_rows(live.input_own)
    del live.input_own
    tails = live.tails + at.hop_c(live.tails)
    live.tails = tails + at.hop_x(tails)
    live.fence()

    q = live.grad_qo
    q[3] = hop_z(q[3], 3)
    live.far2[1] = hop_z(live.far2[1], 2)
    q[1], q[0] = at.sum_x(*q[1]), at.sum_y(*q[0])
    live.near = [near[0], hop_z(near[1], 1)]
    tails = live.tails
    for b in at.bits:
        tails = tails + at.hop_y(tails, b)
    live.tails = tails + at.hop_z(tails, 1)
    live.fence()

    q = live.grad_qo
    q[2], q[1] = hop_z(q[2], 2), hop_z(q[1], 1)
    tails = live.tails + at.hop_z(live.tails, 2)
    layer_out, input_grad = all_rows(live.layer_own), live.input_grad
    live.g = live.near + [live.far2[0], live.far3[0], live.far2[1], live.far3[1]]
    g_gate, g_up, g_down = unpack(at.zs, live.g, [(i * fw, fw, 1) for i in range(3)], 2 * fw)
    takes = [(0, qw, 1), (qw, kw, 2), (qw + kw, kw, 2), (qw + 2 * kw, qw, 1)]
    g_query, g_key, g_value, g_out = unpack(at.zs, q, takes)
    depth = w_query.shape[0]
    own_gains = lax.dynamic_slice_in_dim(tails[:2, :full], at.s * depth, depth, 1)
    entries = inputs.shape[0] * at.count * inputs.shape[1]
    rms = jnp.sqrt(tails[0, full : full + 3] / entries + EPS)
    return (
        layer_out,
        input_grad,
        g_query,
        g_key,
        g_value,
        g_out,
        g_gate,
        g_up,
        g_down,
        own_gains[0],
        own_gains[1],
        rms[0],
        rms[1],
        rms[2],
    )


def solution(mesh):
    devices = mesh.devices.reshape(PARTS, -1, 2, mesh.devices.shape[1] // 2)
    seq, mp = ("z", "y"), ("x", "c")
    rows, single, block = P(seq, None), P(seq), P(seq, mp)
    return jax.shard_map(
        on_device,
        mesh=Mesh(devices, AXES),
        in_specs=(rows, rows, single, single, single, single) + (block,) * 7,
        out_specs=(rows, rows) + (block,) * 7 + (single, single, P(), P(), P()),
        check_vma=False,
    )
```

```python
import functools

import jax
import jax.numpy as jnp
from jax import lax
from jax.experimental import pallas as pl
from jax.experimental.pallas import tpu as pltpu
from jax.sharding import Mesh
from jax.sharding import PartitionSpec as P

HEAD_DIM = 80
SPAN = 128
EPS = 1e-05
THETA = 1000000.0
PARTS = 4
BF = jnp.bfloat16
F32 = jnp.float32
FACTOR = HEAD_DIM**-0.5
LOG2E = 1.4426950408889634
LIMIT = 56 * 1024 * 1024

PLAIN = (((1,), (0,)), ((), ()))
LAST = (((1,), (1,)), ((), ()))
ROWS = (((0,), (0,)), ((), ()))

VM = pl.BlockSpec(memory_space=pltpu.VMEM)
SM = pl.BlockSpec(memory_space=pltpu.SMEM)
ANY = pl.BlockSpec(memory_space=pl.ANY)


def shape(dims, kind=BF):
    return jax.ShapeDtypeStruct(tuple(dims), kind)


def call(body, outs, in_specs, out_specs, scratch=(), cost=2):
    return pl.pallas_call(
        body,
        out_shape=outs,
        in_specs=in_specs,
        out_specs=out_specs,
        scratch_shapes=list(scratch),
        compiler_params=pltpu.CompilerParams(vmem_limit_bytes=LIMIT),
        cost_estimate=pl.CostEstimate(flops=cost * 10**9, bytes_accessed=0, transcendentals=0),
    )


AXES = ("z", "y", "x", "c")


def hop(value, axis, k):
    size = lax.axis_size(axis)
    return lax.ppermute(value, axis, [(i, i ^ k) for i in range(size)])


def dot(left, right, dims=PLAIN):
    return lax.dot_general(left, right, dims, preferred_element_type=F32)


def joined(values, width):
    values = [v.astype(F32) for v in values]
    have = sum(v.shape[1] for v in values)
    if have < width:
        values.append(jnp.zeros((values[0].shape[0], width - have), F32))
    return jnp.concatenate(values, axis=1).astype(BF)


def pack_body(takes, width, cut, z_ref, *refs):
    count = len(takes)
    ins, outs = refs[:count], refs[count:]
    for k in range(PARTS):
        part = z_ref[0] ^ k
        for j in range(PARTS):

            @pl.when(part == j)
            def _():
                values = [ref[:, pl.ds(step * (j // share), step)] for ref, (step, share) in zip(ins, takes)]
                value = joined(values, width)
                if cut and k >= 2:
                    outs[k][...] = value[:, :cut]
                    outs[k + 2][...] = value[:, cut:]
                else:
                    outs[k][...] = value


def pack(z, arrays, takes, width, cut=None):
    depth = arrays[0].shape[0]
    outs = [shape((depth, width))] * PARTS
    if cut:
        outs = outs[:2] + [shape((depth, cut))] * 2 + [shape((depth, width - cut))] * 2
    return call(
        functools.partial(pack_body, takes, width, cut),
        outs,
        [SM] + [VM] * len(arrays),
        [VM] * len(outs),
    )(z, *arrays)


def pack_attn_body(z_ref, wq, wk, wv, wo, gain_one, gain_two, *outs):
    depth, width = outs[0].shape
    kw = wk.shape[0] // 2
    qw = wq.shape[1] // PARTS
    narrow = jnp.concatenate([wk[...].astype(F32), wv[...].astype(F32)], axis=0)
    gains = jnp.concatenate([gain_one[...], gain_two[...]], axis=0).astype(F32)
    fill = jnp.zeros((128 - (4 * kw + 2) % 128, depth), F32)
    tall = jnp.concatenate([narrow, gains, fill], axis=0).T
    for k in range(PARTS):
        part = z_ref[0] ^ k
        for j in range(PARTS):

            @pl.when(part == j)
            def _():
                spot = pl.ds(qw * j, qw)
                h = j // 2
                values = [
                    wq[:, spot],
                    tall[:, kw * h : kw * h + kw],
                    tall[:, kw * (h + 2) : kw * (h + 3)],
                    wo[:, spot],
                    tall[:, 4 * kw : 4 * kw + 2],
                ]
                outs[k][...] = joined(values, width)


def pack_attn(z, wq, wk, wv, wo, gain_one, gain_two, width):
    depth = wq.shape[0]
    return call(
        pack_attn_body, [shape((depth, width))] * PARTS, [SM] + [VM] * 6, [VM] * PARTS
    )(z, wq, wk.T, wv.T, wo, gain_one.reshape(1, -1), gain_two.reshape(1, -1))


def unpack_body(takes, z_ref, *refs):
    ins, outs = refs[:PARTS], refs[PARTS:]
    for ref, (start, step, share) in zip(outs, takes):
        if share == 2:
            ref[...] = jnp.zeros_like(ref)
    depth = ins[0].shape[0]
    for k in range(PARTS):
        part = z_ref[0] ^ k
        flat = None
        if any(share == 2 for start, step, share in takes):
            first = min(start for start, step, share in takes if share == 2)
            last = max(start + step for start, step, share in takes if share == 2)
            fill = jnp.zeros((depth, -(last - first) % 128), F32)
            flat = jnp.concatenate([ins[k][:, pl.ds(first, last - first)].astype(F32), fill], axis=1).T
        for j in range(PARTS):

            @pl.when(part == j)
            def _():
                for ref, (start, step, share) in zip(outs, takes):
                    spot = pl.ds(step * (j // share), step)
                    if share == 1:
                        ref[:, spot] = ins[k][:, pl.ds(start, step)].astype(F32)
                    else:
                        ref[spot, :] += flat[start - first : start - first + step]


def unpack(z, pieces, takes):
    depth = pieces[0].shape[0]
    dims = [(depth, step * PARTS // share) for start, step, share in takes]
    dims = [d[::-1] if take[2] == 2 else d for d, take in zip(dims, takes)]
    return call(
        functools.partial(unpack_body, takes),
        [shape(d, F32) for d in dims],
        [SM] + [VM] * PARTS,
        [VM] * len(takes),
        cost=4,
    )(z, *pieces)


def spot_of(pos, k, j, inner, depth):
    return pl.ds(pl.multiple_of(((pos[1] ^ k) * inner + (pos[2] ^ j)) * depth, 16), depth)


def piece_copies(pos, inner, pieces, store, sem, i, back=False):
    half = inner // 2
    depth = store.shape[1] // (PARTS * inner)
    copies = []
    for k in range(PARTS):
        for j in range(inner):
            ends = (
                pieces[2 * k + j // half].at[pl.ds((j % half) * depth, depth)],
                store.at[i, spot_of(pos, k, j, inner, depth)],
            )
            n = (i * PARTS + k) * inner + j
            copies.append(pltpu.make_async_copy(*(ends[::-1] if back else ends), sem.at[n]))
    return copies


def fetch(pos, inner, pieces, store, sem):
    copies = [piece_copies(pos, inner, pieces[8 * i : 8 * i + 8], store, sem, i) for i in range(2)]
    return start_all(copies)


def start_all(copies):
    for half in copies:
        for c in half:
            c.start()

    def wait(i):
        for c in copies[i]:
            c.wait()

    return wait


def own_rows_body(pos, ids, x_ref, t_ref, x_out, t_out, tall):
    spot = pl.ds(pl.multiple_of(pos[0], 64), 64)
    width = x_ref.shape[1]
    tall[...] = jnp.broadcast_to(ids[...].astype(F32), tall.shape[::-1]).T
    x_out[:, :width] = x_ref[spot, :]
    x_out[:, width:] = tall[spot, :].astype(BF)
    t_out[...] = t_ref[spot, :]


def own_rows(pos, ids, x, t):
    rows, width = x.shape
    return call(
        own_rows_body,
        [shape((64, width + 128)), shape((64, width))],
        [SM] + [VM] * 3,
        [VM] * 2,
        [pltpu.VMEM((rows, 128), F32)],
    )(pos, ids, x, t)


def join_rows(pieces, out):
    n = pieces[0].shape[0]
    for i, ref in enumerate(pieces):
        out[pl.ds(i * n, n), :] = ref[:, : out.shape[1]]


def first_sum_body(mine, got, three):
    three[...] = (mine[...].astype(F32) + got[...].astype(F32)).astype(BF)


def first_sum(mine, got):
    return call(first_sum_body, shape(mine.shape), [VM] * 2, VM)(mine, got)


def second_sum_body(mine_one, got_one, mine_two, got_two, three, one, two):
    one[...] = (mine_one[...].astype(F32) + got_one[...].astype(F32)).astype(BF)
    two[...] = (mine_two[...].astype(F32) + got_two[...].astype(F32) + three[...].astype(F32)).astype(BF)


def second_sum(mine, got, three):
    return call(second_sum_body, [shape(three.shape)] * 2, [VM] * 5, [VM] * 2)(
        mine[1], got[1], mine[2], got[2], three
    )


def last_sum(parts):
    return functools.reduce(jnp.add, [ref[...].astype(F32) for ref in parts])


def mean_scale(value):
    return lax.rsqrt(jnp.mean(value * value, axis=-1, keepdims=True) + EPS)


def back_norm(grad, value, gain):
    scale = mean_scale(value)
    unit = value * scale
    scaled = grad * gain
    return unit, scale * (scaled - unit * jnp.mean(scaled * unit, axis=-1, keepdims=True))


def after_attn_body(mine, got, one, two, x_own, gain, middle, n_own, total):
    branch = last_sum((mine, got, one, two))
    value = x_own[:, : branch.shape[1]].astype(F32) + branch
    middle[...] = value
    n_own[...] = (value * mean_scale(value) * gain[1:2, :]).astype(BF)
    total[...] = jnp.full(total.shape, jnp.sum(branch * branch), F32)


def after_mlp_body(mine, got, one, two, middle, target, d_own, out, total):
    branch = last_sum((mine, got, one, two))
    stream = middle[...] + branch
    d_own[...] = (stream - target[...].astype(F32)).astype(BF)
    out[...] = stream.astype(BF)
    total[0:8, :] = jnp.full((8, 128), jnp.sum(stream * stream), F32)
    total[8:16, :] = jnp.full((8, 128), jnp.sum(branch * branch), F32)


def after_feed_back_body(mine, got, one, two, middle, d_own, gain, d_middle, a_own, gain_grad):
    grad = last_sum((mine, got, one, two))
    unit, back = back_norm(grad, middle[...], gain[1:2, :])
    value = d_own[...].astype(F32) + back
    d_middle[...] = value
    a_own[...] = value.astype(BF)
    gain_grad[...] = jnp.sum(grad * unit, axis=0, keepdims=True)


def after_all_body(mine, got, one, two, x_own, d_middle, gain, out):
    grad = last_sum((mine, got, one, two))
    unit, back = back_norm(grad, x_own[:, : grad.shape[1]].astype(F32), gain[0:1, :])
    out[...] = (d_middle[...] + back).astype(BF)


def spread_rows_body(spots, p0, p1, p2, p3, out):
    n = p0.shape[0]
    for i, ref in enumerate((p0, p1, p2, p3)):
        out[pl.ds(pl.multiple_of(spots[i], 64), n), :] = ref[...]


def spread_rows(spots, pieces):
    n, width = pieces[0].shape
    return call(spread_rows_body, shape((4 * n, width)), [SM] + [VM] * 4, VM)(spots, *pieces)


def rotated(value, cosine, sine):
    half = HEAD_DIM // 2
    a, b = value[:, :half], value[:, half:]
    return jnp.concatenate([a * cosine - b * sine, b * cosine + a * sine], axis=1)


def project_body(qw, inner, pos, cosine, sine, *refs):
    x, w = refs[:8], refs[8:24]
    first, q_ref, kv_ref, gains, row_ids = refs[24:29]
    store, sem = refs[29:]
    wait = fetch(pos, inner, w, store, sem)
    width = first.shape[1]
    step = width // 4
    ids = jnp.concatenate([ref[:, width:] for ref in x], axis=0).astype(F32)
    row_ids[...] = ids.T[0:8, :]
    wait(0)
    spot = 480 - 384
    for p in range(4):
        tail = store[0, pl.ds(p * step, step), 384:512].astype(F32).T
        gains[:, pl.ds(p * step, step)] = tail[spot : spot + 8]
    gain = gains[0:1, :]
    rows = x[0].shape[0]
    for i, ref in enumerate(x):
        value = ref[:, :width].astype(F32)
        first[pl.ds(i * rows, rows), :] = (value * mean_scale(value) * gain).astype(BF)
    cos, sin = cosine[...], sine[...]
    queries, keys, values = [], [], []
    for i in range(2):
        if i:
            wait(1)
        out = dot(first[...], store[i])
        for start in range(0, qw, HEAD_DIM):
            queries.append(rotated(out[:, start : start + HEAD_DIM], cos, sin))
        keys.append(rotated(out[:, qw : qw + HEAD_DIM], cos, sin))
        values.append(out[:, qw + HEAD_DIM : qw + 2 * HEAD_DIM])
    q_ref[...] = jnp.concatenate(queries, axis=1).astype(BF)
    kv_ref[...] = jnp.concatenate(keys + values + [ids[:, :64]], axis=1).astype(BF)


def sems(inner):
    return pltpu.SemaphoreType.DMA((2 * (PARTS + 1) * inner,))


def project(pos, x, cosine, sine, w, qw, inner):
    rows, width = x[0].shape
    rows *= 8
    width -= 128
    return call(
        functools.partial(project_body, qw, inner),
        [
            shape((rows, width)),
            shape((rows, 2 * qw)),
            shape((rows, 384)),
            shape((8, width), F32),
            shape((8, rows), F32),
        ],
        [SM] + [VM] * 10 + [ANY] * 16,
        [VM] * 5,
        [pltpu.VMEM((2, width, 512), BF), sems(inner)],
        cost=12,
    )(pos, cosine, sine, *x, *w)


def out_rows(partial, outs):
    n = outs[0].shape[0]
    for i, ref in enumerate(outs):
        ref[...] = partial[i * n : (i + 1) * n].astype(ref.dtype)


def each(count, step, start):
    if count <= 2:
        for s in range(count):
            start = step(s, start)
        return start
    return lax.fori_loop(0, count, step, start)


def reader(kvs, rows):
    def read(s, lane):
        if len(kvs) > 1:
            return kvs[s][:, lane]
        return kvs[0][pl.ds(pl.multiple_of(s * rows, rows), rows), lane]

    return read


def lanes(i):
    return pl.ds(i * HEAD_DIM, HEAD_DIM)


ID_LANE = pl.ds(4 * HEAD_DIM, 1)


def attend_body(sides, pos, q_ref, row_ids, *refs):
    arrays = sides if sides <= 2 else 1
    kvs, refs = refs[:arrays], refs[arrays:]
    w = refs[:16]
    mixed = refs[16:18]
    lse, sides_out = refs[18], refs[19:27]
    store, sem = refs[27:]
    wait = fetch(pos, sides, w, store, sem)
    rows = q_ref.shape[0]
    qw = q_ref.shape[1] // 2
    ids = row_ids[0:1, :]
    read = reader(kvs, rows)

    def look(s):
        return read(s, ID_LANE).astype(F32) <= ids

    looks = [look(s) for s in range(sides)] if sides <= 2 else None
    lse[...] = jnp.zeros_like(lse)
    head = 0
    c = FACTOR * LOG2E
    for i in range(2):
        outs = []
        for start in range(i * qw, (i + 1) * qw, HEAD_DIM):
            q = q_ref[:, start : start + HEAD_DIM]

            def score(s):
                seen = looks[s] if looks else look(s)
                return jnp.where(seen, dot(read(s, lanes(i)), q, LAST), -1e30)

            scores = [score(s) for s in range(sides)] if sides <= 2 else None

            def highest(s, top):
                value = scores[s] if scores else score(s)
                return jnp.maximum(top, jnp.max(value, axis=0, keepdims=True))

            top = each(sides, highest, jnp.full((1, rows), -1e30, F32))

            def gathered(s, carry):
                total, out = carry
                value = scores[s] if scores else score(s)
                p = jnp.exp2(value * c - top * c)
                total = total + jnp.sum(p, axis=0, keepdims=True)
                return total, out + dot(read(s, lanes(2 + i)), p.astype(BF), ROWS)

            nothing = (jnp.zeros((1, rows), F32), jnp.zeros((HEAD_DIM, rows), F32))
            total, out = each(sides, gathered, nothing)
            outs.append(out / total)
            lse[head : head + 1, :] = top * c + jnp.log2(total)
            head += 1
        fill = jnp.zeros((512 - 320 - qw, rows), F32)
        tall = jnp.concatenate([jnp.zeros((320, rows), F32)] + outs + [fill], axis=0)
        mixed[i][...] = tall.T.astype(BF)
    for i in range(2):
        wait(i)
    partial = dot(mixed[0][...], store[0], LAST) + dot(mixed[1][...], store[1], LAST)
    out_rows(partial, sides_out)


def attend(pos, q, kvs, row_ids, w, sides):
    rows = q.shape[0]
    width = 8 * w[0].shape[0]
    return call(
        functools.partial(attend_body, sides),
        [shape((rows, 512))] * 2
        + [shape((8, rows), F32)]
        + [shape((rows // 8, width))] * 8,
        [SM] + [VM] * (2 + len(kvs)) + [ANY] * 16,
        [VM] * 11,
        [pltpu.VMEM((2, width, 512), BF), sems(sides)],
        cost=12,
    )(pos, q, row_ids, *kvs, *w)


def padded(value, width):
    return jnp.concatenate([value, jnp.zeros((value.shape[0], width - value.shape[1]), value.dtype)], axis=1)


def block_copies(pos, inner, arrays, store, sem, i):
    depth = arrays[1].shape[1]
    half = inner // 2
    cut = arrays[2].shape[1]
    copies = []
    for k in range(PARTS):
        for j in range(inner):
            n = (i * PARTS + k) * inner + j
            if k < 3:
                spot = arrays[k // 2].at[j * 2 + (pos[3] ^ i), pl.ds(depth if k == 1 else 0, depth)]
                to = store.at[i, pl.ds(pl.multiple_of(((pos[1] ^ k) * inner + j) * depth, 16), depth)]
                copies.append(pltpu.make_async_copy(spot, to, sem.at[n]))
                continue
            for late in range(2):
                piece = arrays[2 + 4 * late + 2 * i + j // half]
                lane = pl.ds(cut * late, piece.shape[1])
                to = store.at[i, spot_of(pos, k, j, inner, depth), lane]
                spot = piece.at[pl.ds((j % half) * depth, depth)]
                copies.append(
                    pltpu.make_async_copy(spot, to, sem.at[2 * PARTS * inner + i * inner + j] if late else sem.at[n])
                )
    return copies


def feed_body(fw, inner, pos, *refs):
    n, blocks = refs[:8], refs[8:18]
    hidden, slope, silu = refs[18:20], refs[20:22], refs[22:24]
    rows_in, outs = refs[24], refs[25:33]
    store, sem = refs[33:]
    wait = start_all([block_copies(pos, inner, blocks, store, sem, i) for i in range(2)])
    join_rows(n, rows_in)
    for i in range(2):
        wait(i)
        out = dot(rows_in[...], store[i, :, : 2 * fw])
        gate, upper = out[:, :fw], out[:, fw:]
        sigma = jax.nn.sigmoid(gate)
        act = gate * sigma
        hidden[i][...] = padded(act * upper, 512).astype(BF)
        slope[i][...] = padded(upper * (sigma + act * (1.0 - sigma)), 512).astype(BF)
        silu[i][...] = padded(act, 512).astype(BF)
    out_rows(
        dot(hidden[0][...], store[0, :, 2 * fw :], LAST)
        + dot(hidden[1][...], store[1, :, 2 * fw :], LAST),
        outs,
    )


def feed(pos, n, w, fw, inner):
    rows, width = n[0].shape
    return call(
        functools.partial(feed_body, fw, inner),
        [shape((8 * rows, 512))] * 6 + [shape((8 * rows, width))] + [shape((rows, width))] * 8,
        [SM] + [VM] * 8 + [ANY] * 10,
        [VM] * 15,
        [pltpu.VMEM((2, width, 2 * fw + 512), BF), sems(inner)],
        cost=18,
    )(pos, *n, *w)


def feed_back_body(fw, inner, pos, rows_in, *refs):
    slope, silu = refs[0:2], refs[2:4]
    blocks = refs[4:14]
    d_gu, outs = refs[14:16], refs[16:24]
    store, sem = refs[24:]
    wait = start_all([block_copies(pos, inner, blocks, store, sem, i) for i in range(2)])
    for i in range(2):
        wait(i)
        out = dot(rows_in[...], store[i, :, 2 * fw :])
        a = (out * slope[i][...].astype(F32))[:, :fw]
        b = (out * silu[i][...].astype(F32))[:, :fw]
        d_gu[i][...] = jnp.concatenate([a, b], axis=1).astype(BF)
    out_rows(
        dot(d_gu[0][...], store[0, :, : 2 * fw], LAST)
        + dot(d_gu[1][...], store[1, :, : 2 * fw], LAST),
        outs,
    )


def feed_back(pos, d, slope, silu, w, fw, inner):
    rows, width = d.shape
    return call(
        functools.partial(feed_back_body, fw, inner),
        [shape((rows, 2 * fw))] * 2 + [shape((rows // 8, width))] * 8,
        [SM] + [VM] * 5 + [ANY] * 10,
        [VM] * 10,
        [pltpu.VMEM((2, width, 2 * fw + 512), BF), sems(inner)],
        cost=16,
    )(pos, d, *slope, *silu, *w)


def features(pos, k, step):
    return pl.ds(pl.multiple_of((pos[1] ^ k) * step, 128), step)


def block_grad_body(inner, parts, pos, left, right_a, right_b, out, store, sem):
    step = store.shape[1] // len(parts)
    depth = step // inner
    copies = []
    for p, k in enumerate(parts):
        spot = features(pos, k, step)
        for i, right in enumerate((right_a, right_b)):
            store[i, pl.ds(p * step, step), :] = dot(left[:, spot], right[...], ROWS).astype(BF)
            for j in range(inner):
                n = p * inner + j
                copies.append(
                    pltpu.make_async_copy(
                        store.at[i, pl.ds(n * depth, depth)],
                        out.at[j * 2 + (pos[3] ^ i), pl.ds(p * depth, depth)],
                        sem.at[i * len(parts) * inner + n],
                    )
                )
                copies[-1].start()
    for c in copies:
        c.wait()


def down_grad_body(inner, pos, *refs):
    pieces, right, out, rows_in, store, sem = refs[:8], refs[8:10], *refs[10:]
    join_rows(pieces, rows_in)
    block_grad_body(inner, range(PARTS), pos, rows_in, *right, out, store, sem)


def down_grad(pos, pieces, right, inner):
    rows, width = pieces[0].shape
    rows *= 8
    cols = right[0].shape[1]
    return call(
        functools.partial(down_grad_body, inner),
        [shape((inner * 2, width // inner, cols)), shape((rows, width))],
        [SM] + [VM] * 10,
        [ANY, VM],
        [pltpu.VMEM((2, width, cols), BF), sems(inner)],
        cost=7,
    )(pos, *pieces, *right)


def block_grad(pos, left, right, inner, parts):
    rows, width = left.shape
    cols = right[0].shape[1]
    held = width // PARTS * len(parts)
    return call(
        functools.partial(block_grad_body, inner, parts),
        shape((inner * 2, held // inner, cols)),
        [SM] + [VM] * 3,
        ANY,
        [pltpu.VMEM((2, held, cols), BF), sems(inner)],
        cost=7,
    )(pos, left, *right)


def attend_back_body(sides, pos, q_ref, row_ids, lse, cosine, sine, *refs):
    arrays = sides if sides <= 2 else 1
    d, refs = refs[:8], refs[8:]
    kvs, refs = refs[:arrays], refs[arrays:]
    w = refs[:16]
    dq_ref, own_ref, send_ref, rows_in = refs[16:20]
    store, mix, d_kv, sem = refs[20:]
    join_rows(d, rows_in)
    wait = fetch(pos, sides, w, store, sem)
    rows = q_ref.shape[0]
    qw = q_ref.shape[1] // 2
    for i in range(2):
        wait(i)
        mix[i] = dot(rows_in[...], store[i])[:, 320 : 320 + qw].astype(BF)
    ids = row_ids[0:1, :]
    read = reader(kvs, rows)

    def look(s):
        return read(s, ID_LANE).astype(F32) <= ids

    looks = [look(s) for s in range(sides)] if sides <= 2 else None
    d_q = []
    c = FACTOR * LOG2E
    head = 0
    for i in range(2):
        for start in range(0, qw, HEAD_DIM):
            q = q_ref[:, i * qw + start : i * qw + start + HEAD_DIM]
            dm = mix[i, :, start : start + HEAD_DIM]
            level = lse[head : head + 1, :]
            head += 1

            def pair(s):
                seen = looks[s] if looks else look(s)
                p = jnp.where(seen, jnp.exp2(dot(read(s, lanes(i)), q, LAST) * c - level), 0.0)
                return p, dot(read(s, lanes(2 + i)), dm, LAST)

            held = [pair(s) for s in range(sides)] if sides <= 2 else None

            def weigh(s, delta):
                p, dp = held[s] if held else pair(s)
                return delta + jnp.sum(p * dp, axis=0, keepdims=True)

            delta = each(sides, weigh, jnp.zeros((1, rows), F32))

            def grads(s, out):
                p, dp = held[s] if held else pair(s)
                ds = (p * (dp - delta)).astype(BF)
                d_value = dot(p.astype(BF), dm)
                d_key = dot(ds, q)
                if start == 0:
                    d_kv[2 + i, s] = d_value
                    d_kv[i, s] = d_key
                else:
                    d_kv[2 + i, s] += d_value
                    d_kv[i, s] += d_key
                return out + dot(read(s, lanes(i)), ds, ROWS)

            d_q.append(each(sides, grads, jnp.zeros((HEAD_DIM, rows), F32)))
    tall = jnp.concatenate(d_q + [jnp.zeros((512 - 4 * HEAD_DIM, rows), F32)], axis=0).T * FACTOR
    cos, sin = cosine[...], sine[...]
    dq_ref[...] = jnp.concatenate(
        [rotated(tall[:, h * HEAD_DIM : (h + 1) * HEAD_DIM], cos, -sin) for h in range(4)], axis=1
    ).astype(BF)
    for s in range(sides):
        value = jnp.concatenate([d_kv[0, s] * FACTOR, d_kv[1, s] * FACTOR, d_kv[2, s], d_kv[3, s]], axis=1)
        if s == 0:
            own_ref[...] = value
        else:
            send_ref[pl.ds((s - 1) * rows, rows), :] = value.astype(BF)


def attend_back(pos, d, q, kvs, row_ids, lse, cosine, sine, w, sides):
    rows = q.shape[0]
    width = d[0].shape[1]
    cols = 4 * HEAD_DIM
    return call(
        functools.partial(attend_back_body, sides),
        [shape(q.shape), shape((rows, cols), F32), shape(((sides - 1) * rows, cols)), shape((rows, width))],
        [SM] + [VM] * (13 + len(kvs)) + [ANY] * 16,
        [VM] * 4,
        [
            pltpu.VMEM((2, width, 512), BF),
            pltpu.VMEM((2, rows, q.shape[1] // 2), BF),
            pltpu.VMEM((4, sides, rows, HEAD_DIM), F32),
            sems(sides),
        ],
        cost=18,
    )(pos, q, row_ids, lse, cosine, sine, *d, *kvs, *w)


def split_body(dq_ref, own_ref, got_ref, cosine, sine, *d_qkv):
    qw = dq_ref.shape[1] // 2
    cos, sin = cosine[...], sine[...]
    d_kv = own_ref[...] + got_ref[...].astype(F32)
    d_q = dq_ref[...].astype(F32)
    for i in range(2):
        d_k = rotated(d_kv[:, i * HEAD_DIM : (i + 1) * HEAD_DIM], cos, -sin)
        d_v = d_kv[:, (2 + i) * HEAD_DIM : (3 + i) * HEAD_DIM]
        d_qkv[i][...] = padded(
            jnp.concatenate([d_q[:, i * qw : (i + 1) * qw], d_k, d_v], axis=1), 512
        ).astype(BF)


def split_grads(dq, own, got, cosine, sine):
    rows = dq.shape[0]
    return call(split_body, [shape((rows, 512))] * 2, [VM] * 5, [VM] * 2)(dq, own, got, cosine, sine)


def project_back_body(inner, pos, d_a, d_b, *refs):
    w, outs = refs[:16], refs[16:24]
    store, sem = refs[24:]
    wait = fetch(pos, inner, w, store, sem)
    for i in range(2):
        wait(i)
    out_rows(dot(d_a[...], store[0], LAST) + dot(d_b[...], store[1], LAST), outs)


def project_back(pos, d_qkv, w, inner):
    rows = d_qkv[0].shape[0] // 8
    width = 8 * w[0].shape[0]
    return call(
        functools.partial(project_back_body, inner),
        [shape((rows, width))] * 8,
        [SM] + [VM] * 2 + [ANY] * 16,
        [VM] * 8,
        [pltpu.VMEM((2, width, 512), BF), sems(inner)],
        cost=8,
    )(pos, *d_qkv, *w)


def pair_copies(pos, inner, outs, store, sem, i):
    half = inner // 2
    depth = store.shape[1] // (PARTS * inner)
    copies = []
    for k in range(PARTS):
        for j in range(inner):
            spot = ((k % 2) * half + j % half) * depth
            to = outs[2 * (k // 2) + j // half].at[pl.ds(spot, depth)]
            n = (i * PARTS + k) * inner + j
            copies.append(
                pltpu.make_async_copy(store.at[i, spot_of(pos, k, j, inner, depth)], to, sem.at[n])
            )
    return copies


def attn_grad_body(inner, pos, first, d_all, gain_two, sum_attn, sums, *refs):
    d_qkv, mixed = refs[:2], refs[2:4]
    w, outs = refs[4:20], refs[20:28]
    held, store, sem, out_sem = refs[28:]
    wait = fetch(pos, inner, w, held, sem)
    step = store.shape[1] // PARTS
    copies = [pair_copies(pos, inner, outs[4 * i : 4 * i + 4], store, out_sem, i) for i in range(2)]
    lane = lax.broadcasted_iota(jnp.int32, (1, 128), 1)
    tail = jnp.where(lane == 98, sums[0:1, :], 0.0)
    tail = jnp.where(lane == 99, sum_attn[0:1, :], tail)
    tail = jnp.where(lane == 100, sums[8:9, :], tail)
    wait(0)
    wait(1)
    for k in (3, 2, 1, 0):
        spot = features(pos, k, step)
        rows = [jnp.zeros((97, step), F32), gain_two[0:1, spot], jnp.zeros((30, step), F32)]
        tall = jnp.concatenate(rows, axis=0).T + tail
        values = [dot(first[:, spot], d_qkv[i][...], ROWS) for i in range(2)]
        gain = 0.0
        for i in range(2):
            gain = gain + jnp.sum(values[i] * held[i, spot, :].astype(F32), axis=1, keepdims=True)
        gain = gain / held[0, spot, 480:481].astype(F32)
        tall = tall + jnp.where(lane == 96, gain, 0.0)
        for i in range(2):
            value = values[i] + dot(d_all[:, spot], mixed[i][...], ROWS)
            store[i, spot, :384] = value[:, :384].astype(BF)
            store[i, spot, 384:] = (value[:, 384:] + tall).astype(BF)
            for c in copies[i][k * inner : (k + 1) * inner]:
                c.start()
    for i in range(2):
        for c in copies[i]:
            c.wait()


def attn_grad(pos, first, d_all, gain_two, sum_attn, sums, d_qkv, mixed, w, inner):
    rows, width = first.shape
    return call(
        functools.partial(attn_grad_body, inner),
        [shape((width // 4, 512))] * 8,
        [SM] + [VM] * 9 + [ANY] * 16,
        [ANY] * 8,
        [pltpu.VMEM((2, width, 512), BF), pltpu.VMEM((2, width, 512), BF), sems(inner), sems(inner)],
        cost=12,
    )(pos, first, d_all, gain_two, sum_attn, sums, *d_qkv, *mixed, *w)


def hold(values, *others):
    got = lax.optimization_barrier(tuple(values) + tuple(others))
    return list(got[: len(values)])


class Live:
    def fence(self):
        names = sorted(self.__dict__)
        leaves, tree = jax.tree.flatten([self.__dict__[n] for n in names])
        leaves = lax.optimization_barrier(tuple(leaves))
        self.__dict__.update(zip(names, jax.tree.unflatten(tree, leaves)))


class Place:
    def __init__(self):
        self.inner = lax.axis_size("y")
        self.count = PARTS * self.inner
        self.z, self.y, self.x, self.c = [lax.axis_index(name) for name in AXES]
        self.s = self.z * self.inner + self.y
        self.zs = self.z.reshape(1).astype(jnp.int32)
        self.bits = []
        b = 1
        while b < self.inner:
            self.bits.append(b)
            b *= 2

    def hop_z(self, v, k):
        return hop(v, "z", k)

    def hop_y(self, v, b):
        return hop(v, "y", b)

    def hop_x(self, v):
        return hop(v, "x", 1)

    def hop_c(self, v):
        return hop(v, "c", 1)

    def low_y(self, v):
        for b in self.bits[:-1]:
            v = jnp.concatenate([v, self.hop_y(v, b)], 0)
        return v

    def far_y(self, v):
        return self.hop_y(v, self.bits[-1])

    def add(self, own, got):
        return (own.astype(F32) + got.astype(F32)).astype(BF)

    def sum_y(self, own, far):
        value = self.add(own, self.far_y(far))
        for b in reversed(self.bits[:-1]):
            n = value.shape[0] // 2
            value = self.add(value[:n], self.hop_y(value[n:], b))
        return value

    def sum_x(self, own, other):
        return self.add(own, self.hop_x(other))

    def gather(self, own):
        mine = [own, self.hop_z(own, 1), self.hop_z(own, 2)]
        mine.append(self.hop_z(mine[2], 1))
        return mine + [self.hop_c(v) for v in mine]

    def scatter_one(self, outs):
        mine = list(outs[:4])
        got = [self.hop_c(v) for v in outs[4:]]
        one, two = second_sum(mine, got, self.hop_z(first_sum(mine[3], got[3]), 1))
        return [mine[0], got[0], one, two]

    def scatter_two(self, left):
        return left[0], left[1], self.hop_z(left[2], 1), self.hop_z(left[3], 2)

    def scatter(self, outs):
        return self.scatter_two(self.scatter_one(outs))


def tables(place):
    half = HEAD_DIM // 2
    freq = THETA ** (-(jnp.arange(half, dtype=F32) * 2.0 / HEAD_DIM))
    angle = place[:, None] * freq[None, :]
    return (jnp.cos(angle), jnp.sin(angle))


def on_device(
    inputs,
    targets,
    seq_ids,
    block_ids,
    attn_gain,
    mlp_gain,
    w_query,
    w_key,
    w_value,
    w_out,
    w_gate,
    w_up,
    w_down,
):
    at = Place()
    inner = at.inner
    full = inputs.shape[1]
    half_span = SPAN // 2
    kw = w_key.shape[1] // 2
    qw = w_query.shape[1] // PARTS
    fw = w_gate.shape[1] // PARTS
    row_f32 = shape((half_span, full), F32)
    row_bf = shape((half_span, full))

    off = jnp.where(seq_ids[0] == at.x, 0, SPAN)
    pos = jnp.stack([off + at.c * half_span, at.z, at.y, at.x, at.c]).astype(jnp.int32)
    spots = [
        (off if xr == 0 else SPAN - off) + (at.c ^ cr) * half_span for xr in range(2) for cr in range(2)
    ]
    spots = jnp.stack(spots).astype(jnp.int32)

    def all_rows(own):
        across = at.hop_x(own)
        return [own, at.hop_c(own), across, at.hop_c(across)]

    rows = 2 * PARTS * half_span
    count = jnp.arange(rows, dtype=jnp.int32)
    zz = at.z ^ ((count // half_span) % PARTS)
    cc = at.c ^ (count // (half_span * PARTS))
    place = ((zz * inner + at.y) * SPAN + cc * half_span + count % half_span).astype(F32)
    cosine, sine = tables(place)

    def listed(w):
        return [v for i in range(2) for k in range(PARTS) for v in w[k][i]]

    def gather_blocks(pair):
        return lax.all_gather(pair, ("y", "x"), axis=0)

    def scatter_blocks(blocks, count):
        blocks = blocks.reshape(-1, blocks.shape[-1])
        got = lax.psum_scatter(blocks, ("y", "x"), scatter_dimension=0, tiled=True)
        n = got.shape[0] // count
        return [got[k * n : (k + 1) * n] for k in range(count)]

    hop_x, hop_z, low_y, far_y = at.hop_x, at.hop_z, at.low_y, at.far_y
    live = Live()
    live.w = [w_gate, w_up, w_down]
    live.rows = [inputs, targets]
    live.qo = pack_attn(at.zs, w_query, w_key, w_value, w_out, attn_gain, mlp_gain, 512)
    live.fence()

    q = live.qo
    z = [q[0]] + [hop_z(q[k], k) for k in range(1, PARTS)]
    live.x_own, live.t_own = own_rows(pos, block_ids.reshape(1, -1), *live.rows)
    live.g = list(pack(at.zs, live.w, [(fw, 1)] * 3, 2 * fw + 512, 2 * fw))
    del live.w, live.rows
    live.g[1] = hop_z(hold([live.g[1]], z[1])[0], 1)
    v = low_y(z[0])
    w = far_y(v)
    live.q0 = (v, w, hop_x(v))
    live.q1 = (low_y(z[1]), low_y(hop_x(z[1])))
    live.z = z[2:]
    live.fence()

    near = gather_blocks(jnp.concatenate(live.g[:2], 0))
    v, w, u = live.q0
    q0 = ((v, w), (u, hop_x(w)))
    v, u = live.q1
    q1 = ((v, far_y(v)), (u, far_y(u)))
    v = low_y(live.z[0])
    w = far_y(v)
    q2 = ((v, w), (hop_x(v), hop_x(w)))
    u, v = low_y(hop_x(live.z[1])), low_y(live.z[1])
    q3 = ((v, far_y(v)), (u, far_y(u)))
    live.x_all = at.gather(live.x_own)
    live.w_qo = listed([q0, q1, q2, q3])
    live.g[2] = hop_z(live.g[2], 2)
    del live.z, live.q0, live.q1
    live.fence()

    live.first, live.query, kv, live.gain, live.row_ids = project(
        pos, live.x_all, cosine, sine, live.w_qo, qw, inner
    )
    live.kvs = [kv]
    live.g[4] = hop_z(live.g[4], 2)
    live.fence()

    g2 = gather_blocks(jnp.concatenate([live.g[2], live.g[4]], 1))

    kvs = live.kvs
    for b in at.bits:
        kvs = kvs + [at.hop_y(v, b) for v in kvs]
    if inner > 2:
        kvs = [jnp.concatenate(kvs, 0)]
    live.kvs = kvs
    mixed_a, mixed_b, live.lse, *live.outs = attend(
        pos, live.query, kvs, live.row_ids, live.w_qo, inner
    )
    live.mixed = (mixed_a, mixed_b)
    live.g[3] = hop_z(live.g[3], 3)
    live.w_near = near
    live.fence()

    live.left = at.scatter_one(live.outs)
    live.g[5] = hop_z(live.g[5], 3)
    v = low_y(live.g[3])
    live.g3 = (v, far_y(v), low_y(hop_x(live.g[3])))
    del live.outs
    live.fence()

    v, w, u = live.g3
    live.g3 = [v, w, u, far_y(u)]
    v = low_y(live.g[5])
    w = far_y(v)
    live.g3 += [v, w, hop_x(v), hop_x(w)]
    del live.g
    live.middle, n_own, live.sum_attn = call(
        after_attn_body,
        [row_f32, row_bf, shape((8, 128), F32)],
        [VM] * 6,
        [VM] * 3,
    )(*at.scatter_two(live.left), live.x_own, live.gain)
    live.n_all = at.gather(n_own)
    live.w_two = g2
    del live.left
    live.fence()

    live.w_ff = [live.w_near, live.w_two, *live.g3]
    del live.w_near, live.w_two, live.g3
    out = feed(pos, live.n_all, live.w_ff, fw, inner)
    live.hidden, live.slope, live.silu = out[:2], out[2:4], out[4:6]
    live.n_all, outs = out[6], out[7:]
    live.d_own, live.layer_own, live.sums = call(
        after_mlp_body,
        [row_bf, row_bf, shape((16, 128), F32)],
        [VM] * 6,
        [VM] * 3,
    )(*at.scatter(outs), live.middle, live.t_own)
    del live.t_own
    live.fence()

    live.d_rows = at.gather(live.d_own)
    live.layer_out = all_rows(live.layer_own)
    del live.layer_own
    live.fence()


    live.grad_d, live.d_rows = down_grad(pos, live.d_rows, live.hidden, inner)
    live.fence()

    d = scatter_blocks(live.grad_d, 4)
    out = feed_back(pos, live.d_rows, live.slope, live.silu, live.w_ff, fw, inner)
    live.d_gu, live.outs = out[:2], out[2:]
    del live.slope, live.silu, live.w_ff, live.d_rows, live.hidden, live.grad_d
    live.fence()

    live.left = at.scatter_one(live.outs)
    del live.outs
    live.far = block_grad(pos, live.n_all, live.d_gu, inner, (2, 3))
    live.fence()

    far = scatter_blocks(live.far, 2)
    live.d_middle, live.a_own, live.grad_gain_two = call(
        after_feed_back_body,
        [row_f32, row_bf, shape((1, full), F32)],
        [VM] * 7,
        [VM] * 3,
    )(*at.scatter_two(live.left), live.middle, live.d_own, live.gain)
    del live.middle, live.d_own, live.left, live.far
    live.near = block_grad(pos, live.n_all, live.d_gu, inner, (0, 1))
    del live.n_all, live.d_gu
    live.fence()

    near = scatter_blocks(live.near, 2)
    live.a_all = at.gather(live.a_own)
    del live.a_own, live.near
    live.fence()

    live.d_query, live.d_kv, live.sent, live.a_all = attend_back(
        pos, live.a_all, live.query, live.kvs, live.row_ids, live.lse, cosine, sine, live.w_qo, inner
    )
    del live.query, live.kvs, live.row_ids, live.lse
    live.d = [d[0], hop_z(d[1], 1), d[2], hop_z(d[3], 3)]
    live.fence()

    d_kv, sent = live.d_kv, live.sent
    if inner > 2:
        sent = jnp.concatenate([d_kv, sent.astype(F32)], 0)
        for b in reversed(at.bits[1:]):
            n = sent.shape[0] // 2
            sent = sent[:n] + at.hop_y(sent[n:].astype(BF), b).astype(F32)
        d_kv, sent = sent[:rows], sent[rows:].astype(BF)
    sent = at.hop_y(sent, at.bits[0])
    live.d_qkv = split_grads(live.d_query, d_kv, sent, cosine, sine)
    live.d[2] = hop_z(live.d[2], 2)
    del live.d_kv, live.sent, live.d_query
    live.fence()

    tails = (live.grad_gain_two, live.sum_attn, live.sums)
    q = attn_grad(pos, live.first, live.a_all, *tails, live.d_qkv, live.mixed, live.w_qo, inner)
    live.q_near, live.q_far = (q[0:2], q[4:6]), (q[2:4], q[6:8])
    live.far3 = hop_z(far[1], 3)
    del live.first, live.a_all, live.mixed
    del live.grad_gain_two, live.sum_attn, live.sums
    live.fence()

    live.left = at.scatter_one(project_back(pos, live.d_qkv, live.w_qo, inner))
    del live.d_qkv, live.w_qo
    q_near, q_far = live.q_near, live.q_far
    del live.q_near, live.q_far
    (a, b), (c, d) = q_far
    q_far = at.sum_y(at.sum_x(a, c), at.sum_x(b, d))
    q_near = at.sum_x(*[at.sum_y(*side) for side in q_near])
    far2 = hop_z(far[0], 2)
    live.fence()

    (live.input_own,) = call(
        after_all_body,
        [row_bf],
        [VM] * 7,
        [VM],
    )(*at.scatter_two(live.left), live.x_own, live.d_middle, live.gain)
    del live.left, live.x_own, live.d_middle
    live.q_near, live.q_far, live.far2 = q_near, q_far, far2
    (live.g_down,) = unpack(at.zs, live.d, [(0, fw, 1)])
    live.layer_out = spread_rows(spots, live.layer_out)
    del live.d
    live.fence()

    near_own, near_one = hold(near, live.input_own)
    live.g = [near_own, hop_z(near_one, 1), live.far2, live.far3]
    live.input_grad = all_rows(live.input_own)
    del live.far2, live.far3, live.input_own
    n = live.q_far.shape[0] // 2
    live.q = [live.q_near[:n], live.q_near[n:], hop_z(live.q_far[:n], 2), hop_z(live.q_far[n:], 3)]
    del live.q_near, live.q_far
    live.fence()

    q = live.q
    q[1] = hop_z(q[1], 1)
    layer_out, input_grad = live.layer_out, spread_rows(spots, live.input_grad)
    g_gate, g_up = unpack(at.zs, live.g, [(0, fw, 1), (fw, fw, 1)])
    g_down = live.g_down
    takes = [(0, qw, 1), (qw, kw, 2), (qw + kw, kw, 2), (qw + 2 * kw, qw, 1)]
    g_query, g_key, g_value, g_out = unpack(at.zs, q, takes)
    g_key, g_value = g_key.T, g_value.T
    tails = sum(p[:, 384:512].astype(F32) for p in q)
    tails = tails + at.hop_c(tails)
    entries = inputs.shape[0] * at.count * inputs.shape[1]
    rms = jnp.sqrt(tails[0, 98:101] / entries + EPS)
    return (
        layer_out,
        input_grad,
        g_query,
        g_key,
        g_value,
        g_out,
        g_gate,
        g_up,
        g_down,
        tails[:, 96],
        tails[:, 97],
        rms[0],
        rms[1],
        rms[2],
    )


def solution(mesh):
    devices = mesh.devices.reshape(PARTS, -1, 2, mesh.devices.shape[1] // 2)
    seq, mp = ("z", "y"), ("x", "c")
    rows, single, block = P(seq, None), P(seq), P(seq, mp)
    return jax.shard_map(
        on_device,
        mesh=Mesh(devices, AXES),
        in_specs=(rows, rows, single, single, single, single) + (block,) * 7,
        out_specs=(rows, rows) + (block,) * 7 + (single, single, P(), P(), P()),
        check_vma=False,
    )
```

```python
import functools

import jax
import jax.numpy as jnp
from jax import lax
from jax.experimental import pallas as pl
from jax.experimental.pallas import tpu as pltpu
from jax.sharding import Mesh
from jax.sharding import PartitionSpec as P

HEAD_DIM = 80
SPAN = 128
EPS = 1e-05
THETA = 1000000.0
PARTS = 4
BF = jnp.bfloat16
F32 = jnp.float32
FACTOR = HEAD_DIM**-0.5
LOG2E = 1.4426950408889634
LIMIT = 56 * 1024 * 1024

PLAIN = (((1,), (0,)), ((), ()))
LAST = (((1,), (1,)), ((), ()))
ROWS = (((0,), (0,)), ((), ()))

VM = pl.BlockSpec(memory_space=pltpu.VMEM)
SM = pl.BlockSpec(memory_space=pltpu.SMEM)
ANY = pl.BlockSpec(memory_space=pl.ANY)


def shape(dims, kind=BF):
    return jax.ShapeDtypeStruct(tuple(dims), kind)


def call(body, outs, in_specs, out_specs, scratch=(), cost=2):
    return pl.pallas_call(
        body,
        out_shape=outs,
        in_specs=in_specs,
        out_specs=out_specs,
        scratch_shapes=list(scratch),
        compiler_params=pltpu.CompilerParams(vmem_limit_bytes=LIMIT),
        cost_estimate=pl.CostEstimate(flops=cost * 10**9, bytes_accessed=0, transcendentals=0),
    )


AXES = ("z", "y", "x", "c")


def hop(value, axis, k):
    size = lax.axis_size(axis)
    return lax.ppermute(value, axis, [(i, i ^ k) for i in range(size)])


def dot(left, right, dims=PLAIN):
    return lax.dot_general(left, right, dims, preferred_element_type=F32)


def joined(values, width):
    values = [v.astype(F32) for v in values]
    have = sum(v.shape[1] for v in values)
    if have < width:
        values.append(jnp.zeros((values[0].shape[0], width - have), F32))
    return jnp.concatenate(values, axis=1).astype(BF)


def pack_body(takes, width, cut, z_ref, *refs):
    count = len(takes)
    ins, outs = refs[:count], refs[count:]
    for k in range(PARTS):
        part = z_ref[0] ^ k
        for j in range(PARTS):

            @pl.when(part == j)
            def _():
                values = [ref[:, pl.ds(step * (j // share), step)] for ref, (step, share) in zip(ins, takes)]
                value = joined(values, width)
                if cut and k >= 2:
                    outs[k][...] = value[:, :cut]
                    outs[k + 2][...] = value[:, cut:]
                else:
                    outs[k][...] = value


def pack(z, arrays, takes, width, cut=None):
    depth = arrays[0].shape[0]
    outs = [shape((depth, width))] * PARTS
    if cut:
        outs = outs[:2] + [shape((depth, cut))] * 2 + [shape((depth, width - cut))] * 2
    return call(
        functools.partial(pack_body, takes, width, cut),
        outs,
        [SM] + [VM] * len(arrays),
        [VM] * len(outs),
    )(z, *arrays)


def pack_attn_body(z_ref, wq, wk, wv, wo, gain_one, gain_two, *outs):
    depth, width = outs[0].shape
    kw = wk.shape[0] // 2
    qw = wq.shape[1] // PARTS
    narrow = jnp.concatenate([wk[...].astype(F32), wv[...].astype(F32)], axis=0)
    gains = jnp.concatenate([gain_one[...], gain_two[...]], axis=0).astype(F32)
    fill = jnp.zeros((128 - (4 * kw + 2) % 128, depth), F32)
    tall = jnp.concatenate([narrow, gains, fill], axis=0).T
    for k in range(PARTS):
        part = z_ref[0] ^ k
        for j in range(PARTS):

            @pl.when(part == j)
            def _():
                spot = pl.ds(qw * j, qw)
                h = j // 2
                values = [
                    wq[:, spot],
                    tall[:, kw * h : kw * h + kw],
                    tall[:, kw * (h + 2) : kw * (h + 3)],
                    wo[:, spot],
                    tall[:, 4 * kw : 4 * kw + 2],
                ]
                outs[k][...] = joined(values, width)


def pack_attn(z, wq, wk, wv, wo, gain_one, gain_two, width):
    depth = wq.shape[0]
    return call(
        pack_attn_body, [shape((depth, width))] * PARTS, [SM] + [VM] * 6, [VM] * PARTS
    )(z, wq, wk.T, wv.T, wo, gain_one.reshape(1, -1), gain_two.reshape(1, -1))


def unpack_body(takes, z_ref, *refs):
    ins, outs = refs[:PARTS], refs[PARTS:]
    for ref, (start, step, share) in zip(outs, takes):
        if share == 2:
            ref[...] = jnp.zeros_like(ref)
    depth = ins[0].shape[0]
    for k in range(PARTS):
        part = z_ref[0] ^ k
        flat = None
        if any(share == 2 for start, step, share in takes):
            first = min(start for start, step, share in takes if share == 2)
            last = max(start + step for start, step, share in takes if share == 2)
            fill = jnp.zeros((depth, -(last - first) % 128), F32)
            flat = jnp.concatenate([ins[k][:, pl.ds(first, last - first)].astype(F32), fill], axis=1).T
        for j in range(PARTS):

            @pl.when(part == j)
            def _():
                for ref, (start, step, share) in zip(outs, takes):
                    spot = pl.ds(step * (j // share), step)
                    if share == 1:
                        ref[:, spot] = ins[k][:, pl.ds(start, step)].astype(F32)
                    else:
                        ref[spot, :] += flat[start - first : start - first + step]


def unpack(z, pieces, takes):
    depth = pieces[0].shape[0]
    dims = [(depth, step * PARTS // share) for start, step, share in takes]
    dims = [d[::-1] if take[2] == 2 else d for d, take in zip(dims, takes)]
    return call(
        functools.partial(unpack_body, takes),
        [shape(d, F32) for d in dims],
        [SM] + [VM] * PARTS,
        [VM] * len(takes),
        cost=4,
    )(z, *pieces)


def spot_of(pos, k, j, inner, depth):
    return pl.ds(pl.multiple_of(((pos[1] ^ k) * inner + (pos[2] ^ j)) * depth, 16), depth)


def piece_copies(pos, inner, pieces, store, sem, i, lanes):
    half = inner // 2
    depth = store.shape[1] // (PARTS * inner)
    copies = []
    for k in range(PARTS):
        for j in range(inner):
            piece = pieces[2 * k + j // half].at[pl.ds((j % half) * depth, depth), lanes]
            n = (i * PARTS + k) * inner + j
            copies.append(
                pltpu.make_async_copy(piece, store.at[i, spot_of(pos, k, j, inner, depth)], sem.at[n])
            )
    return copies


def fetch(pos, inner, pieces, store, sem, start=0):
    lanes = pl.ds(start, store.shape[2])
    copies = [piece_copies(pos, inner, pieces[8 * i : 8 * i + 8], store, sem, i, lanes) for i in range(2)]
    return start_all(copies)


def start_all(copies):
    for half in copies:
        for c in half:
            c.start()

    def wait(i):
        for c in copies[i]:
            c.wait()

    return wait


def own_rows_body(pos, ids, x_ref, t_ref, x_out, t_out, tall):
    spot = pl.ds(pl.multiple_of(pos[0], 64), 64)
    width = x_ref.shape[1]
    tall[...] = jnp.broadcast_to(ids[...].astype(F32), tall.shape[::-1]).T
    x_out[:, :width] = x_ref[spot, :]
    x_out[:, width:] = tall[spot, :].astype(BF)
    t_out[...] = t_ref[spot, :]


def own_rows(pos, ids, x, t):
    rows, width = x.shape
    return call(
        own_rows_body,
        [shape((64, width + 128)), shape((64, width))],
        [SM] + [VM] * 3,
        [VM] * 2,
        [pltpu.VMEM((rows, 128), F32)],
    )(pos, ids, x, t)


def join_rows(pieces, out):
    n = pieces[0].shape[0]
    for i, ref in enumerate(pieces):
        out[pl.ds(i * n, n), :] = ref[:, : out.shape[1]]


def first_sum_body(mine, got, three):
    three[...] = (mine[...].astype(F32) + got[...].astype(F32)).astype(BF)


def first_sum(mine, got):
    return call(first_sum_body, shape(mine.shape), [VM] * 2, VM)(mine, got)


def second_sum_body(mine_one, mine_two, got, three, one, two):
    n = one.shape[0]
    one[...] = (mine_one[...].astype(F32) + got[pl.ds(n, n), :].astype(F32)).astype(BF)
    value = mine_two[...].astype(F32) + got[pl.ds(2 * n, n), :].astype(F32)
    two[...] = (value + three[...].astype(F32)).astype(BF)


def second_sum(mine, got, three):
    return call(second_sum_body, [shape(three.shape)] * 2, [VM] * 4, [VM] * 2)(
        mine[1], mine[2], got, three
    )


def last_sum(mine, got, one, two):
    first = mine[...].astype(F32) + got[pl.ds(0, mine.shape[0]), :].astype(F32)
    return first + one[...].astype(F32) + two[...].astype(F32)


def mean_scale(value):
    return lax.rsqrt(jnp.mean(value * value, axis=-1, keepdims=True) + EPS)


def back_norm(grad, value, gain):
    scale = mean_scale(value)
    unit = value * scale
    scaled = grad * gain
    return unit, scale * (scaled - unit * jnp.mean(scaled * unit, axis=-1, keepdims=True))


def after_attn_body(mine, got, one, two, x_own, gain, middle, n_own, total):
    branch = last_sum(mine, got, one, two)
    value = x_own[:, : branch.shape[1]].astype(F32) + branch
    middle[...] = value
    n_own[...] = (value * mean_scale(value) * gain[1:2, :]).astype(BF)
    total[...] = jnp.full(total.shape, jnp.sum(branch * branch), F32)


def after_mlp_body(mine, got, one, two, middle, target, d_own, out, total):
    branch = last_sum(mine, got, one, two)
    stream = middle[...] + branch
    d_own[...] = (stream - target[...].astype(F32)).astype(BF)
    out[...] = stream.astype(BF)
    total[0:8, :] = jnp.full((8, 128), jnp.sum(stream * stream), F32)
    total[8:16, :] = jnp.full((8, 128), jnp.sum(branch * branch), F32)


def after_feed_back_body(mine, got, one, two, middle, d_own, gain, d_middle, a_own, gain_grad):
    grad = last_sum(mine, got, one, two)
    unit, back = back_norm(grad, middle[...], gain[1:2, :])
    value = d_own[...].astype(F32) + back
    d_middle[...] = value
    a_own[...] = value.astype(BF)
    gain_grad[...] = jnp.sum(grad * unit, axis=0, keepdims=True)


def after_all_body(mine, got, one, two, x_own, d_middle, gain, out):
    grad = last_sum(mine, got, one, two)
    unit, back = back_norm(grad, x_own[:, : grad.shape[1]].astype(F32), gain[0:1, :])
    out[...] = (d_middle[...] + back).astype(BF)


def spread_rows_body(spots, p0, p1, p2, p3, out):
    n = p0.shape[0]
    for i, ref in enumerate((p0, p1, p2, p3)):
        out[pl.ds(pl.multiple_of(spots[i], 64), n), :] = ref[...]


def spread_rows(spots, pieces):
    n, width = pieces[0].shape
    return call(spread_rows_body, shape((4 * n, width)), [SM] + [VM] * 4, VM)(spots, *pieces)


def rotated(value, cosine, sine):
    half = HEAD_DIM // 2
    a, b = value[:, :half], value[:, half:]
    return jnp.concatenate([a * cosine - b * sine, b * cosine + a * sine], axis=1)


def project_body(qw, inner, pos, cosine, sine, *refs):
    x, w = refs[:8], refs[8:24]
    first, q_ref, kv_ref, gains, row_ids = refs[24:29]
    store, sem = refs[29:]
    wait = fetch(pos, inner, w, store, sem)
    width = first.shape[1]
    step = width // 4
    ids = jnp.concatenate([ref[:, width:] for ref in x], axis=0).astype(F32)
    row_ids[...] = ids.T[0:8, :]
    wait(0)
    spot = 480 - 384
    for p in range(4):
        tail = store[0, pl.ds(p * step, step), 384:512].astype(F32).T
        gains[:, pl.ds(p * step, step)] = tail[spot : spot + 8]
    gain = gains[0:1, :]
    rows = x[0].shape[0]
    for i, ref in enumerate(x):
        value = ref[:, :width].astype(F32)
        first[pl.ds(i * rows, rows), :] = (value * mean_scale(value) * gain).astype(BF)
    cos, sin = cosine[...], sine[...]
    queries, keys, values = [], [], []
    for i in range(2):
        if i:
            wait(1)
        out = dot(first[...], store[i, :, :384])
        for start in range(0, qw, HEAD_DIM):
            queries.append(rotated(out[:, start : start + HEAD_DIM], cos, sin))
        keys.append(rotated(out[:, qw : qw + HEAD_DIM], cos, sin))
        values.append(out[:, qw + HEAD_DIM : qw + 2 * HEAD_DIM])
    q_ref[...] = jnp.concatenate(queries, axis=1).astype(BF)
    kv_ref[...] = jnp.concatenate(keys + values + [ids[:, :64]], axis=1).astype(BF)


def sems(inner):
    return pltpu.SemaphoreType.DMA((2 * PARTS * inner,))


def project(pos, x, cosine, sine, w, qw, inner):
    rows, width = x[0].shape
    rows *= 8
    width -= 128
    return call(
        functools.partial(project_body, qw, inner),
        [
            shape((rows, width)),
            shape((rows, 2 * qw)),
            shape((rows, 384)),
            shape((8, width), F32),
            shape((8, rows), F32),
        ],
        [SM] + [VM] * 10 + [ANY] * 16,
        [VM] * 5,
        [pltpu.VMEM((2, width, 512), BF), sems(inner)],
        cost=12,
    )(pos, cosine, sine, *x, *w)


def out_rows(partial, outs):
    n = outs[0].shape[0]
    spots = [(i * n, n) for i in range(4)] + [(7 * n, n), (4 * n, 3 * n)]
    for (start, size), ref in zip(spots, outs):
        ref[...] = partial[start : start + size].astype(ref.dtype)


def row_shapes(rows, width):
    return [shape((rows, width))] * 5 + [shape((3 * rows, width))]


def each(count, step, start):
    if count <= 2:
        for s in range(count):
            start = step(s, start)
        return start
    return lax.fori_loop(0, count, step, start)


def reader(kvs, rows):
    def read(s, lane):
        if len(kvs) > 1:
            return kvs[s][:, lane]
        return kvs[0][pl.ds(pl.multiple_of(s * rows, rows), rows), lane]

    return read


def lanes(i):
    return pl.ds(i * HEAD_DIM, HEAD_DIM)


ID_LANE = pl.ds(4 * HEAD_DIM, 1)


def attend_body(sides, pos, q_ref, row_ids, *refs):
    arrays = sides if sides <= 2 else 1
    kvs, refs = refs[:arrays], refs[arrays:]
    w = refs[:16]
    mixed = refs[16:18]
    lse, sides_out = refs[18], refs[19:25]
    store, sem = refs[25:]
    wait = fetch(pos, sides, w, store, sem, 256)
    rows = q_ref.shape[0]
    qw = q_ref.shape[1] // 2
    ids = row_ids[0:1, :]
    read = reader(kvs, rows)

    def look(s):
        return read(s, ID_LANE).astype(F32) <= ids

    looks = [look(s) for s in range(sides)] if sides <= 2 else None
    lse[...] = jnp.zeros_like(lse)
    head = 0
    c = FACTOR * LOG2E
    for i in range(2):
        outs = []
        for start in range(i * qw, (i + 1) * qw, HEAD_DIM):
            q = q_ref[:, start : start + HEAD_DIM]

            def score(s):
                seen = looks[s] if looks else look(s)
                return jnp.where(seen, dot(read(s, lanes(i)), q, LAST), -1e30)

            scores = [score(s) for s in range(sides)] if sides <= 2 else None

            def highest(s, top):
                value = scores[s] if scores else score(s)
                return jnp.maximum(top, jnp.max(value, axis=0, keepdims=True))

            top = each(sides, highest, jnp.full((1, rows), -1e30, F32))

            def gathered(s, carry):
                total, out = carry
                value = scores[s] if scores else score(s)
                p = jnp.exp2(value * c - top * c)
                total = total + jnp.sum(p, axis=0, keepdims=True)
                return total, out + dot(read(s, lanes(2 + i)), p.astype(BF), ROWS)

            nothing = (jnp.zeros((1, rows), F32), jnp.zeros((HEAD_DIM, rows), F32))
            total, out = each(sides, gathered, nothing)
            outs.append(out / total)
            lse[head : head + 1, :] = top * c + jnp.log2(total)
            head += 1
        fill = jnp.zeros((512 - 320 - qw, rows), F32)
        tall = jnp.concatenate([jnp.zeros((64, rows), F32)] + outs + [fill], axis=0)
        mixed[i][...] = tall.T.astype(BF)
    for i in range(2):
        wait(i)
    partial = dot(mixed[0][...], store[0], LAST) + dot(mixed[1][...], store[1], LAST)
    out_rows(partial, sides_out)


def attend(pos, q, kvs, row_ids, w, sides):
    rows = q.shape[0]
    width = 8 * w[0].shape[0]
    return call(
        functools.partial(attend_body, sides),
        [shape((rows, 256))] * 2
        + [shape((8, rows), F32)]
        + row_shapes(rows // 8, width),
        [SM] + [VM] * (2 + len(kvs)) + [ANY] * 16,
        [VM] * 9,
        [pltpu.VMEM((2, width, 256), BF), sems(sides)],
        cost=12,
    )(pos, q, row_ids, *kvs, *w)


def padded(value, width):
    return jnp.concatenate([value, jnp.zeros((value.shape[0], width - value.shape[1]), value.dtype)], axis=1)


def block_copies(pos, inner, arrays, store, sem, i):
    depth = arrays[1].shape[1]
    half = inner // 2
    cut = arrays[2].shape[1]
    copies = [[], []]
    for k in range(PARTS):
        for j in range(inner):
            n = (i * PARTS + k) * inner + j
            if k < 3:
                row = pl.ds(pl.multiple_of(((pos[1] ^ k) * inner + j) * depth, 16), depth)
                for late in range(2):
                    lane = pl.ds(cut, store.shape[2] - cut) if late else pl.ds(0, cut)
                    spot = arrays[k // 2].at[j * 2 + (pos[3] ^ i), pl.ds(depth if k == 1 else 0, depth), lane]
                    to = store.at[i, row, lane]
                    copies[late].append(pltpu.make_async_copy(spot, to, sem.at[late, n]))
                continue
            for late in range(2):
                piece = arrays[2 + 4 * late + 2 * i + j // half]
                lane = pl.ds(cut * late, piece.shape[1])
                to = store.at[i, spot_of(pos, k, j, inner, depth), lane]
                spot = piece.at[pl.ds((j % half) * depth, depth)]
                copies[late].append(pltpu.make_async_copy(spot, to, sem.at[late, n]))
    return copies


def feed_body(fw, inner, pos, *refs):
    n, blocks = refs[:8], refs[8:18]
    hidden, slope, silu = refs[18:20], refs[20:22], refs[22:24]
    rows_out, outs = refs[24], refs[25:31]
    rows_in, kept, store, sem, out_sem = refs[31:]
    copies = [block_copies(pos, inner, blocks, store, sem, i) for i in range(2)]
    wait = start_all([copies[0][0], copies[1][0], copies[0][1] + copies[1][1]])
    join_rows(n, rows_in)
    saves = [pltpu.make_async_copy(rows_in, rows_out, out_sem.at[6])]
    saves[0].start()
    for i in range(2):
        wait(i)
        out = dot(rows_in[...], store[i, :, : 2 * fw])
        gate, upper = out[:, :fw], out[:, fw:]
        sigma = jax.nn.sigmoid(gate)
        act = gate * sigma
        values = (act * upper, upper * (sigma + act * (1.0 - sigma)), act)
        for n, (value, to) in enumerate(zip(values, (hidden, slope, silu))):
            kept[2 * n + i] = padded(value, 512).astype(BF)
            saves.append(pltpu.make_async_copy(kept.at[2 * n + i], to[i], out_sem.at[2 * n + i]))
            saves[-1].start()
    wait(2)
    out_rows(
        dot(kept[0], store[0, :, 2 * fw :], LAST) + dot(kept[1], store[1, :, 2 * fw :], LAST),
        outs,
    )
    for c in saves:
        c.wait()


def feed(pos, n, w, fw, inner):
    rows, width = n[0].shape
    return call(
        functools.partial(feed_body, fw, inner),
        [shape((8 * rows, 512))] * 6 + [shape((8 * rows, width))] + row_shapes(rows, width),
        [SM] + [VM] * 8 + [ANY] * 10,
        [ANY] * 7 + [VM] * 6,
        [
            pltpu.VMEM((8 * rows, width), BF),
            pltpu.VMEM((6, 8 * rows, 512), BF),
            pltpu.VMEM((2, width, 2 * fw + 512), BF),
            pltpu.SemaphoreType.DMA((2, 2 * PARTS * inner)),
            pltpu.SemaphoreType.DMA((7,)),
        ],
        cost=18,
    )(pos, *n, *w)


def feed_back_body(fw, inner, pos, rows_in, *refs):
    slope, silu = refs[0:2], refs[2:4]
    blocks = refs[4:14]
    d_gu, outs = refs[14:16], refs[16:22]
    kept, store, sem, out_sem = refs[22:]
    copies = [block_copies(pos, inner, blocks, store, sem, i) for i in range(2)]
    wait = start_all([copies[0][1], copies[1][1], copies[0][0] + copies[1][0]])
    saves = []
    for i in range(2):
        wait(i)
        out = dot(rows_in[...], store[i, :, 2 * fw :])
        a = (out * slope[i][...].astype(F32))[:, :fw]
        b = (out * silu[i][...].astype(F32))[:, :fw]
        kept[i] = jnp.concatenate([a, b], axis=1).astype(BF)
        saves.append(pltpu.make_async_copy(kept.at[i], d_gu[i], out_sem.at[i]))
        saves[-1].start()
    wait(2)
    out_rows(
        dot(kept[0], store[0, :, : 2 * fw], LAST) + dot(kept[1], store[1, :, : 2 * fw], LAST),
        outs,
    )
    for c in saves:
        c.wait()


def feed_back(pos, d, slope, silu, w, fw, inner):
    rows, width = d.shape
    return call(
        functools.partial(feed_back_body, fw, inner),
        [shape((rows, 2 * fw))] * 2 + row_shapes(rows // 8, width),
        [SM] + [VM] * 5 + [ANY] * 10,
        [ANY] * 2 + [VM] * 6,
        [
            pltpu.VMEM((2, rows, 2 * fw), BF),
            pltpu.VMEM((2, width, 2 * fw + 512), BF),
            pltpu.SemaphoreType.DMA((2, 2 * PARTS * inner)),
            pltpu.SemaphoreType.DMA((2,)),
        ],
        cost=16,
    )(pos, d, *slope, *silu, *w)


def features(pos, k, step):
    return pl.ds(pl.multiple_of((pos[1] ^ k) * step, 128), step)


def block_grad_body(inner, parts, pos, left, right_a, right_b, out, store, sem):
    step = store.shape[1] // len(parts)
    depth = step // inner
    copies = []
    for p, k in enumerate(parts):
        spot = features(pos, k, step)
        for i, right in enumerate((right_a, right_b)):
            store[i, pl.ds(p * step, step), :] = dot(left[:, spot], right[...], ROWS).astype(BF)
            for j in range(inner):
                n = p * inner + j
                copies.append(
                    pltpu.make_async_copy(
                        store.at[i, pl.ds(n * depth, depth)],
                        out.at[j * 2 + (pos[3] ^ i), pl.ds(p * depth, depth)],
                        sem.at[i * len(parts) * inner + n],
                    )
                )
                copies[-1].start()
    for c in copies:
        c.wait()


def down_grad_body(inner, pos, *refs):
    pieces, right, out, rows_in, store, sem = refs[:8], refs[8:10], *refs[10:]
    join_rows(pieces, rows_in)
    block_grad_body(inner, range(PARTS), pos, rows_in, *right, out, store, sem)


def down_grad(pos, pieces, right, inner):
    rows, width = pieces[0].shape
    rows *= 8
    cols = right[0].shape[1]
    return call(
        functools.partial(down_grad_body, inner),
        [shape((inner * 2, width // inner, cols)), shape((rows, width))],
        [SM] + [VM] * 10,
        [ANY, VM],
        [pltpu.VMEM((2, width, cols), BF), sems(inner)],
        cost=7,
    )(pos, *pieces, *right)


def block_grad(pos, left, right, inner, parts):
    rows, width = left.shape
    cols = right[0].shape[1]
    held = width // PARTS * len(parts)
    return call(
        functools.partial(block_grad_body, inner, parts),
        shape((inner * 2, held // inner, cols)),
        [SM] + [VM] * 3,
        ANY,
        [pltpu.VMEM((2, held, cols), BF), sems(inner)],
        cost=7,
    )(pos, left, *right)


def attend_back_body(sides, pos, q_ref, row_ids, lse, cosine, sine, *refs):
    arrays = sides if sides <= 2 else 1
    d, refs = refs[:8], refs[8:]
    kvs, refs = refs[:arrays], refs[arrays:]
    w = refs[:16]
    dq_ref, own_ref, send_ref, rows_in = refs[16:20]
    store, mix, d_kv, sem = refs[20:]
    join_rows(d, rows_in)
    wait = fetch(pos, sides, w, store, sem, 256)
    rows = q_ref.shape[0]
    qw = q_ref.shape[1] // 2
    for i in range(2):
        wait(i)
        mix[i] = dot(rows_in[...], store[i])[:, 64 : 64 + qw].astype(BF)
    ids = row_ids[0:1, :]
    read = reader(kvs, rows)

    def look(s):
        return read(s, ID_LANE).astype(F32) <= ids

    looks = [look(s) for s in range(sides)] if sides <= 2 else None
    d_q = []
    c = FACTOR * LOG2E
    head = 0
    for i in range(2):
        for start in range(0, qw, HEAD_DIM):
            q = q_ref[:, i * qw + start : i * qw + start + HEAD_DIM]
            dm = mix[i, :, start : start + HEAD_DIM]
            level = lse[head : head + 1, :]
            head += 1

            def pair(s):
                seen = looks[s] if looks else look(s)
                p = jnp.where(seen, jnp.exp2(dot(read(s, lanes(i)), q, LAST) * c - level), 0.0)
                return p, dot(read(s, lanes(2 + i)), dm, LAST)

            held = [pair(s) for s in range(sides)] if sides <= 2 else None

            def weigh(s, delta):
                p, dp = held[s] if held else pair(s)
                return delta + jnp.sum(p * dp, axis=0, keepdims=True)

            delta = each(sides, weigh, jnp.zeros((1, rows), F32))

            def grads(s, out):
                p, dp = held[s] if held else pair(s)
                ds = (p * (dp - delta)).astype(BF)
                d_value = dot(p.astype(BF), dm)
                d_key = dot(ds, q)
                if start == 0:
                    d_kv[2 + i, s] = d_value
                    d_kv[i, s] = d_key
                else:
                    d_kv[2 + i, s] += d_value
                    d_kv[i, s] += d_key
                return out + dot(read(s, lanes(i)), ds, ROWS)

            d_q.append(each(sides, grads, jnp.zeros((HEAD_DIM, rows), F32)))
    tall = jnp.concatenate(d_q + [jnp.zeros((512 - 4 * HEAD_DIM, rows), F32)], axis=0).T * FACTOR
    cos, sin = cosine[...], sine[...]
    dq_ref[...] = jnp.concatenate(
        [rotated(tall[:, h * HEAD_DIM : (h + 1) * HEAD_DIM], cos, -sin) for h in range(4)], axis=1
    ).astype(BF)
    for s in range(sides):
        value = jnp.concatenate([d_kv[0, s] * FACTOR, d_kv[1, s] * FACTOR, d_kv[2, s], d_kv[3, s]], axis=1)
        if s == 0:
            own_ref[...] = value
        else:
            send_ref[pl.ds((s - 1) * rows, rows), :] = value.astype(BF)


def attend_back(pos, d, q, kvs, row_ids, lse, cosine, sine, w, sides):
    rows = q.shape[0]
    width = d[0].shape[1]
    cols = 4 * HEAD_DIM
    return call(
        functools.partial(attend_back_body, sides),
        [shape(q.shape), shape((rows, cols), F32), shape(((sides - 1) * rows, cols)), shape((rows, width))],
        [SM] + [VM] * (13 + len(kvs)) + [ANY] * 16,
        [VM] * 4,
        [
            pltpu.VMEM((2, width, 256), BF),
            pltpu.VMEM((2, rows, q.shape[1] // 2), BF),
            pltpu.VMEM((4, sides, rows, HEAD_DIM), F32),
            sems(sides),
        ],
        cost=18,
    )(pos, q, row_ids, lse, cosine, sine, *d, *kvs, *w)


def split_body(dq_ref, own_ref, got_ref, cosine, sine, *d_qkv):
    qw = dq_ref.shape[1] // 2
    cos, sin = cosine[...], sine[...]
    d_kv = own_ref[...] + got_ref[...].astype(F32)
    d_q = dq_ref[...].astype(F32)
    for i in range(2):
        d_k = rotated(d_kv[:, i * HEAD_DIM : (i + 1) * HEAD_DIM], cos, -sin)
        d_v = d_kv[:, (2 + i) * HEAD_DIM : (3 + i) * HEAD_DIM]
        d_qkv[i][...] = padded(
            jnp.concatenate([d_q[:, i * qw : (i + 1) * qw], d_k, d_v], axis=1), 384
        ).astype(BF)


def split_grads(dq, own, got, cosine, sine):
    rows = dq.shape[0]
    return call(split_body, [shape((rows, 384))] * 2, [VM] * 5, [VM] * 2)(dq, own, got, cosine, sine)


def project_back_body(inner, pos, d_a, d_b, *refs):
    w, outs = refs[:16], refs[16:22]
    store, sem = refs[22:]
    wait = fetch(pos, inner, w, store, sem)
    for i in range(2):
        wait(i)
    out_rows(dot(d_a[...], store[0], LAST) + dot(d_b[...], store[1], LAST), outs)


def project_back(pos, d_qkv, w, inner):
    rows = d_qkv[0].shape[0] // 8
    width = 8 * w[0].shape[0]
    return call(
        functools.partial(project_back_body, inner),
        row_shapes(rows, width),
        [SM] + [VM] * 2 + [ANY] * 16,
        [VM] * 6,
        [pltpu.VMEM((2, width, 384), BF), sems(inner)],
        cost=8,
    )(pos, *d_qkv, *w)


def pair_copies(pos, inner, far, near, store, sem, i):
    half = inner // 2
    depth = store.shape[1] // (PARTS * inner)
    copies = []
    for k in range(PARTS):
        for j in range(inner):
            if k >= 2:
                to = far[j // half].at[pl.ds(((k % 2) * half + j % half) * depth, depth)]
            else:
                to = near.at[(pos[2] ^ j) * 2 + (pos[3] ^ i), pl.ds(k * depth, depth)]
            n = (i * PARTS + k) * inner + j
            copies.append(
                pltpu.make_async_copy(store.at[i, spot_of(pos, k, j, inner, depth)], to, sem.at[n])
            )
    return copies


def attn_grad_body(inner, pos, first, d_all, gain_two, sum_attn, sums, *refs):
    d_qkv, mixed = refs[:2], refs[2:4]
    w, outs, near = refs[4:20], refs[20:24], refs[24]
    held, store, sem, out_sem = refs[25:]
    wait = fetch(pos, inner, w, held, sem)
    step = store.shape[1] // PARTS
    copies = [pair_copies(pos, inner, outs[2 * i : 2 * i + 2], near, store, out_sem, i) for i in range(2)]
    lane = lax.broadcasted_iota(jnp.int32, (1, 128), 1)
    tail = jnp.where(lane == 98, sums[0:1, :], 0.0)
    tail = jnp.where(lane == 99, sum_attn[0:1, :], tail)
    tail = jnp.where(lane == 100, sums[8:9, :], tail)
    for k in (3, 2, 1, 0):
        spot = features(pos, k, step)
        rows = [jnp.zeros((97, step), F32), gain_two[0:1, spot], jnp.zeros((30, step), F32)]
        tall = jnp.concatenate(rows, axis=0).T + tail
        values = [dot(first[:, spot], d_qkv[i][...], ROWS) for i in range(2)]
        others = [dot(d_all[:, spot], mixed[i][...], ROWS) for i in range(2)]
        if k == 3:
            wait(0)
            wait(1)
        gain = 0.0
        for i in range(2):
            gain = gain + jnp.sum(values[i] * held[i, spot, :384].astype(F32), axis=1, keepdims=True)
        gain = gain / held[0, spot, 480:481].astype(F32)
        tall = tall + jnp.where(lane == 96, gain, 0.0)
        for i in range(2):
            store[i, spot, :256] = values[i][:, :256].astype(BF)
            store[i, spot, 256:384] = (values[i][:, 256:] + others[i][:, :128]).astype(BF)
            store[i, spot, 384:] = (others[i][:, 128:] + tall).astype(BF)
            for c in copies[i][k * inner : (k + 1) * inner]:
                c.start()
    for i in range(2):
        for c in copies[i]:
            c.wait()


def attn_grad(pos, first, d_all, gain_two, sum_attn, sums, d_qkv, mixed, w, inner):
    rows, width = first.shape
    return call(
        functools.partial(attn_grad_body, inner),
        [shape((width // 4, 512))] * 4 + [shape((inner * 2, width // (2 * inner), 512))],
        [SM] + [VM] * 9 + [ANY] * 16,
        [ANY] * 5,
        [pltpu.VMEM((2, width, 512), BF), pltpu.VMEM((2, width, 512), BF), sems(inner), sems(inner)],
        cost=12,
    )(pos, first, d_all, gain_two, sum_attn, sums, *d_qkv, *mixed, *w)


def hold(values, *others):
    got = lax.optimization_barrier(tuple(values) + tuple(others))
    return list(got[: len(values)])


class Live:
    def fence(self):
        names = sorted(self.__dict__)
        leaves, tree = jax.tree.flatten([self.__dict__[n] for n in names])
        leaves = lax.optimization_barrier(tuple(leaves))
        self.__dict__.update(zip(names, jax.tree.unflatten(tree, leaves)))


class Place:
    def __init__(self):
        self.inner = lax.axis_size("y")
        self.count = PARTS * self.inner
        self.z, self.y, self.x, self.c = [lax.axis_index(name) for name in AXES]
        self.s = self.z * self.inner + self.y
        self.zs = self.z.reshape(1).astype(jnp.int32)
        self.bits = []
        b = 1
        while b < self.inner:
            self.bits.append(b)
            b *= 2

    def hop_z(self, v, k):
        return hop(v, "z", k)

    def hop_y(self, v, b):
        return hop(v, "y", b)

    def hop_x(self, v):
        return hop(v, "x", 1)

    def hop_c(self, v):
        return hop(v, "c", 1)

    def low_y(self, v):
        for b in self.bits[:-1]:
            v = jnp.concatenate([v, self.hop_y(v, b)], 0)
        return v

    def far_y(self, v):
        return self.hop_y(v, self.bits[-1])

    def add(self, own, got):
        return (own.astype(F32) + got.astype(F32)).astype(BF)

    def halves(self, own, got):
        n = own.shape[0] // 2
        return [self.add(own[:n], got[:n]), self.add(own[n:], got[n:])]

    def sum_y(self, own, far):
        value = self.add(own, self.far_y(far))
        for b in reversed(self.bits[:-1]):
            n = value.shape[0] // 2
            value = self.add(value[:n], self.hop_y(value[n:], b))
        return value

    def sum_x(self, own, other):
        return self.add(own, self.hop_x(other))

    def gather(self, own):
        mine = [own, self.hop_z(own, 1), self.hop_z(own, 2)]
        mine.append(self.hop_z(mine[2], 1))
        return mine + [self.hop_c(v) for v in mine]

    def scatter_one(self, outs):
        mine = list(outs[:4])
        last, rest = [self.hop_c(v) for v in outs[4:]]
        one, two = second_sum(mine, rest, self.hop_z(first_sum(mine[3], last), 1))
        return [mine[0], rest, one, two]

    def scatter_two(self, left):
        return left[0], left[1], self.hop_z(left[2], 1), self.hop_z(left[3], 2)

    def scatter(self, outs):
        return self.scatter_two(self.scatter_one(outs))


def tables(place):
    half = HEAD_DIM // 2
    freq = THETA ** (-(jnp.arange(half, dtype=F32) * 2.0 / HEAD_DIM))
    angle = place[:, None] * freq[None, :]
    return (jnp.cos(angle), jnp.sin(angle))


def on_device(
    inputs,
    targets,
    seq_ids,
    block_ids,
    attn_gain,
    mlp_gain,
    w_query,
    w_key,
    w_value,
    w_out,
    w_gate,
    w_up,
    w_down,
):
    at = Place()
    inner = at.inner
    full = inputs.shape[1]
    half_span = SPAN // 2
    kw = w_key.shape[1] // 2
    qw = w_query.shape[1] // PARTS
    fw = w_gate.shape[1] // PARTS
    row_f32 = shape((half_span, full), F32)
    row_bf = shape((half_span, full))

    off = jnp.where(seq_ids[0] == at.x, 0, SPAN)
    pos = jnp.stack([off + at.c * half_span, at.z, at.y, at.x, at.c]).astype(jnp.int32)
    spots = [
        (off if xr == 0 else SPAN - off) + (at.c ^ cr) * half_span for xr in range(2) for cr in range(2)
    ]
    spots = jnp.stack(spots).astype(jnp.int32)

    def all_rows(own):
        across = at.hop_x(own)
        return [own, at.hop_c(own), across, at.hop_c(across)]

    rows = 2 * PARTS * half_span
    count = jnp.arange(rows, dtype=jnp.int32)
    zz = at.z ^ ((count // half_span) % PARTS)
    cc = at.c ^ (count // (half_span * PARTS))
    place = ((zz * inner + at.y) * SPAN + cc * half_span + count % half_span).astype(F32)
    cosine, sine = tables(place)

    def listed(w):
        return [v for i in range(2) for k in range(PARTS) for v in w[k][i]]

    def gather_blocks(pair):
        return lax.all_gather(pair, ("y", "x"), axis=0)

    def scatter_blocks(blocks, count):
        blocks = blocks.reshape(-1, blocks.shape[-1])
        got = lax.psum_scatter(blocks, ("y", "x"), scatter_dimension=0, tiled=True)
        n = got.shape[0] // count
        return [got[k * n : (k + 1) * n] for k in range(count)]

    hop_x, hop_z, low_y, far_y = at.hop_x, at.hop_z, at.low_y, at.far_y
    live = Live()
    live.w = [w_gate, w_up, w_down]
    live.rows = [inputs, targets]
    live.qo = pack_attn(at.zs, w_query, w_key, w_value, w_out, attn_gain, mlp_gain, 512)
    live.fence()

    q = live.qo
    z = [q[0]] + [hop_z(q[k], k) for k in range(1, PARTS)]
    live.x_own, live.t_own = own_rows(pos, block_ids.reshape(1, -1), *live.rows)
    live.g = list(pack(at.zs, live.w, [(fw, 1)] * 3, 2 * fw + 512, 2 * fw))
    del live.w, live.rows
    live.g[1] = hop_z(hold([live.g[1]], z[1])[0], 1)
    v = low_y(z[0])
    w = far_y(v)
    live.q0 = (v, w, hop_x(v))
    live.q1 = (low_y(z[1]), low_y(hop_x(z[1])))
    live.z = z[2:]
    live.fence()

    near = gather_blocks(jnp.concatenate(live.g[:2], 0))
    v, w, u = live.q0
    q0 = ((v, w), (u, hop_x(w)))
    v, u = live.q1
    q1 = ((v, far_y(v)), (u, far_y(u)))
    v = low_y(live.z[0])
    w = far_y(v)
    q2 = ((v, w), (hop_x(v), hop_x(w)))
    u, v = low_y(hop_x(live.z[1])), low_y(live.z[1])
    q3 = ((v, far_y(v)), (u, far_y(u)))
    live.x_all = at.gather(live.x_own)
    live.w_qo = listed([q0, q1, q2, q3])
    live.g[2] = hop_z(live.g[2], 2)
    del live.z, live.q0, live.q1
    live.fence()

    live.first, live.query, kv, live.gain, live.row_ids = project(
        pos, live.x_all, cosine, sine, live.w_qo, qw, inner
    )
    live.kvs = [kv]
    live.g[4] = hop_z(live.g[4], 2)
    live.fence()

    g2 = gather_blocks(jnp.concatenate([live.g[2], live.g[4]], 1))

    kvs = live.kvs
    for b in at.bits:
        kvs = kvs + [at.hop_y(v, b) for v in kvs]
    if inner > 2:
        kvs = [jnp.concatenate(kvs, 0)]
    live.kvs = kvs
    mixed_a, mixed_b, live.lse, *live.outs = attend(
        pos, live.query, kvs, live.row_ids, live.w_qo, inner
    )
    live.mixed = (mixed_a, mixed_b)
    live.g[3] = hop_z(live.g[3], 3)
    live.w_near = near
    live.fence()

    live.left = at.scatter_one(live.outs)
    live.g[5] = hop_z(live.g[5], 3)
    v = low_y(live.g[3])
    live.g3 = (v, far_y(v), low_y(hop_x(live.g[3])))
    del live.outs
    live.fence()

    v, w, u = live.g3
    live.g3 = [v, w, u, far_y(u)]
    v = low_y(live.g[5])
    w = far_y(v)
    live.g3 += [v, w, hop_x(v), hop_x(w)]
    del live.g
    live.middle, n_own, live.sum_attn = call(
        after_attn_body,
        [row_f32, row_bf, shape((8, 128), F32)],
        [VM] * 6,
        [VM] * 3,
    )(*at.scatter_two(live.left), live.x_own, live.gain)
    live.n_all = at.gather(n_own)
    live.w_two = g2
    del live.left
    live.fence()

    live.w_ff = [live.w_near, live.w_two, *live.g3]
    del live.w_near, live.w_two, live.g3
    out = feed(pos, live.n_all, live.w_ff, fw, inner)
    live.hidden, live.slope, live.silu = out[:2], out[2:4], out[4:6]
    live.n_all, outs = out[6], out[7:]
    live.d_own, live.layer_own, live.sums = call(
        after_mlp_body,
        [row_bf, row_bf, shape((16, 128), F32)],
        [VM] * 6,
        [VM] * 3,
    )(*at.scatter(outs), live.middle, live.t_own)
    del live.t_own
    live.fence()

    live.d_rows = at.gather(live.d_own)
    live.layer_out = all_rows(live.layer_own)
    del live.layer_own
    live.fence()


    live.grad_d, live.d_rows = down_grad(pos, live.d_rows, live.hidden, inner)
    live.fence()

    d = scatter_blocks(live.grad_d, 4)
    out = feed_back(pos, live.d_rows, live.slope, live.silu, live.w_ff, fw, inner)
    live.d_gu, live.outs = out[:2], out[2:]
    del live.slope, live.silu, live.w_ff, live.d_rows, live.hidden, live.grad_d
    live.fence()

    live.left = at.scatter_one(live.outs)
    del live.outs
    live.far = block_grad(pos, live.n_all, live.d_gu, inner, (2, 3))
    live.fence()

    far = scatter_blocks(live.far, 2)
    live.d_middle, live.a_own, live.grad_gain_two = call(
        after_feed_back_body,
        [row_f32, row_bf, shape((1, full), F32)],
        [VM] * 7,
        [VM] * 3,
    )(*at.scatter_two(live.left), live.middle, live.d_own, live.gain)
    del live.middle, live.d_own, live.left, live.far
    live.near = block_grad(pos, live.n_all, live.d_gu, inner, (0, 1))
    del live.n_all, live.d_gu
    live.fence()

    near = scatter_blocks(live.near, 2)
    live.a_all = at.gather(live.a_own)
    del live.a_own, live.near
    live.fence()

    live.d_query, live.d_kv, live.sent, live.a_all = attend_back(
        pos, live.a_all, live.query, live.kvs, live.row_ids, live.lse, cosine, sine, live.w_qo, inner
    )
    del live.query, live.kvs, live.row_ids, live.lse
    live.d = [d[0], hop_z(d[1], 1), d[2], hop_z(d[3], 3)]
    live.fence()

    d_kv, sent = live.d_kv, live.sent
    if inner > 2:
        sent = jnp.concatenate([d_kv, sent.astype(F32)], 0)
        for b in reversed(at.bits[1:]):
            n = sent.shape[0] // 2
            sent = sent[:n] + at.hop_y(sent[n:].astype(BF), b).astype(F32)
        d_kv, sent = sent[:rows], sent[rows:].astype(BF)
    sent = at.hop_y(sent, at.bits[0])
    live.d_qkv = split_grads(live.d_query, d_kv, sent, cosine, sine)
    live.d[2] = hop_z(live.d[2], 2)
    del live.d_kv, live.sent, live.d_query
    live.fence()

    tails = (live.grad_gain_two, live.sum_attn, live.sums)
    q = attn_grad(pos, live.first, live.a_all, *tails, live.d_qkv, live.mixed, live.w_qo, inner)
    live.q_far, live.q_near = (q[0:2], q[2:4]), q[4]
    live.far3 = hop_z(far[1], 3)
    del live.first, live.a_all, live.mixed
    del live.grad_gain_two, live.sum_attn, live.sums
    live.fence()

    live.left = at.scatter_one(project_back(pos, live.d_qkv, live.w_qo, inner))
    del live.d_qkv, live.w_qo
    q_near, q_far = scatter_blocks(live.q_near, 2), live.q_far
    del live.q_near, live.q_far
    (a, b), (c, d) = q_far
    q_far, last = at.sum_x(a, c), at.sum_x(b, d)
    if inner == 2:
        q_far = at.halves(q_far, at.far_y(last))
    else:
        q_far = jnp.split(at.sum_y(q_far, last), 2)
    far2 = hop_z(far[0], 2)
    live.fence()

    (live.input_own,) = call(
        after_all_body,
        [row_bf],
        [VM] * 7,
        [VM],
    )(*at.scatter_two(live.left), live.x_own, live.d_middle, live.gain)
    del live.left, live.x_own, live.d_middle
    live.q_far, live.far2 = q_far, far2
    (live.g_down,) = unpack(at.zs, live.d, [(0, fw, 1)])
    live.layer_out = spread_rows(spots, live.layer_out)
    del live.d
    live.fence()

    near_own, near_one = hold(near, live.input_own)
    live.g = [near_own, hop_z(near_one, 1), live.far2, live.far3]
    live.input_grad = all_rows(live.input_own)
    del live.far2, live.far3, live.input_own
    live.q = [hop_z(live.q_far[0], 2), hop_z(live.q_far[1], 3)]
    del live.q_far
    live.fence()

    q_near = hold(q_near, live.q[0])
    q = [q_near[0], hop_z(q_near[1], 1), *live.q]
    layer_out, input_grad = live.layer_out, spread_rows(spots, live.input_grad)
    g_gate, g_up = unpack(at.zs, live.g, [(0, fw, 1), (fw, fw, 1)])
    g_down = live.g_down
    takes = [(0, qw, 1), (qw, kw, 2), (qw + kw, kw, 2), (qw + 2 * kw, qw, 1)]
    g_query, g_key, g_value, g_out = unpack(at.zs, q, takes)
    g_key, g_value = g_key.T, g_value.T
    tails = sum(p[:, 384:512].astype(F32) for p in q)
    tails = tails + at.hop_c(tails)
    entries = inputs.shape[0] * at.count * inputs.shape[1]
    rms = jnp.sqrt(tails[0, 98:101] / entries + EPS)
    return (
        layer_out,
        input_grad,
        g_query,
        g_key,
        g_value,
        g_out,
        g_gate,
        g_up,
        g_down,
        tails[:, 96],
        tails[:, 97],
        rms[0],
        rms[1],
        rms[2],
    )


def solution(mesh):
    devices = mesh.devices.reshape(PARTS, -1, 2, mesh.devices.shape[1] // 2)
    seq, mp = ("z", "y"), ("x", "c")
    rows, single, block = P(seq, None), P(seq), P(seq, mp)
    return jax.shard_map(
        on_device,
        mesh=Mesh(devices, AXES),
        in_specs=(rows, rows, single, single, single, single) + (block,) * 7,
        out_specs=(rows, rows) + (block,) * 7 + (single, single, P(), P(), P()),
        check_vma=False,
    )
```

```python
import functools

import jax
import jax.numpy as jnp
from jax import lax
from jax.experimental import pallas as pl
from jax.experimental.pallas import tpu as pltpu
from jax.sharding import Mesh
from jax.sharding import PartitionSpec as P

HEAD_DIM = 80
SPAN = 128
EPS = 1e-05
THETA = 1000000.0
PARTS = 4
BF = jnp.bfloat16
F32 = jnp.float32
FACTOR = HEAD_DIM**-0.5
LOG2E = 1.4426950408889634
LIMIT = 48 * 1024 * 1024

PLAIN = (((1,), (0,)), ((), ()))
LAST = (((1,), (1,)), ((), ()))
ROWS = (((0,), (0,)), ((), ()))

VM = pl.BlockSpec(memory_space=pltpu.VMEM)
SM = pl.BlockSpec(memory_space=pltpu.SMEM)
ANY = pl.BlockSpec(memory_space=pl.ANY)


def shape(dims, kind=BF):
    return jax.ShapeDtypeStruct(tuple(dims), kind)


def call(body, outs, in_specs, out_specs, scratch=(), cost=2):
    return pl.pallas_call(
        body,
        out_shape=outs,
        in_specs=in_specs,
        out_specs=out_specs,
        scratch_shapes=list(scratch),
        compiler_params=pltpu.CompilerParams(vmem_limit_bytes=LIMIT if cost > 4 else 16 * 1024 * 1024),
        cost_estimate=pl.CostEstimate(flops=cost * 10**9, bytes_accessed=0, transcendentals=0),
    )


AXES = ("z", "y", "x", "c")


def hop(value, axis, k):
    size = lax.axis_size(axis)
    return lax.ppermute(value, axis, [(i, i ^ k) for i in range(size)])


def dot(left, right, dims=PLAIN):
    return lax.dot_general(left, right, dims, preferred_element_type=F32)


def joined(values, width):
    values = [v.astype(F32) for v in values]
    have = sum(v.shape[1] for v in values)
    if have < width:
        values.append(jnp.zeros((values[0].shape[0], width - have), F32))
    return jnp.concatenate(values, axis=1).astype(BF)


def pack_body(takes, width, cut, z_ref, *refs):
    count = len(takes)
    ins, outs = refs[:count], refs[count:]
    for k in range(PARTS):
        part = z_ref[0] ^ k
        for j in range(PARTS):

            @pl.when(part == j)
            def _():
                values = [ref[:, pl.ds(step * (j // share), step)] for ref, (step, share) in zip(ins, takes)]
                value = joined(values, width)
                if cut and k >= 2:
                    outs[k][...] = value[:, :cut]
                    outs[k + 2][...] = value[:, cut:]
                else:
                    outs[k][...] = value


def pack(z, arrays, takes, width, cut=None):
    depth = arrays[0].shape[0]
    outs = [shape((depth, width))] * PARTS
    if cut:
        outs = outs[:2] + [shape((depth, cut))] * 2 + [shape((depth, width - cut))] * 2
    return call(
        functools.partial(pack_body, takes, width, cut),
        outs,
        [SM] + [VM] * len(arrays),
        [VM] * len(outs),
    )(z, *arrays)


def pack_attn_body(z_ref, wq, wk, wv, wo, gain_one, gain_two, *outs):
    depth, width = outs[0].shape
    kw = wk.shape[0] // 2
    qw = wq.shape[1] // PARTS
    narrow = jnp.concatenate([wk[...].astype(F32), wv[...].astype(F32)], axis=0)
    gains = jnp.concatenate([gain_one[...], gain_two[...]], axis=0).astype(F32)
    fill = jnp.zeros((128 - (4 * kw + 2) % 128, depth), F32)
    tall = jnp.concatenate([narrow, gains, fill], axis=0).T
    for k in range(PARTS):
        part = z_ref[0] ^ k
        for j in range(PARTS):

            @pl.when(part == j)
            def _():
                spot = pl.ds(qw * j, qw)
                h = j // 2
                values = [
                    wq[:, spot],
                    tall[:, kw * h : kw * h + kw],
                    tall[:, kw * (h + 2) : kw * (h + 3)],
                    wo[:, spot],
                    tall[:, 4 * kw : 4 * kw + 2],
                ]
                outs[k][...] = joined(values, width)


def pack_attn(z, wq, wk, wv, wo, gain_one, gain_two, width):
    depth = wq.shape[0]
    return call(
        pack_attn_body, [shape((depth, width))] * PARTS, [SM] + [VM] * 6, [VM] * PARTS
    )(z, wq, wk.T, wv.T, wo, gain_one.reshape(1, -1), gain_two.reshape(1, -1))


def unpack_body(takes, z_ref, *refs):
    ins, outs = refs[:PARTS], refs[PARTS:]
    for ref, (start, step, share) in zip(outs, takes):
        if share == 2:
            ref[...] = jnp.zeros_like(ref)
    depth = ins[0].shape[0]
    for k in range(PARTS):
        part = z_ref[0] ^ k
        flat = None
        if any(share == 2 for start, step, share in takes):
            first = min(start for start, step, share in takes if share == 2)
            last = max(start + step for start, step, share in takes if share == 2)
            fill = jnp.zeros((depth, -(last - first) % 128), F32)
            flat = jnp.concatenate([ins[k][:, pl.ds(first, last - first)].astype(F32), fill], axis=1).T
        for j in range(PARTS):

            @pl.when(part == j)
            def _():
                for ref, (start, step, share) in zip(outs, takes):
                    spot = pl.ds(step * (j // share), step)
                    if share == 1:
                        ref[:, spot] = ins[k][:, pl.ds(start, step)].astype(F32)
                    else:
                        ref[spot, :] += flat[start - first : start - first + step]


def unpack(z, pieces, takes):
    depth = pieces[0].shape[0]
    dims = [(depth, step * PARTS // share) for start, step, share in takes]
    dims = [d[::-1] if take[2] == 2 else d for d, take in zip(dims, takes)]
    return call(
        functools.partial(unpack_body, takes),
        [shape(d, F32) for d in dims],
        [SM] + [VM] * PARTS,
        [VM] * len(takes),
        cost=4,
    )(z, *pieces)


def spot_of(pos, k, j, inner, depth):
    return pl.ds(pl.multiple_of(((pos[1] ^ k) * inner + (pos[2] ^ j)) * depth, 16), depth)


def piece_copies(pos, inner, pieces, store, sem, i, lanes):
    half = inner // 2
    depth = store.shape[1] // (PARTS * inner)
    copies = []
    for k in range(PARTS):
        for j in range(inner):
            piece = pieces[2 * k + j // half].at[pl.ds((j % half) * depth, depth), lanes]
            n = (i * PARTS + k) * inner + j
            copies.append(
                pltpu.make_async_copy(piece, store.at[i, spot_of(pos, k, j, inner, depth)], sem.at[n])
            )
    return copies


def fetch(pos, inner, pieces, store, sem, start=0):
    lanes = pl.ds(start, store.shape[2])
    copies = [piece_copies(pos, inner, pieces[8 * i : 8 * i + 8], store, sem, i, lanes) for i in range(2)]
    return start_all(copies)


def start_all(copies):
    for half in copies:
        for c in half:
            c.start()

    def wait(i):
        for c in copies[i]:
            c.wait()

    return wait


def own_rows_body(pos, ids, x_ref, t_ref, x_out, t_out, tall):
    spot = pl.ds(pl.multiple_of(pos[0], 64), 64)
    width = x_ref.shape[1]
    tall[...] = jnp.broadcast_to(ids[...].astype(F32), tall.shape[::-1]).T
    x_out[:, :width] = x_ref[spot, :]
    x_out[:, width:] = tall[spot, :].astype(BF)
    t_out[...] = t_ref[spot, :]


def own_rows(pos, ids, x, t):
    rows, width = x.shape
    return call(
        own_rows_body,
        [shape((64, width + 128)), shape((64, width))],
        [SM] + [VM] * 3,
        [VM] * 2,
        [pltpu.VMEM((rows, 128), F32)],
    )(pos, ids, x, t)


def join_rows(pieces, out):
    n = pieces[0].shape[0]
    for i, ref in enumerate(pieces):
        out[pl.ds(i * n, n), :] = ref[:, : out.shape[1]]


def first_sum_body(mine, got, three):
    three[...] = (mine[...].astype(F32) + got[...].astype(F32)).astype(BF)


def first_sum(mine, got):
    return call(first_sum_body, shape(mine.shape), [VM] * 2, VM)(mine, got)


def second_sum_body(mine_one, mine_two, got, three, one, two):
    n = one.shape[0]
    one[...] = (mine_one[...].astype(F32) + got[pl.ds(n, n), :].astype(F32)).astype(BF)
    value = mine_two[...].astype(F32) + got[pl.ds(2 * n, n), :].astype(F32)
    two[...] = (value + three[...].astype(F32)).astype(BF)


def second_sum(mine, got, three):
    return call(second_sum_body, [shape(three.shape)] * 2, [VM] * 4, [VM] * 2)(
        mine[1], mine[2], got, three
    )


def last_sum(mine, got, one, two):
    first = mine[...].astype(F32) + got[pl.ds(0, mine.shape[0]), :].astype(F32)
    return first + one[...].astype(F32) + two[...].astype(F32)


def mean_scale(value):
    return lax.rsqrt(jnp.mean(value * value, axis=-1, keepdims=True) + EPS)


def back_norm(grad, value, gain):
    scale = mean_scale(value)
    unit = value * scale
    scaled = grad * gain
    return unit, scale * (scaled - unit * jnp.mean(scaled * unit, axis=-1, keepdims=True))


def after_attn_body(mine, got, one, two, x_own, gain, middle, n_own, total):
    branch = last_sum(mine, got, one, two)
    value = x_own[:, : branch.shape[1]].astype(F32) + branch
    middle[...] = value
    n_own[...] = (value * mean_scale(value) * gain[1:2, :]).astype(BF)
    total[...] = jnp.full(total.shape, jnp.sum(branch * branch), F32)


def after_mlp_body(mine, got, one, two, middle, target, d_own, out, total):
    branch = last_sum(mine, got, one, two)
    stream = middle[...] + branch
    d_own[...] = (stream - target[...].astype(F32)).astype(BF)
    out[...] = stream.astype(BF)
    total[0:8, :] = jnp.full((8, 128), jnp.sum(stream * stream), F32)
    total[8:16, :] = jnp.full((8, 128), jnp.sum(branch * branch), F32)


def after_feed_back_body(mine, got, one, two, middle, d_own, gain, d_middle, a_own, gain_grad):
    grad = last_sum(mine, got, one, two)
    unit, back = back_norm(grad, middle[...], gain[1:2, :])
    value = d_own[...].astype(F32) + back
    d_middle[...] = value
    a_own[...] = value.astype(BF)
    gain_grad[...] = jnp.sum(grad * unit, axis=0, keepdims=True)


def after_all_body(mine, got, one, two, x_own, d_middle, gain, out):
    grad = last_sum(mine, got, one, two)
    unit, back = back_norm(grad, x_own[:, : grad.shape[1]].astype(F32), gain[0:1, :])
    out[...] = (d_middle[...] + back).astype(BF)


def spread_rows_body(spots, p0, p1, p2, p3, out):
    n = p0.shape[0]
    for i, ref in enumerate((p0, p1, p2, p3)):
        out[pl.ds(pl.multiple_of(spots[i], 64), n), :] = ref[...]


def spread_rows(spots, pieces):
    n, width = pieces[0].shape
    return call(spread_rows_body, shape((4 * n, width)), [SM] + [VM] * 4, VM)(spots, *pieces)


def rotated(value, cosine, sine):
    half = HEAD_DIM // 2
    a, b = value[:, :half], value[:, half:]
    return jnp.concatenate([a * cosine - b * sine, b * cosine + a * sine], axis=1)


def project_body(qw, inner, pos, cosine, sine, *refs):
    x, w = refs[:8], refs[8:24]
    first, q_ref, kv_ref, gains, row_ids = refs[24:29]
    store, sem = refs[29:]
    wait = fetch(pos, inner, w, store, sem)
    width = first.shape[1]
    step = width // 4
    ids = jnp.concatenate([ref[:, width:] for ref in x], axis=0).astype(F32)
    row_ids[...] = ids.T[0:8, :]
    wait(0)
    spot = 480 - 384
    for p in range(4):
        tail = store[0, pl.ds(p * step, step), 384:512].astype(F32).T
        gains[:, pl.ds(p * step, step)] = tail[spot : spot + 8]
    gain = gains[0:1, :]
    rows = x[0].shape[0]
    for i, ref in enumerate(x):
        value = ref[:, :width].astype(F32)
        first[pl.ds(i * rows, rows), :] = (value * mean_scale(value) * gain).astype(BF)
    cos, sin = cosine[...], sine[...]
    queries, keys, values = [], [], []
    for i in range(2):
        if i:
            wait(1)
        out = dot(first[...], store[i, :, :384])
        for start in range(0, qw, HEAD_DIM):
            queries.append(rotated(out[:, start : start + HEAD_DIM], cos, sin))
        keys.append(rotated(out[:, qw : qw + HEAD_DIM], cos, sin))
        values.append(out[:, qw + HEAD_DIM : qw + 2 * HEAD_DIM])
    q_ref[...] = jnp.concatenate(queries, axis=1).astype(BF)
    kv_ref[...] = jnp.concatenate(keys + values + [ids[:, :64]], axis=1).astype(BF)


def sems(inner):
    return pltpu.SemaphoreType.DMA((2 * PARTS * inner,))


def project(pos, x, cosine, sine, w, qw, inner):
    rows, width = x[0].shape
    rows *= 8
    width -= 128
    return call(
        functools.partial(project_body, qw, inner),
        [
            shape((rows, width)),
            shape((rows, 2 * qw)),
            shape((rows, 384)),
            shape((8, width), F32),
            shape((8, rows), F32),
        ],
        [SM] + [VM] * 10 + [ANY] * 16,
        [VM] * 5,
        [pltpu.VMEM((2, width, 512), BF), sems(inner)],
        cost=12,
    )(pos, cosine, sine, *x, *w)


def out_rows(partial, outs):
    n = outs[0].shape[0]
    spots = [(i * n, n) for i in range(4)] + [(7 * n, n), (4 * n, 3 * n)]
    for (start, size), ref in zip(spots, outs):
        ref[...] = partial[start : start + size].astype(ref.dtype)


def row_shapes(rows, width):
    return [shape((rows, width))] * 5 + [shape((3 * rows, width))]


def each(count, step, start):
    if count <= 2:
        for s in range(count):
            start = step(s, start)
        return start
    return lax.fori_loop(0, count, step, start)


def reader(kvs, rows):
    def read(s, lane):
        if len(kvs) > 1:
            return kvs[s][:, lane]
        return kvs[0][pl.ds(pl.multiple_of(s * rows, rows), rows), lane]

    return read


def lanes(i):
    return pl.ds(i * HEAD_DIM, HEAD_DIM)


ID_LANE = pl.ds(4 * HEAD_DIM, 1)


def attend_body(sides, pos, q_ref, row_ids, *refs):
    arrays = sides if sides <= 2 else 1
    kvs, refs = refs[:arrays], refs[arrays:]
    w = refs[:16]
    mixed = refs[16:18]
    lse, sides_out = refs[18], refs[19:25]
    store, sem = refs[25:]
    wait = fetch(pos, sides, w, store, sem, 256)
    rows = q_ref.shape[0]
    qw = q_ref.shape[1] // 2
    ids = row_ids[0:1, :]
    read = reader(kvs, rows)

    def look(s):
        return read(s, ID_LANE).astype(F32) <= ids

    looks = [look(s) for s in range(sides)] if sides <= 2 else None
    lse[...] = jnp.zeros_like(lse)
    head = 0
    c = FACTOR * LOG2E
    for i in range(2):
        outs = []
        for start in range(i * qw, (i + 1) * qw, HEAD_DIM):
            q = q_ref[:, start : start + HEAD_DIM]

            def score(s):
                seen = looks[s] if looks else look(s)
                return jnp.where(seen, dot(read(s, lanes(i)), q, LAST), -1e30)

            scores = [score(s) for s in range(sides)] if sides <= 2 else None

            def highest(s, top):
                value = scores[s] if scores else score(s)
                return jnp.maximum(top, jnp.max(value, axis=0, keepdims=True))

            top = each(sides, highest, jnp.full((1, rows), -1e30, F32))

            def gathered(s, carry):
                total, out = carry
                value = scores[s] if scores else score(s)
                p = jnp.exp2(value * c - top * c)
                total = total + jnp.sum(p, axis=0, keepdims=True)
                return total, out + dot(read(s, lanes(2 + i)), p.astype(BF), ROWS)

            nothing = (jnp.zeros((1, rows), F32), jnp.zeros((HEAD_DIM, rows), F32))
            total, out = each(sides, gathered, nothing)
            outs.append(out / total)
            lse[head : head + 1, :] = top * c + jnp.log2(total)
            head += 1
        fill = jnp.zeros((512 - 320 - qw, rows), F32)
        tall = jnp.concatenate([jnp.zeros((64, rows), F32)] + outs + [fill], axis=0)
        mixed[i][...] = tall.T.astype(BF)
    for i in range(2):
        wait(i)
    partial = dot(mixed[0][...], store[0], LAST) + dot(mixed[1][...], store[1], LAST)
    out_rows(partial, sides_out)


def attend(pos, q, kvs, row_ids, w, sides):
    rows = q.shape[0]
    width = 8 * w[0].shape[0]
    return call(
        functools.partial(attend_body, sides),
        [shape((rows, 256))] * 2
        + [shape((8, rows), F32)]
        + row_shapes(rows // 8, width),
        [SM] + [VM] * (2 + len(kvs)) + [ANY] * 16,
        [VM] * 9,
        [pltpu.VMEM((2, width, 256), BF), sems(sides)],
        cost=12,
    )(pos, q, row_ids, *kvs, *w)


def padded(value, width):
    return jnp.concatenate([value, jnp.zeros((value.shape[0], width - value.shape[1]), value.dtype)], axis=1)


def block_copies(pos, inner, arrays, store, sem, i):
    depth = arrays[1].shape[1]
    half = inner // 2
    cut = arrays[2].shape[1]
    copies = [[], []]
    for k in range(PARTS):
        for j in range(inner):
            n = (i * PARTS + k) * inner + j
            if k < 3:
                row = pl.ds(pl.multiple_of(((pos[1] ^ k) * inner + j) * depth, 16), depth)
                for late in range(2):
                    lane = pl.ds(cut, store.shape[2] - cut) if late else pl.ds(0, cut)
                    spot = arrays[k // 2].at[j * 2 + (pos[3] ^ i), pl.ds(depth if k == 1 else 0, depth), lane]
                    to = store.at[i, row, lane]
                    copies[late].append(pltpu.make_async_copy(spot, to, sem.at[late, n]))
                continue
            for late in range(2):
                piece = arrays[2 + 4 * late + 2 * i + j // half]
                lane = pl.ds(cut * late, piece.shape[1])
                to = store.at[i, spot_of(pos, k, j, inner, depth), lane]
                spot = piece.at[pl.ds((j % half) * depth, depth)]
                copies[late].append(pltpu.make_async_copy(spot, to, sem.at[late, n]))
    return copies


def feed_body(fw, inner, pos, *refs):
    n, blocks = refs[:8], refs[8:18]
    hidden, slope, silu = refs[18:20], refs[20:22], refs[22:24]
    rows_out, outs = refs[24], refs[25:31]
    rows_in, kept, store, sem, out_sem = refs[31:]
    copies = [block_copies(pos, inner, blocks, store, sem, i) for i in range(2)]
    wait = start_all([copies[0][0], copies[1][0], copies[0][1] + copies[1][1]])
    join_rows(n, rows_in)
    saves = [pltpu.make_async_copy(rows_in, rows_out, out_sem.at[6])]
    saves[0].start()
    for i in range(2):
        wait(i)
        out = dot(rows_in[...], store[i, :, : 2 * fw])
        gate, upper = out[:, :fw], out[:, fw:]
        sigma = jax.nn.sigmoid(gate)
        act = gate * sigma
        values = (act * upper, upper * (sigma + act * (1.0 - sigma)), act)
        for n, (value, to) in enumerate(zip(values, (hidden, slope, silu))):
            kept[2 * n + i] = padded(value, 512).astype(BF)
            saves.append(pltpu.make_async_copy(kept.at[2 * n + i], to[i], out_sem.at[2 * n + i]))
            saves[-1].start()
    wait(2)
    out_rows(
        dot(kept[0], store[0, :, 2 * fw :], LAST) + dot(kept[1], store[1, :, 2 * fw :], LAST),
        outs,
    )
    for c in saves:
        c.wait()


def feed(pos, n, w, fw, inner):
    rows, width = n[0].shape
    return call(
        functools.partial(feed_body, fw, inner),
        [shape((8 * rows, 512))] * 6 + [shape((8 * rows, width))] + row_shapes(rows, width),
        [SM] + [VM] * 8 + [ANY] * 10,
        [ANY] * 7 + [VM] * 6,
        [
            pltpu.VMEM((8 * rows, width), BF),
            pltpu.VMEM((6, 8 * rows, 512), BF),
            pltpu.VMEM((2, width, 2 * fw + 512), BF),
            pltpu.SemaphoreType.DMA((2, 2 * PARTS * inner)),
            pltpu.SemaphoreType.DMA((7,)),
        ],
        cost=18,
    )(pos, *n, *w)


def feed_back_body(fw, inner, pos, rows_in, *refs):
    slope, silu = refs[0:2], refs[2:4]
    blocks = refs[4:14]
    d_gu, outs = refs[14:16], refs[16:22]
    kept, store, sem, out_sem = refs[22:]
    copies = [block_copies(pos, inner, blocks, store, sem, i) for i in range(2)]
    wait = start_all([copies[0][1], copies[1][1], copies[0][0] + copies[1][0]])
    saves = []
    for i in range(2):
        wait(i)
        out = dot(rows_in[...], store[i, :, 2 * fw :])
        a = (out * slope[i][...].astype(F32))[:, :fw]
        b = (out * silu[i][...].astype(F32))[:, :fw]
        kept[i] = jnp.concatenate([a, b], axis=1).astype(BF)
        saves.append(pltpu.make_async_copy(kept.at[i], d_gu[i], out_sem.at[i]))
        saves[-1].start()
    wait(2)
    out_rows(
        dot(kept[0], store[0, :, : 2 * fw], LAST) + dot(kept[1], store[1, :, : 2 * fw], LAST),
        outs,
    )
    for c in saves:
        c.wait()


def feed_back(pos, d, slope, silu, w, fw, inner):
    rows, width = d.shape
    return call(
        functools.partial(feed_back_body, fw, inner),
        [shape((rows, 2 * fw))] * 2 + row_shapes(rows // 8, width),
        [SM] + [VM] * 5 + [ANY] * 10,
        [ANY] * 2 + [VM] * 6,
        [
            pltpu.VMEM((2, rows, 2 * fw), BF),
            pltpu.VMEM((2, width, 2 * fw + 512), BF),
            pltpu.SemaphoreType.DMA((2, 2 * PARTS * inner)),
            pltpu.SemaphoreType.DMA((2,)),
        ],
        cost=16,
    )(pos, d, *slope, *silu, *w)


def features(pos, k, step):
    return pl.ds(pl.multiple_of((pos[1] ^ k) * step, 128), step)


def block_grad_body(inner, parts, pos, left, right_a, right_b, out, store, sem):
    step = store.shape[1] // len(parts)
    depth = step // inner
    copies = []
    for p, k in enumerate(parts):
        spot = features(pos, k, step)
        for i, right in enumerate((right_a, right_b)):
            store[i, pl.ds(p * step, step), :] = dot(left[:, spot], right[...], ROWS).astype(BF)
            for j in range(inner):
                n = p * inner + j
                copies.append(
                    pltpu.make_async_copy(
                        store.at[i, pl.ds(n * depth, depth)],
                        out.at[j * 2 + (pos[3] ^ i), pl.ds(p * depth, depth)],
                        sem.at[i * len(parts) * inner + n],
                    )
                )
                copies[-1].start()
    for c in copies:
        c.wait()


def down_grad_body(inner, pos, *refs):
    pieces, right, out, rows_in, store, sem = refs[:8], refs[8:10], *refs[10:]
    join_rows(pieces, rows_in)
    block_grad_body(inner, range(PARTS), pos, rows_in, *right, out, store, sem)


def down_grad(pos, pieces, right, inner):
    rows, width = pieces[0].shape
    rows *= 8
    cols = right[0].shape[1]
    return call(
        functools.partial(down_grad_body, inner),
        [shape((inner * 2, width // inner, cols)), shape((rows, width))],
        [SM] + [VM] * 10,
        [ANY, VM],
        [pltpu.VMEM((2, width, cols), BF), sems(inner)],
        cost=7,
    )(pos, *pieces, *right)


def block_grad(pos, left, right, inner, parts):
    rows, width = left.shape
    cols = right[0].shape[1]
    held = width // PARTS * len(parts)
    return call(
        functools.partial(block_grad_body, inner, parts),
        shape((inner * 2, held // inner, cols)),
        [SM] + [VM] * 3,
        ANY,
        [pltpu.VMEM((2, held, cols), BF), sems(inner)],
        cost=7,
    )(pos, left, *right)


def attend_back_body(sides, pos, q_ref, row_ids, lse, cosine, sine, *refs):
    arrays = sides if sides <= 2 else 1
    d, refs = refs[:8], refs[8:]
    kvs, refs = refs[:arrays], refs[arrays:]
    w = refs[:16]
    dq_ref, own_ref, send_ref, rows_in = refs[16:20]
    store, mix, d_kv, sem = refs[20:]
    join_rows(d, rows_in)
    wait = fetch(pos, sides, w, store, sem, 256)
    rows = q_ref.shape[0]
    qw = q_ref.shape[1] // 2
    for i in range(2):
        wait(i)
        mix[i] = dot(rows_in[...], store[i])[:, 64 : 64 + qw].astype(BF)
    ids = row_ids[0:1, :]
    read = reader(kvs, rows)

    def look(s):
        return read(s, ID_LANE).astype(F32) <= ids

    looks = [look(s) for s in range(sides)] if sides <= 2 else None
    d_q = []
    c = FACTOR * LOG2E
    head = 0
    for i in range(2):
        for start in range(0, qw, HEAD_DIM):
            q = q_ref[:, i * qw + start : i * qw + start + HEAD_DIM]
            dm = mix[i, :, start : start + HEAD_DIM]
            level = lse[head : head + 1, :]
            head += 1

            def pair(s):
                seen = looks[s] if looks else look(s)
                p = jnp.where(seen, jnp.exp2(dot(read(s, lanes(i)), q, LAST) * c - level), 0.0)
                return p, dot(read(s, lanes(2 + i)), dm, LAST)

            held = [pair(s) for s in range(sides)] if sides <= 2 else None

            def weigh(s, delta):
                p, dp = held[s] if held else pair(s)
                return delta + jnp.sum(p * dp, axis=0, keepdims=True)

            delta = each(sides, weigh, jnp.zeros((1, rows), F32))

            def grads(s, out):
                p, dp = held[s] if held else pair(s)
                ds = (p * (dp - delta)).astype(BF)
                d_value = dot(p.astype(BF), dm)
                d_key = dot(ds, q)
                if start == 0:
                    d_kv[2 + i, s] = d_value
                    d_kv[i, s] = d_key
                else:
                    d_kv[2 + i, s] += d_value
                    d_kv[i, s] += d_key
                return out + dot(read(s, lanes(i)), ds, ROWS)

            d_q.append(each(sides, grads, jnp.zeros((HEAD_DIM, rows), F32)))
    tall = jnp.concatenate(d_q + [jnp.zeros((512 - 4 * HEAD_DIM, rows), F32)], axis=0).T * FACTOR
    cos, sin = cosine[...], sine[...]
    dq_ref[...] = jnp.concatenate(
        [rotated(tall[:, h * HEAD_DIM : (h + 1) * HEAD_DIM], cos, -sin) for h in range(4)], axis=1
    ).astype(BF)
    for s in range(sides):
        value = jnp.concatenate([d_kv[0, s] * FACTOR, d_kv[1, s] * FACTOR, d_kv[2, s], d_kv[3, s]], axis=1)
        if s == 0:
            own_ref[...] = value
        else:
            send_ref[pl.ds((s - 1) * rows, rows), :] = value.astype(BF)


def attend_back(pos, d, q, kvs, row_ids, lse, cosine, sine, w, sides):
    rows = q.shape[0]
    width = d[0].shape[1]
    cols = 4 * HEAD_DIM
    return call(
        functools.partial(attend_back_body, sides),
        [shape(q.shape), shape((rows, cols), F32), shape(((sides - 1) * rows, cols)), shape((rows, width))],
        [SM] + [VM] * (13 + len(kvs)) + [ANY] * 16,
        [VM] * 4,
        [
            pltpu.VMEM((2, width, 256), BF),
            pltpu.VMEM((2, rows, q.shape[1] // 2), BF),
            pltpu.VMEM((4, sides, rows, HEAD_DIM), F32),
            sems(sides),
        ],
        cost=18,
    )(pos, q, row_ids, lse, cosine, sine, *d, *kvs, *w)


def split_body(dq_ref, own_ref, got_ref, cosine, sine, *d_qkv):
    qw = dq_ref.shape[1] // 2
    cos, sin = cosine[...], sine[...]
    d_kv = own_ref[...] + got_ref[...].astype(F32)
    d_q = dq_ref[...].astype(F32)
    for i in range(2):
        d_k = rotated(d_kv[:, i * HEAD_DIM : (i + 1) * HEAD_DIM], cos, -sin)
        d_v = d_kv[:, (2 + i) * HEAD_DIM : (3 + i) * HEAD_DIM]
        d_qkv[i][...] = padded(
            jnp.concatenate([d_q[:, i * qw : (i + 1) * qw], d_k, d_v], axis=1), 384
        ).astype(BF)


def split_grads(dq, own, got, cosine, sine):
    rows = dq.shape[0]
    return call(split_body, [shape((rows, 384))] * 2, [VM] * 5, [VM] * 2)(dq, own, got, cosine, sine)


def project_back_body(inner, pos, d_a, d_b, *refs):
    w, outs = refs[:16], refs[16:22]
    store, sem = refs[22:]
    wait = fetch(pos, inner, w, store, sem)
    for i in range(2):
        wait(i)
    out_rows(dot(d_a[...], store[0], LAST) + dot(d_b[...], store[1], LAST), outs)


def project_back(pos, d_qkv, w, inner):
    rows = d_qkv[0].shape[0] // 8
    width = 8 * w[0].shape[0]
    return call(
        functools.partial(project_back_body, inner),
        row_shapes(rows, width),
        [SM] + [VM] * 2 + [ANY] * 16,
        [VM] * 6,
        [pltpu.VMEM((2, width, 384), BF), sems(inner)],
        cost=8,
    )(pos, *d_qkv, *w)


def pair_copies(pos, inner, far, near, store, sem, i):
    half = inner // 2
    depth = store.shape[1] // (PARTS * inner)
    copies = []
    for k in range(PARTS):
        for j in range(inner):
            if k >= 2:
                to = far[j // half].at[pl.ds(((k % 2) * half + j % half) * depth, depth)]
            else:
                to = near.at[(pos[2] ^ j) * 2 + (pos[3] ^ i), pl.ds(k * depth, depth)]
            n = (i * PARTS + k) * inner + j
            copies.append(
                pltpu.make_async_copy(store.at[i, spot_of(pos, k, j, inner, depth)], to, sem.at[n])
            )
    return copies


def attn_grad_body(inner, pos, first, d_all, gain_two, sum_attn, sums, *refs):
    d_qkv, mixed = refs[:2], refs[2:4]
    w, outs, near = refs[4:20], refs[20:24], refs[24]
    held, store, sem, out_sem = refs[25:]
    wait = fetch(pos, inner, w, held, sem)
    step = store.shape[1] // PARTS
    copies = [pair_copies(pos, inner, outs[2 * i : 2 * i + 2], near, store, out_sem, i) for i in range(2)]
    lane = lax.broadcasted_iota(jnp.int32, (1, 128), 1)
    tail = jnp.where(lane == 98, sums[0:1, :], 0.0)
    tail = jnp.where(lane == 99, sum_attn[0:1, :], tail)
    tail = jnp.where(lane == 100, sums[8:9, :], tail)
    for k in (3, 2, 1, 0):
        spot = features(pos, k, step)
        rows = [jnp.zeros((97, step), F32), gain_two[0:1, spot], jnp.zeros((30, step), F32)]
        tall = jnp.concatenate(rows, axis=0).T + tail
        values = [dot(first[:, spot], d_qkv[i][...], ROWS) for i in range(2)]
        others = [dot(d_all[:, spot], mixed[i][...], ROWS) for i in range(2)]
        if k == 3:
            wait(0)
            wait(1)
        gain = 0.0
        for i in range(2):
            gain = gain + jnp.sum(values[i] * held[i, spot, :384].astype(F32), axis=1, keepdims=True)
        gain = gain / held[0, spot, 480:481].astype(F32)
        tall = tall + jnp.where(lane == 96, gain, 0.0)
        for i in range(2):
            store[i, spot, :256] = values[i][:, :256].astype(BF)
            store[i, spot, 256:384] = (values[i][:, 256:] + others[i][:, :128]).astype(BF)
            store[i, spot, 384:] = (others[i][:, 128:] + tall).astype(BF)
            for c in copies[i][k * inner : (k + 1) * inner]:
                c.start()
    for i in range(2):
        for c in copies[i]:
            c.wait()


def attn_grad(pos, first, d_all, gain_two, sum_attn, sums, d_qkv, mixed, w, inner):
    rows, width = first.shape
    return call(
        functools.partial(attn_grad_body, inner),
        [shape((width // 4, 512))] * 4 + [shape((inner * 2, width // (2 * inner), 512))],
        [SM] + [VM] * 9 + [ANY] * 16,
        [ANY] * 5,
        [pltpu.VMEM((2, width, 512), BF), pltpu.VMEM((2, width, 512), BF), sems(inner), sems(inner)],
        cost=12,
    )(pos, first, d_all, gain_two, sum_attn, sums, *d_qkv, *mixed, *w)


def hold(values, *others):
    got = lax.optimization_barrier(tuple(values) + tuple(others))
    return list(got[: len(values)])


class Live:
    def fence(self):
        names = sorted(self.__dict__)
        leaves, tree = jax.tree.flatten([self.__dict__[n] for n in names])
        leaves = lax.optimization_barrier(tuple(leaves))
        self.__dict__.update(zip(names, jax.tree.unflatten(tree, leaves)))


class Place:
    def __init__(self):
        self.inner = lax.axis_size("y")
        self.count = PARTS * self.inner
        self.z, self.y, self.x, self.c = [lax.axis_index(name) for name in AXES]
        self.s = self.z * self.inner + self.y
        self.zs = self.z.reshape(1).astype(jnp.int32)
        self.bits = []
        b = 1
        while b < self.inner:
            self.bits.append(b)
            b *= 2

    def hop_z(self, v, k):
        return hop(v, "z", k)

    def hop_y(self, v, b):
        return hop(v, "y", b)

    def hop_x(self, v):
        return hop(v, "x", 1)

    def hop_c(self, v):
        return hop(v, "c", 1)

    def low_y(self, v):
        for b in self.bits[:-1]:
            v = jnp.concatenate([v, self.hop_y(v, b)], 0)
        return v

    def far_y(self, v):
        return self.hop_y(v, self.bits[-1])

    def add(self, own, got):
        return (own.astype(F32) + got.astype(F32)).astype(BF)

    def halves(self, own, got):
        n = own.shape[0] // 2
        return [self.add(own[:n], got[:n]), self.add(own[n:], got[n:])]

    def sum_y(self, own, far):
        value = self.add(own, self.far_y(far))
        for b in reversed(self.bits[:-1]):
            n = value.shape[0] // 2
            value = self.add(value[:n], self.hop_y(value[n:], b))
        return value

    def sum_x(self, own, other):
        return self.add(own, self.hop_x(other))

    def gather(self, own):
        mine = [own, self.hop_z(own, 1), self.hop_z(own, 2)]
        mine.append(self.hop_z(mine[2], 1))
        return mine + [self.hop_c(v) for v in mine]

    def scatter_one(self, outs):
        mine = list(outs[:4])
        last, rest = [self.hop_c(v) for v in outs[4:]]
        one, two = second_sum(mine, rest, self.hop_z(first_sum(mine[3], last), 1))
        return [mine[0], rest, one, two]

    def scatter_two(self, left):
        return left[0], left[1], self.hop_z(left[2], 1), self.hop_z(left[3], 2)

    def scatter(self, outs):
        return self.scatter_two(self.scatter_one(outs))


def tables(place):
    half = HEAD_DIM // 2
    freq = THETA ** (-(jnp.arange(half, dtype=F32) * 2.0 / HEAD_DIM))
    angle = place[:, None] * freq[None, :]
    return (jnp.cos(angle), jnp.sin(angle))


def on_device(
    inputs,
    targets,
    seq_ids,
    block_ids,
    attn_gain,
    mlp_gain,
    w_query,
    w_key,
    w_value,
    w_out,
    w_gate,
    w_up,
    w_down,
):
    at = Place()
    inner = at.inner
    full = inputs.shape[1]
    half_span = SPAN // 2
    kw = w_key.shape[1] // 2
    qw = w_query.shape[1] // PARTS
    fw = w_gate.shape[1] // PARTS
    row_f32 = shape((half_span, full), F32)
    row_bf = shape((half_span, full))

    off = jnp.where(seq_ids[0] == at.x, 0, SPAN)
    pos = jnp.stack([off + at.c * half_span, at.z, at.y, at.x, at.c]).astype(jnp.int32)
    spots = [
        (off if xr == 0 else SPAN - off) + (at.c ^ cr) * half_span for xr in range(2) for cr in range(2)
    ]
    spots = jnp.stack(spots).astype(jnp.int32)

    def all_rows(own):
        across = at.hop_x(own)
        return [own, at.hop_c(own), across, at.hop_c(across)]

    rows = 2 * PARTS * half_span
    count = jnp.arange(rows, dtype=jnp.int32)
    zz = at.z ^ ((count // half_span) % PARTS)
    cc = at.c ^ (count // (half_span * PARTS))
    place = ((zz * inner + at.y) * SPAN + cc * half_span + count % half_span).astype(F32)
    cosine, sine = tables(place)

    def listed(w):
        return [v for i in range(2) for k in range(PARTS) for v in w[k][i]]

    def gather_blocks(pair):
        return lax.all_gather(pair, ("y", "x"), axis=0)

    def scatter_blocks(blocks, count):
        blocks = blocks.reshape(-1, blocks.shape[-1])
        got = lax.psum_scatter(blocks, ("y", "x"), scatter_dimension=0, tiled=True)
        n = got.shape[0] // count
        return [got[k * n : (k + 1) * n] for k in range(count)]

    hop_x, hop_z, low_y, far_y = at.hop_x, at.hop_z, at.low_y, at.far_y
    live = Live()
    live.w = [w_gate, w_up, w_down]
    live.rows = [inputs, targets]
    live.qo = pack_attn(at.zs, w_query, w_key, w_value, w_out, attn_gain, mlp_gain, 512)
    live.fence()

    q = live.qo
    z = [q[0]] + [hop_z(q[k], k) for k in range(1, PARTS)]
    live.x_own, live.t_own = own_rows(pos, block_ids.reshape(1, -1), *live.rows)
    live.g = list(pack(at.zs, live.w, [(fw, 1)] * 3, 2 * fw + 512, 2 * fw))
    del live.w, live.rows
    live.g[1] = hop_z(hold([live.g[1]], z[1])[0], 1)
    v = low_y(z[0])
    w = far_y(v)
    live.q0 = (v, w, hop_x(v))
    live.q1 = (low_y(z[1]), low_y(hop_x(z[1])))
    live.z = z[2:]
    live.fence()

    near = gather_blocks(jnp.concatenate(live.g[:2], 0))
    v, w, u = live.q0
    q0 = ((v, w), (u, hop_x(w)))
    v, u = live.q1
    q1 = ((v, far_y(v)), (u, far_y(u)))
    v = low_y(live.z[0])
    w = far_y(v)
    q2 = ((v, w), (hop_x(v), hop_x(w)))
    u, v = low_y(hop_x(live.z[1])), low_y(live.z[1])
    q3 = ((v, far_y(v)), (u, far_y(u)))
    live.x_all = at.gather(live.x_own)
    live.w_qo = listed([q0, q1, q2, q3])
    live.g[2] = hop_z(live.g[2], 2)
    del live.z, live.q0, live.q1
    live.fence()

    live.first, live.query, kv, live.gain, live.row_ids = project(
        pos, live.x_all, cosine, sine, live.w_qo, qw, inner
    )
    live.kvs = [kv]
    live.g[4] = hop_z(live.g[4], 2)
    live.fence()

    g2 = gather_blocks(jnp.concatenate([live.g[2], live.g[4]], 1))

    kvs = live.kvs
    for b in at.bits:
        kvs = kvs + [at.hop_y(v, b) for v in kvs]
    if inner > 2:
        kvs = [jnp.concatenate(kvs, 0)]
    live.kvs = kvs
    mixed_a, mixed_b, live.lse, *live.outs = attend(
        pos, live.query, kvs, live.row_ids, live.w_qo, inner
    )
    live.mixed = (mixed_a, mixed_b)
    live.g[3] = hop_z(live.g[3], 3)
    live.w_near = near
    live.fence()

    live.left = at.scatter_one(live.outs)
    live.g[5] = hop_z(live.g[5], 3)
    v = low_y(live.g[3])
    live.g3 = (v, far_y(v), low_y(hop_x(live.g[3])))
    del live.outs
    live.fence()

    v, w, u = live.g3
    live.g3 = [v, w, u, far_y(u)]
    v = low_y(live.g[5])
    w = far_y(v)
    live.g3 += [v, w, hop_x(v), hop_x(w)]
    del live.g
    live.middle, n_own, live.sum_attn = call(
        after_attn_body,
        [row_f32, row_bf, shape((8, 128), F32)],
        [VM] * 6,
        [VM] * 3,
    )(*at.scatter_two(live.left), live.x_own, live.gain)
    live.n_all = at.gather(n_own)
    live.w_two = g2
    del live.left
    live.fence()

    live.w_ff = [live.w_near, live.w_two, *live.g3]
    del live.w_near, live.w_two, live.g3
    out = feed(pos, live.n_all, live.w_ff, fw, inner)
    live.hidden, live.slope, live.silu = out[:2], out[2:4], out[4:6]
    live.n_all, outs = out[6], out[7:]
    live.d_own, live.layer_own, live.sums = call(
        after_mlp_body,
        [row_bf, row_bf, shape((16, 128), F32)],
        [VM] * 6,
        [VM] * 3,
    )(*at.scatter(outs), live.middle, live.t_own)
    del live.t_own
    live.fence()

    live.d_rows = at.gather(live.d_own)
    live.layer_out = all_rows(live.layer_own)
    del live.layer_own
    live.fence()


    live.grad_d, live.d_rows = down_grad(pos, live.d_rows, live.hidden, inner)
    live.fence()

    d = scatter_blocks(live.grad_d, 4)
    out = feed_back(pos, live.d_rows, live.slope, live.silu, live.w_ff, fw, inner)
    live.d_gu, live.outs = out[:2], out[2:]
    del live.slope, live.silu, live.w_ff, live.d_rows, live.hidden, live.grad_d
    live.fence()

    live.left = at.scatter_one(live.outs)
    del live.outs
    live.far = block_grad(pos, live.n_all, live.d_gu, inner, (2, 3))
    live.fence()

    far = scatter_blocks(live.far, 2)
    live.d_middle, live.a_own, live.grad_gain_two = call(
        after_feed_back_body,
        [row_f32, row_bf, shape((1, full), F32)],
        [VM] * 7,
        [VM] * 3,
    )(*at.scatter_two(live.left), live.middle, live.d_own, live.gain)
    del live.middle, live.d_own, live.left, live.far
    live.near = block_grad(pos, live.n_all, live.d_gu, inner, (0, 1))
    del live.n_all, live.d_gu
    live.fence()

    near = scatter_blocks(live.near, 2)
    live.a_all = at.gather(live.a_own)
    del live.a_own, live.near
    live.fence()

    live.d_query, live.d_kv, live.sent, live.a_all = attend_back(
        pos, live.a_all, live.query, live.kvs, live.row_ids, live.lse, cosine, sine, live.w_qo, inner
    )
    del live.query, live.kvs, live.row_ids, live.lse
    live.d = [d[0], hop_z(d[1], 1), d[2], hop_z(d[3], 3)]
    live.fence()

    d_kv, sent = live.d_kv, live.sent
    if inner > 2:
        sent = jnp.concatenate([d_kv, sent.astype(F32)], 0)
        for b in reversed(at.bits[1:]):
            n = sent.shape[0] // 2
            sent = sent[:n] + at.hop_y(sent[n:].astype(BF), b).astype(F32)
        d_kv, sent = sent[:rows], sent[rows:].astype(BF)
    sent = at.hop_y(sent, at.bits[0])
    live.d_qkv = split_grads(live.d_query, d_kv, sent, cosine, sine)
    live.d[2] = hop_z(live.d[2], 2)
    del live.d_kv, live.sent, live.d_query
    live.fence()

    tails = (live.grad_gain_two, live.sum_attn, live.sums)
    q = attn_grad(pos, live.first, live.a_all, *tails, live.d_qkv, live.mixed, live.w_qo, inner)
    live.q_far, live.q_near = (q[0:2], q[2:4]), q[4]
    live.far3 = hop_z(far[1], 3)
    del live.first, live.a_all, live.mixed
    del live.grad_gain_two, live.sum_attn, live.sums
    live.fence()

    live.left = at.scatter_one(project_back(pos, live.d_qkv, live.w_qo, inner))
    del live.d_qkv, live.w_qo
    q_near, q_far = scatter_blocks(live.q_near, 2), live.q_far
    del live.q_near, live.q_far
    (a, b), (c, d) = q_far
    q_far, last = at.sum_x(a, c), at.sum_x(b, d)
    if inner == 2:
        q_far = at.halves(q_far, at.far_y(last))
    else:
        q_far = jnp.split(at.sum_y(q_far, last), 2)
    far2 = hop_z(far[0], 2)
    live.fence()

    (live.input_own,) = call(
        after_all_body,
        [row_bf],
        [VM] * 7,
        [VM],
    )(*at.scatter_two(live.left), live.x_own, live.d_middle, live.gain)
    del live.left, live.x_own, live.d_middle
    live.q_far, live.far2 = q_far, far2
    (live.g_down,) = unpack(at.zs, live.d, [(0, fw, 1)])
    live.layer_out = spread_rows(spots, live.layer_out)
    del live.d
    live.fence()

    near_own, near_one = hold(near, live.input_own)
    live.g = [near_own, hop_z(near_one, 1), live.far2, live.far3]
    live.input_grad = all_rows(live.input_own)
    del live.far2, live.far3, live.input_own
    live.q = [hop_z(live.q_far[0], 2), hop_z(live.q_far[1], 3)]
    del live.q_far
    live.fence()

    q_near = hold(q_near, live.q[0])
    q = [q_near[0], hop_z(q_near[1], 1), *live.q]
    layer_out, input_grad = live.layer_out, spread_rows(spots, live.input_grad)
    g_gate, g_up = unpack(at.zs, live.g, [(0, fw, 1), (fw, fw, 1)])
    g_down = live.g_down
    takes = [(0, qw, 1), (qw, kw, 2), (qw + kw, kw, 2), (qw + 2 * kw, qw, 1)]
    g_query, g_key, g_value, g_out = unpack(at.zs, q, takes)
    g_key, g_value = g_key.T, g_value.T
    tails = sum(p[:, 384:512].astype(F32) for p in q)
    tails = tails + at.hop_c(tails)
    entries = inputs.shape[0] * at.count * inputs.shape[1]
    rms = jnp.sqrt(tails[0, 98:101] / entries + EPS)
    return (
        layer_out,
        input_grad,
        g_query,
        g_key,
        g_value,
        g_out,
        g_gate,
        g_up,
        g_down,
        tails[:, 96],
        tails[:, 97],
        rms[0],
        rms[1],
        rms[2],
    )


def solution(mesh):
    devices = mesh.devices.reshape(PARTS, -1, 2, mesh.devices.shape[1] // 2)
    seq, mp = ("z", "y"), ("x", "c")
    rows, single, block = P(seq, None), P(seq), P(seq, mp)
    return jax.shard_map(
        on_device,
        mesh=Mesh(devices, AXES),
        in_specs=(rows, rows, single, single, single, single) + (block,) * 7,
        out_specs=(rows, rows) + (block,) * 7 + (single, single, P(), P(), P()),
        check_vma=False,
    )
```

```python
import functools

import jax
import jax.numpy as jnp
from jax import lax
from jax.experimental import pallas as pl
from jax.experimental.pallas import tpu as pltpu
from jax.sharding import Mesh
from jax.sharding import PartitionSpec as P

HEAD_DIM = 80
SPAN = 128
EPS = 1e-05
THETA = 1000000.0
PARTS = 4
BF = jnp.bfloat16
F32 = jnp.float32
FACTOR = HEAD_DIM**-0.5
LOG2E = 1.4426950408889634
LIMIT = 50 * 1024 * 1024

PLAIN = (((1,), (0,)), ((), ()))
LAST = (((1,), (1,)), ((), ()))
ROWS = (((0,), (0,)), ((), ()))

VM = pl.BlockSpec(memory_space=pltpu.VMEM)
SM = pl.BlockSpec(memory_space=pltpu.SMEM)
ANY = pl.BlockSpec(memory_space=pl.ANY)


def shape(dims, kind=BF):
    return jax.ShapeDtypeStruct(tuple(dims), kind)


def call(body, outs, in_specs, out_specs, scratch=(), cost=2):
    return pl.pallas_call(
        body,
        out_shape=outs,
        in_specs=in_specs,
        out_specs=out_specs,
        scratch_shapes=list(scratch),
        compiler_params=pltpu.CompilerParams(vmem_limit_bytes=LIMIT if cost > 4 else 16 * 1024 * 1024),
        cost_estimate=pl.CostEstimate(flops=cost * 10**9, bytes_accessed=0, transcendentals=0),
    )


AXES = ("z", "y", "x", "c")


def hop(value, axis, k):
    size = lax.axis_size(axis)
    return lax.ppermute(value, axis, [(i, i ^ k) for i in range(size)])


def dot(left, right, dims=PLAIN):
    return lax.dot_general(left, right, dims, preferred_element_type=F32)


def joined(values, width):
    values = [v.astype(F32) for v in values]
    have = sum(v.shape[1] for v in values)
    if have < width:
        values.append(jnp.zeros((values[0].shape[0], width - have), F32))
    return jnp.concatenate(values, axis=1).astype(BF)


def pack_body(takes, width, cut, z_ref, *refs):
    count = len(takes)
    ins, outs = refs[:count], refs[count:]
    for k in range(PARTS):
        part = z_ref[0] ^ k
        for j in range(PARTS):

            @pl.when(part == j)
            def _():
                values = [ref[:, pl.ds(step * (j // share), step)] for ref, (step, share) in zip(ins, takes)]
                value = joined(values, width)
                if cut and k >= 2:
                    outs[k][...] = value[:, :cut]
                    outs[k + 2][...] = value[:, cut:]
                else:
                    outs[k][...] = value


def pack(z, arrays, takes, width, cut=None):
    depth = arrays[0].shape[0]
    outs = [shape((depth, width))] * PARTS
    if cut:
        outs = outs[:2] + [shape((depth, cut))] * 2 + [shape((depth, width - cut))] * 2
    return call(
        functools.partial(pack_body, takes, width, cut),
        outs,
        [SM] + [VM] * len(arrays),
        [VM] * len(outs),
    )(z, *arrays)


def pack_attn_body(z_ref, wq, wk, wv, wo, gain_one, gain_two, *outs):
    depth, width = outs[0].shape
    kw = wk.shape[0] // 2
    qw = wq.shape[1] // PARTS
    narrow = jnp.concatenate([wk[...].astype(F32), wv[...].astype(F32)], axis=0)
    gains = jnp.concatenate([gain_one[...], gain_two[...]], axis=0).astype(F32)
    fill = jnp.zeros((128 - (4 * kw + 2) % 128, depth), F32)
    tall = jnp.concatenate([narrow, gains, fill], axis=0).T
    for k in range(PARTS):
        part = z_ref[0] ^ k
        for j in range(PARTS):

            @pl.when(part == j)
            def _():
                spot = pl.ds(qw * j, qw)
                h = j // 2
                values = [
                    wq[:, spot],
                    tall[:, kw * h : kw * h + kw],
                    tall[:, kw * (h + 2) : kw * (h + 3)],
                    wo[:, spot],
                    tall[:, 4 * kw : 4 * kw + 2],
                ]
                outs[k][...] = joined(values, width)


def pack_attn(z, wq, wk, wv, wo, gain_one, gain_two, width):
    depth = wq.shape[0]
    return call(
        pack_attn_body, [shape((depth, width))] * PARTS, [SM] + [VM] * 6, [VM] * PARTS
    )(z, wq, wk.T, wv.T, wo, gain_one.reshape(1, -1), gain_two.reshape(1, -1))


def unpack_body(takes, z_ref, *refs):
    ins, outs = refs[:PARTS], refs[PARTS:]
    for ref, (start, step, share) in zip(outs, takes):
        if share == 2:
            ref[...] = jnp.zeros_like(ref)
    depth = ins[0].shape[0]
    for k in range(PARTS):
        part = z_ref[0] ^ k
        flat = None
        if any(share == 2 for start, step, share in takes):
            first = min(start for start, step, share in takes if share == 2)
            last = max(start + step for start, step, share in takes if share == 2)
            fill = jnp.zeros((depth, -(last - first) % 128), F32)
            flat = jnp.concatenate([ins[k][:, pl.ds(first, last - first)].astype(F32), fill], axis=1).T
        for j in range(PARTS):

            @pl.when(part == j)
            def _():
                for ref, (start, step, share) in zip(outs, takes):
                    spot = pl.ds(step * (j // share), step)
                    if share == 1:
                        ref[:, spot] = ins[k][:, pl.ds(start, step)].astype(F32)
                    else:
                        ref[spot, :] += flat[start - first : start - first + step]


def unpack(z, pieces, takes):
    depth = pieces[0].shape[0]
    dims = [(depth, step * PARTS // share) for start, step, share in takes]
    dims = [d[::-1] if take[2] == 2 else d for d, take in zip(dims, takes)]
    return call(
        functools.partial(unpack_body, takes),
        [shape(d, F32) for d in dims],
        [SM] + [VM] * PARTS,
        [VM] * len(takes),
        cost=4,
    )(z, *pieces)


def spot_of(pos, k, j, inner, depth):
    return pl.ds(pl.multiple_of(((pos[1] ^ k) * inner + (pos[2] ^ j)) * depth, 16), depth)


def piece_copies(pos, inner, pieces, store, sem, i, lanes):
    half = inner // 2
    depth = store.shape[1] // (PARTS * inner)
    copies = []
    for k in range(PARTS):
        for j in range(inner):
            piece = pieces[2 * k + j // half].at[pl.ds((j % half) * depth, depth), lanes]
            n = (i * PARTS + k) * inner + j
            copies.append(
                pltpu.make_async_copy(piece, store.at[i, spot_of(pos, k, j, inner, depth)], sem.at[n])
            )
    return copies


def fetch(pos, inner, pieces, store, sem, start=0):
    lanes = pl.ds(start, store.shape[2])
    copies = [piece_copies(pos, inner, pieces[8 * i : 8 * i + 8], store, sem, i, lanes) for i in range(2)]
    return start_all(copies)


def start_all(copies):
    for half in copies:
        for c in half:
            c.start()

    def wait(i):
        for c in copies[i]:
            c.wait()

    return wait


def own_rows_body(pos, ids, x_ref, t_ref, x_out, t_out, tall):
    spot = pl.ds(pl.multiple_of(pos[0], 64), 64)
    width = x_ref.shape[1]
    tall[...] = jnp.broadcast_to(ids[...].astype(F32), tall.shape[::-1]).T
    x_out[:, :width] = x_ref[spot, :]
    x_out[:, width:] = tall[spot, :].astype(BF)
    t_out[...] = t_ref[spot, :]


def own_rows(pos, ids, x, t):
    rows, width = x.shape
    return call(
        own_rows_body,
        [shape((64, width + 128)), shape((64, width))],
        [SM] + [VM] * 3,
        [VM] * 2,
        [pltpu.VMEM((rows, 128), F32)],
    )(pos, ids, x, t)


def join_rows(pieces, out):
    n = pieces[0].shape[0]
    for i, ref in enumerate(pieces):
        out[pl.ds(i * n, n), :] = ref[:, : out.shape[1]]


def first_sum_body(mine, got, three):
    three[...] = (mine[...].astype(F32) + got[...].astype(F32)).astype(BF)


def first_sum(mine, got):
    return call(first_sum_body, shape(mine.shape), [VM] * 2, VM)(mine, got)


def second_sum_body(mine_one, mine_two, got, three, one, two):
    n = one.shape[0]
    one[...] = (mine_one[...].astype(F32) + got[pl.ds(n, n), :].astype(F32)).astype(BF)
    value = mine_two[...].astype(F32) + got[pl.ds(2 * n, n), :].astype(F32)
    two[...] = (value + three[...].astype(F32)).astype(BF)


def second_sum(mine, got, three):
    return call(second_sum_body, [shape(three.shape)] * 2, [VM] * 4, [VM] * 2)(
        mine[1], mine[2], got, three
    )


def last_sum(mine, got, one, two):
    first = mine[...].astype(F32) + got[pl.ds(0, mine.shape[0]), :].astype(F32)
    return first + one[...].astype(F32) + two[...].astype(F32)


def mean_scale(value):
    return lax.rsqrt(jnp.mean(value * value, axis=-1, keepdims=True) + EPS)


def back_norm(grad, value, gain):
    scale = mean_scale(value)
    unit = value * scale
    scaled = grad * gain
    return unit, scale * (scaled - unit * jnp.mean(scaled * unit, axis=-1, keepdims=True))


def after_attn_body(mine, got, one, two, x_own, gain, middle, n_own, total):
    branch = last_sum(mine, got, one, two)
    value = x_own[:, : branch.shape[1]].astype(F32) + branch
    middle[...] = value
    n_own[...] = (value * mean_scale(value) * gain[1:2, :]).astype(BF)
    total[...] = jnp.full(total.shape, jnp.sum(branch * branch), F32)


def after_mlp_body(mine, got, one, two, middle, target, d_own, out, total):
    branch = last_sum(mine, got, one, two)
    stream = middle[...] + branch
    d_own[...] = (stream - target[...].astype(F32)).astype(BF)
    out[...] = stream.astype(BF)
    total[0:8, :] = jnp.full((8, 128), jnp.sum(stream * stream), F32)
    total[8:16, :] = jnp.full((8, 128), jnp.sum(branch * branch), F32)


def after_feed_back_body(mine, got, one, two, middle, d_own, gain, d_middle, a_own, gain_grad):
    grad = last_sum(mine, got, one, two)
    unit, back = back_norm(grad, middle[...], gain[1:2, :])
    value = d_own[...].astype(F32) + back
    d_middle[...] = value
    a_own[...] = value.astype(BF)
    gain_grad[...] = jnp.sum(grad * unit, axis=0, keepdims=True)


def after_all_body(mine, got, one, two, x_own, d_middle, gain, out):
    grad = last_sum(mine, got, one, two)
    unit, back = back_norm(grad, x_own[:, : grad.shape[1]].astype(F32), gain[0:1, :])
    out[...] = (d_middle[...] + back).astype(BF)


def spread_rows_body(spots, p0, p1, p2, p3, out):
    n = p0.shape[0]
    for i, ref in enumerate((p0, p1, p2, p3)):
        out[pl.ds(pl.multiple_of(spots[i], 64), n), :] = ref[...]


def spread_rows(spots, pieces):
    n, width = pieces[0].shape
    return call(spread_rows_body, shape((4 * n, width)), [SM] + [VM] * 4, VM)(spots, *pieces)


def rotated(value, cosine, sine):
    half = HEAD_DIM // 2
    a, b = value[:, :half], value[:, half:]
    return jnp.concatenate([a * cosine - b * sine, b * cosine + a * sine], axis=1)


def project_body(qw, inner, pos, cosine, sine, *refs):
    x, w = refs[:8], refs[8:24]
    first, q_ref, kv_ref, gains, row_ids = refs[24:29]
    store, sem = refs[29:]
    wait = fetch(pos, inner, w, store, sem)
    width = first.shape[1]
    step = width // 4
    ids = jnp.concatenate([ref[:, width:] for ref in x], axis=0).astype(F32)
    row_ids[...] = ids.T[0:8, :]
    wait(0)
    spot = 480 - 384
    for p in range(4):
        tail = store[0, pl.ds(p * step, step), 384:512].astype(F32).T
        gains[:, pl.ds(p * step, step)] = tail[spot : spot + 8]
    gain = gains[0:1, :]
    rows = x[0].shape[0]
    for i, ref in enumerate(x):
        value = ref[:, :width].astype(F32)
        first[pl.ds(i * rows, rows), :] = (value * mean_scale(value) * gain).astype(BF)
    cos, sin = cosine[...], sine[...]
    queries, keys, values = [], [], []
    for i in range(2):
        if i:
            wait(1)
        out = dot(first[...], store[i, :, :384])
        for start in range(0, qw, HEAD_DIM):
            queries.append(rotated(out[:, start : start + HEAD_DIM], cos, sin))
        keys.append(rotated(out[:, qw : qw + HEAD_DIM], cos, sin))
        values.append(out[:, qw + HEAD_DIM : qw + 2 * HEAD_DIM])
    q_ref[...] = jnp.concatenate(queries, axis=1).astype(BF)
    kv_ref[...] = jnp.concatenate(keys + values + [ids[:, :64]], axis=1).astype(BF)


def sems(inner):
    return pltpu.SemaphoreType.DMA((2 * PARTS * inner,))


def project(pos, x, cosine, sine, w, qw, inner):
    rows, width = x[0].shape
    rows *= 8
    width -= 128
    return call(
        functools.partial(project_body, qw, inner),
        [
            shape((rows, width)),
            shape((rows, 2 * qw)),
            shape((rows, 384)),
            shape((8, width), F32),
            shape((8, rows), F32),
        ],
        [SM] + [VM] * 10 + [ANY] * 16,
        [VM] * 5,
        [pltpu.VMEM((2, width, 512), BF), sems(inner)],
        cost=12,
    )(pos, cosine, sine, *x, *w)


def out_rows(partial, outs):
    n = outs[0].shape[0]
    spots = [(i * n, n) for i in range(4)] + [(7 * n, n), (4 * n, 3 * n)]
    for (start, size), ref in zip(spots, outs):
        ref[...] = partial[start : start + size].astype(ref.dtype)


def row_shapes(rows, width):
    return [shape((rows, width))] * 5 + [shape((3 * rows, width))]


def each(count, step, start):
    if count <= 2:
        for s in range(count):
            start = step(s, start)
        return start
    return lax.fori_loop(0, count, step, start)


def reader(kvs, rows):
    def read(s, lane):
        if len(kvs) > 1:
            return kvs[s][:, lane]
        return kvs[0][pl.ds(pl.multiple_of(s * rows, rows), rows), lane]

    return read


def lanes(i):
    return pl.ds(i * HEAD_DIM, HEAD_DIM)


ID_LANE = pl.ds(4 * HEAD_DIM, 1)


def attend_body(sides, pos, q_ref, row_ids, *refs):
    arrays = sides if sides <= 2 else 1
    kvs, refs = refs[:arrays], refs[arrays:]
    w = refs[:16]
    mixed = refs[16:18]
    lse, sides_out = refs[18], refs[19:25]
    store, sem = refs[25:]
    wait = fetch(pos, sides, w, store, sem, 256)
    rows = q_ref.shape[0]
    qw = q_ref.shape[1] // 2
    ids = row_ids[0:1, :]
    read = reader(kvs, rows)

    def look(s):
        return read(s, ID_LANE).astype(F32) <= ids

    looks = [look(s) for s in range(sides)] if sides <= 2 else None
    lse[...] = jnp.zeros_like(lse)
    head = 0
    c = FACTOR * LOG2E
    for i in range(2):
        outs = []
        for start in range(i * qw, (i + 1) * qw, HEAD_DIM):
            q = q_ref[:, start : start + HEAD_DIM]

            def score(s):
                seen = looks[s] if looks else look(s)
                return jnp.where(seen, dot(read(s, lanes(i)), q, LAST), -1e30)

            scores = [score(s) for s in range(sides)] if sides <= 2 else None

            def highest(s, top):
                value = scores[s] if scores else score(s)
                return jnp.maximum(top, jnp.max(value, axis=0, keepdims=True))

            top = each(sides, highest, jnp.full((1, rows), -1e30, F32))

            def gathered(s, carry):
                total, out = carry
                value = scores[s] if scores else score(s)
                p = jnp.exp2(value * c - top * c)
                total = total + jnp.sum(p, axis=0, keepdims=True)
                return total, out + dot(read(s, lanes(2 + i)), p.astype(BF), ROWS)

            nothing = (jnp.zeros((1, rows), F32), jnp.zeros((HEAD_DIM, rows), F32))
            total, out = each(sides, gathered, nothing)
            outs.append(out / total)
            lse[head : head + 1, :] = top * c + jnp.log2(total)
            head += 1
        fill = jnp.zeros((512 - 320 - qw, rows), F32)
        tall = jnp.concatenate([jnp.zeros((64, rows), F32)] + outs + [fill], axis=0)
        mixed[i][...] = tall.T.astype(BF)
    for i in range(2):
        wait(i)
    partial = dot(mixed[0][...], store[0], LAST) + dot(mixed[1][...], store[1], LAST)
    out_rows(partial, sides_out)


def attend(pos, q, kvs, row_ids, w, sides):
    rows = q.shape[0]
    width = 8 * w[0].shape[0]
    return call(
        functools.partial(attend_body, sides),
        [shape((rows, 256))] * 2
        + [shape((8, rows), F32)]
        + row_shapes(rows // 8, width),
        [SM] + [VM] * (2 + len(kvs)) + [ANY] * 16,
        [VM] * 9,
        [pltpu.VMEM((2, width, 256), BF), sems(sides)],
        cost=12,
    )(pos, q, row_ids, *kvs, *w)


def padded(value, width):
    return jnp.concatenate([value, jnp.zeros((value.shape[0], width - value.shape[1]), value.dtype)], axis=1)


def block_copies(pos, inner, arrays, store, sem, i):
    depth = arrays[1].shape[1]
    half = inner // 2
    cut = arrays[2].shape[1]
    copies = [[], []]
    for k in range(PARTS):
        for j in range(inner):
            n = (i * PARTS + k) * inner + j
            if k < 3:
                row = pl.ds(pl.multiple_of(((pos[1] ^ k) * inner + j) * depth, 16), depth)
                for late in range(2):
                    lane = pl.ds(cut, store.shape[2] - cut) if late else pl.ds(0, cut)
                    spot = arrays[k // 2].at[j * 2 + (pos[3] ^ i), pl.ds(depth if k == 1 else 0, depth), lane]
                    to = store.at[i, row, lane]
                    copies[late].append(pltpu.make_async_copy(spot, to, sem.at[late, n]))
                continue
            for late in range(2):
                piece = arrays[2 + 4 * late + 2 * i + j // half]
                lane = pl.ds(cut * late, piece.shape[1])
                to = store.at[i, spot_of(pos, k, j, inner, depth), lane]
                spot = piece.at[pl.ds((j % half) * depth, depth)]
                copies[late].append(pltpu.make_async_copy(spot, to, sem.at[late, n]))
    return copies


def feed_body(fw, inner, pos, *refs):
    n, blocks = refs[:8], refs[8:18]
    hidden, slope, silu = refs[18:20], refs[20:22], refs[22:24]
    rows_out, outs = refs[24], refs[25:31]
    rows_in, kept, store, sem, out_sem = refs[31:]
    copies = [block_copies(pos, inner, blocks, store, sem, i) for i in range(2)]
    wait = start_all([copies[0][0], copies[1][0], copies[0][1] + copies[1][1]])
    join_rows(n, rows_in)
    saves = [pltpu.make_async_copy(rows_in, rows_out, out_sem.at[6])]
    saves[0].start()
    for i in range(2):
        wait(i)
        out = dot(rows_in[...], store[i, :, : 2 * fw])
        gate, upper = out[:, :fw], out[:, fw:]
        sigma = jax.nn.sigmoid(gate)
        act = gate * sigma
        values = (act * upper, upper * (sigma + act * (1.0 - sigma)), act)
        for n, (value, to) in enumerate(zip(values, (hidden, slope, silu))):
            kept[2 * n + i] = padded(value, 512).astype(BF)
            saves.append(pltpu.make_async_copy(kept.at[2 * n + i], to[i], out_sem.at[2 * n + i]))
            saves[-1].start()
    wait(2)
    out_rows(
        dot(kept[0], store[0, :, 2 * fw :], LAST) + dot(kept[1], store[1, :, 2 * fw :], LAST),
        outs,
    )
    for c in saves:
        c.wait()


def feed(pos, n, w, fw, inner):
    rows, width = n[0].shape
    return call(
        functools.partial(feed_body, fw, inner),
        [shape((8 * rows, 512))] * 6 + [shape((8 * rows, width))] + row_shapes(rows, width),
        [SM] + [VM] * 8 + [ANY] * 10,
        [ANY] * 7 + [VM] * 6,
        [
            pltpu.VMEM((8 * rows, width), BF),
            pltpu.VMEM((6, 8 * rows, 512), BF),
            pltpu.VMEM((2, width, 2 * fw + 512), BF),
            pltpu.SemaphoreType.DMA((2, 2 * PARTS * inner)),
            pltpu.SemaphoreType.DMA((7,)),
        ],
        cost=18,
    )(pos, *n, *w)


def feed_back_body(fw, inner, pos, rows_in, *refs):
    slope, silu = refs[0:2], refs[2:4]
    blocks = refs[4:14]
    d_gu, outs = refs[14:16], refs[16:22]
    kept, store, sem, out_sem = refs[22:]
    copies = [block_copies(pos, inner, blocks, store, sem, i) for i in range(2)]
    wait = start_all([copies[0][1], copies[1][1], copies[0][0] + copies[1][0]])
    saves = []
    for i in range(2):
        wait(i)
        out = dot(rows_in[...], store[i, :, 2 * fw :])
        a = (out * slope[i][...].astype(F32))[:, :fw]
        b = (out * silu[i][...].astype(F32))[:, :fw]
        kept[i] = jnp.concatenate([a, b], axis=1).astype(BF)
        saves.append(pltpu.make_async_copy(kept.at[i], d_gu[i], out_sem.at[i]))
        saves[-1].start()
    wait(2)
    out_rows(
        dot(kept[0], store[0, :, : 2 * fw], LAST) + dot(kept[1], store[1, :, : 2 * fw], LAST),
        outs,
    )
    for c in saves:
        c.wait()


def feed_back(pos, d, slope, silu, w, fw, inner):
    rows, width = d.shape
    return call(
        functools.partial(feed_back_body, fw, inner),
        [shape((rows, 2 * fw))] * 2 + row_shapes(rows // 8, width),
        [SM] + [VM] * 5 + [ANY] * 10,
        [ANY] * 2 + [VM] * 6,
        [
            pltpu.VMEM((2, rows, 2 * fw), BF),
            pltpu.VMEM((2, width, 2 * fw + 512), BF),
            pltpu.SemaphoreType.DMA((2, 2 * PARTS * inner)),
            pltpu.SemaphoreType.DMA((2,)),
        ],
        cost=16,
    )(pos, d, *slope, *silu, *w)


def features(pos, k, step):
    return pl.ds(pl.multiple_of((pos[1] ^ k) * step, 128), step)


def block_grad_body(inner, parts, pos, left, right_a, right_b, out, store, sem):
    step = store.shape[1] // len(parts)
    depth = step // inner
    copies = []
    for p, k in enumerate(parts):
        spot = features(pos, k, step)
        for i, right in enumerate((right_a, right_b)):
            store[i, pl.ds(p * step, step), :] = dot(left[:, spot], right[...], ROWS).astype(BF)
            for j in range(inner):
                n = p * inner + j
                copies.append(
                    pltpu.make_async_copy(
                        store.at[i, pl.ds(n * depth, depth)],
                        out.at[j * 2 + (pos[3] ^ i), pl.ds(p * depth, depth)],
                        sem.at[i * len(parts) * inner + n],
                    )
                )
                copies[-1].start()
    for c in copies:
        c.wait()


def down_grad_body(inner, pos, *refs):
    pieces, right, out, rows_in, store, sem = refs[:8], refs[8:10], *refs[10:]
    join_rows(pieces, rows_in)
    block_grad_body(inner, range(PARTS), pos, rows_in, *right, out, store, sem)


def down_grad(pos, pieces, right, inner):
    rows, width = pieces[0].shape
    rows *= 8
    cols = right[0].shape[1]
    return call(
        functools.partial(down_grad_body, inner),
        [shape((inner * 2, width // inner, cols)), shape((rows, width))],
        [SM] + [VM] * 10,
        [ANY, VM],
        [pltpu.VMEM((2, width, cols), BF), sems(inner)],
        cost=7,
    )(pos, *pieces, *right)


def block_grad(pos, left, right, inner, parts):
    rows, width = left.shape
    cols = right[0].shape[1]
    held = width // PARTS * len(parts)
    return call(
        functools.partial(block_grad_body, inner, parts),
        shape((inner * 2, held // inner, cols)),
        [SM] + [VM] * 3,
        ANY,
        [pltpu.VMEM((2, held, cols), BF), sems(inner)],
        cost=7,
    )(pos, left, *right)


def attend_back_body(sides, pos, q_ref, row_ids, lse, cosine, sine, *refs):
    arrays = sides if sides <= 2 else 1
    d, refs = refs[:8], refs[8:]
    kvs, refs = refs[:arrays], refs[arrays:]
    w = refs[:16]
    dq_ref, own_ref, send_ref, rows_in = refs[16:20]
    store, mix, d_kv, sem = refs[20:]
    join_rows(d, rows_in)
    wait = fetch(pos, sides, w, store, sem, 256)
    rows = q_ref.shape[0]
    qw = q_ref.shape[1] // 2
    for i in range(2):
        wait(i)
        mix[i] = dot(rows_in[...], store[i])[:, 64 : 64 + qw].astype(BF)
    ids = row_ids[0:1, :]
    read = reader(kvs, rows)

    def look(s):
        return read(s, ID_LANE).astype(F32) <= ids

    looks = [look(s) for s in range(sides)] if sides <= 2 else None
    d_q = []
    c = FACTOR * LOG2E
    head = 0
    for i in range(2):
        for start in range(0, qw, HEAD_DIM):
            q = q_ref[:, i * qw + start : i * qw + start + HEAD_DIM]
            dm = mix[i, :, start : start + HEAD_DIM]
            level = lse[head : head + 1, :]
            head += 1

            def pair(s):
                seen = looks[s] if looks else look(s)
                p = jnp.where(seen, jnp.exp2(dot(read(s, lanes(i)), q, LAST) * c - level), 0.0)
                return p, dot(read(s, lanes(2 + i)), dm, LAST)

            held = [pair(s) for s in range(sides)] if sides <= 2 else None

            def weigh(s, delta):
                p, dp = held[s] if held else pair(s)
                return delta + jnp.sum(p * dp, axis=0, keepdims=True)

            delta = each(sides, weigh, jnp.zeros((1, rows), F32))

            def grads(s, out):
                p, dp = held[s] if held else pair(s)
                ds = (p * (dp - delta)).astype(BF)
                d_value = dot(p.astype(BF), dm)
                d_key = dot(ds, q)
                if start == 0:
                    d_kv[2 + i, s] = d_value
                    d_kv[i, s] = d_key
                else:
                    d_kv[2 + i, s] += d_value
                    d_kv[i, s] += d_key
                return out + dot(read(s, lanes(i)), ds, ROWS)

            d_q.append(each(sides, grads, jnp.zeros((HEAD_DIM, rows), F32)))
    tall = jnp.concatenate(d_q + [jnp.zeros((512 - 4 * HEAD_DIM, rows), F32)], axis=0).T * FACTOR
    cos, sin = cosine[...], sine[...]
    dq_ref[...] = jnp.concatenate(
        [rotated(tall[:, h * HEAD_DIM : (h + 1) * HEAD_DIM], cos, -sin) for h in range(4)], axis=1
    ).astype(BF)
    for s in range(sides):
        value = jnp.concatenate([d_kv[0, s] * FACTOR, d_kv[1, s] * FACTOR, d_kv[2, s], d_kv[3, s]], axis=1)
        if s == 0:
            own_ref[...] = value
        else:
            send_ref[pl.ds((s - 1) * rows, rows), :] = value.astype(BF)


def attend_back(pos, d, q, kvs, row_ids, lse, cosine, sine, w, sides):
    rows = q.shape[0]
    width = d[0].shape[1]
    cols = 4 * HEAD_DIM
    return call(
        functools.partial(attend_back_body, sides),
        [shape(q.shape), shape((rows, cols), F32), shape(((sides - 1) * rows, cols)), shape((rows, width))],
        [SM] + [VM] * (13 + len(kvs)) + [ANY] * 16,
        [VM] * 4,
        [
            pltpu.VMEM((2, width, 256), BF),
            pltpu.VMEM((2, rows, q.shape[1] // 2), BF),
            pltpu.VMEM((4, sides, rows, HEAD_DIM), F32),
            sems(sides),
        ],
        cost=18,
    )(pos, q, row_ids, lse, cosine, sine, *d, *kvs, *w)


def split_body(dq_ref, own_ref, got_ref, cosine, sine, *d_qkv):
    qw = dq_ref.shape[1] // 2
    cos, sin = cosine[...], sine[...]
    d_kv = own_ref[...] + got_ref[...].astype(F32)
    d_q = dq_ref[...].astype(F32)
    for i in range(2):
        d_k = rotated(d_kv[:, i * HEAD_DIM : (i + 1) * HEAD_DIM], cos, -sin)
        d_v = d_kv[:, (2 + i) * HEAD_DIM : (3 + i) * HEAD_DIM]
        d_qkv[i][...] = padded(
            jnp.concatenate([d_q[:, i * qw : (i + 1) * qw], d_k, d_v], axis=1), 384
        ).astype(BF)


def split_grads(dq, own, got, cosine, sine):
    rows = dq.shape[0]
    return call(split_body, [shape((rows, 384))] * 2, [VM] * 5, [VM] * 2)(dq, own, got, cosine, sine)


def project_back_body(inner, pos, d_a, d_b, *refs):
    w, outs = refs[:16], refs[16:22]
    store, sem = refs[22:]
    wait = fetch(pos, inner, w, store, sem)
    for i in range(2):
        wait(i)
    out_rows(dot(d_a[...], store[0], LAST) + dot(d_b[...], store[1], LAST), outs)


def project_back(pos, d_qkv, w, inner):
    rows = d_qkv[0].shape[0] // 8
    width = 8 * w[0].shape[0]
    return call(
        functools.partial(project_back_body, inner),
        row_shapes(rows, width),
        [SM] + [VM] * 2 + [ANY] * 16,
        [VM] * 6,
        [pltpu.VMEM((2, width, 384), BF), sems(inner)],
        cost=8,
    )(pos, *d_qkv, *w)


def pair_copies(pos, inner, far, near, store, sem, i):
    half = inner // 2
    depth = store.shape[1] // (PARTS * inner)
    copies = []
    for k in range(PARTS):
        for j in range(inner):
            if k >= 2:
                to = far[j // half].at[pl.ds(((k % 2) * half + j % half) * depth, depth)]
            else:
                to = near.at[(pos[2] ^ j) * 2 + (pos[3] ^ i), pl.ds(k * depth, depth)]
            n = (i * PARTS + k) * inner + j
            copies.append(
                pltpu.make_async_copy(store.at[i, spot_of(pos, k, j, inner, depth)], to, sem.at[n])
            )
    return copies


def attn_grad_body(inner, pos, first, d_all, gain_two, sum_attn, sums, *refs):
    d_qkv, mixed = refs[:2], refs[2:4]
    w, outs, near = refs[4:20], refs[20:24], refs[24]
    held, store, sem, out_sem = refs[25:]
    wait = fetch(pos, inner, w, held, sem)
    step = store.shape[1] // PARTS
    copies = [pair_copies(pos, inner, outs[2 * i : 2 * i + 2], near, store, out_sem, i) for i in range(2)]
    lane = lax.broadcasted_iota(jnp.int32, (1, 128), 1)
    tail = jnp.where(lane == 98, sums[0:1, :], 0.0)
    tail = jnp.where(lane == 99, sum_attn[0:1, :], tail)
    tail = jnp.where(lane == 100, sums[8:9, :], tail)
    for k in (3, 2, 1, 0):
        spot = features(pos, k, step)
        rows = [jnp.zeros((97, step), F32), gain_two[0:1, spot], jnp.zeros((30, step), F32)]
        tall = jnp.concatenate(rows, axis=0).T + tail
        values = [dot(first[:, spot], d_qkv[i][...], ROWS) for i in range(2)]
        others = [dot(d_all[:, spot], mixed[i][...], ROWS) for i in range(2)]
        if k == 3:
            wait(0)
            wait(1)
        gain = 0.0
        for i in range(2):
            gain = gain + jnp.sum(values[i] * held[i, spot, :384].astype(F32), axis=1, keepdims=True)
        gain = gain / held[0, spot, 480:481].astype(F32)
        tall = tall + jnp.where(lane == 96, gain, 0.0)
        for i in range(2):
            store[i, spot, :256] = values[i][:, :256].astype(BF)
            store[i, spot, 256:384] = (values[i][:, 256:] + others[i][:, :128]).astype(BF)
            store[i, spot, 384:] = (others[i][:, 128:] + tall).astype(BF)
            for c in copies[i][k * inner : (k + 1) * inner]:
                c.start()
    for i in range(2):
        for c in copies[i]:
            c.wait()


def attn_grad(pos, first, d_all, gain_two, sum_attn, sums, d_qkv, mixed, w, inner):
    rows, width = first.shape
    return call(
        functools.partial(attn_grad_body, inner),
        [shape((width // 4, 512))] * 4 + [shape((inner * 2, width // (2 * inner), 512))],
        [SM] + [VM] * 9 + [ANY] * 16,
        [ANY] * 5,
        [pltpu.VMEM((2, width, 512), BF), pltpu.VMEM((2, width, 512), BF), sems(inner), sems(inner)],
        cost=12,
    )(pos, first, d_all, gain_two, sum_attn, sums, *d_qkv, *mixed, *w)


def hold(values, *others):
    got = lax.optimization_barrier(tuple(values) + tuple(others))
    return list(got[: len(values)])


class Live:
    def fence(self):
        names = sorted(self.__dict__)
        leaves, tree = jax.tree.flatten([self.__dict__[n] for n in names])
        leaves = lax.optimization_barrier(tuple(leaves))
        self.__dict__.update(zip(names, jax.tree.unflatten(tree, leaves)))


class Place:
    def __init__(self):
        self.inner = lax.axis_size("y")
        self.count = PARTS * self.inner
        self.z, self.y, self.x, self.c = [lax.axis_index(name) for name in AXES]
        self.s = self.z * self.inner + self.y
        self.zs = self.z.reshape(1).astype(jnp.int32)
        self.bits = []
        b = 1
        while b < self.inner:
            self.bits.append(b)
            b *= 2

    def hop_z(self, v, k):
        return hop(v, "z", k)

    def hop_y(self, v, b):
        return hop(v, "y", b)

    def hop_x(self, v):
        return hop(v, "x", 1)

    def hop_c(self, v):
        return hop(v, "c", 1)

    def low_y(self, v):
        for b in self.bits[:-1]:
            v = jnp.concatenate([v, self.hop_y(v, b)], 0)
        return v

    def far_y(self, v):
        return self.hop_y(v, self.bits[-1])

    def add(self, own, got):
        return (own.astype(F32) + got.astype(F32)).astype(BF)

    def halves(self, own, got):
        n = own.shape[0] // 2
        return [self.add(own[:n], got[:n]), self.add(own[n:], got[n:])]

    def sum_y(self, own, far):
        value = self.add(own, self.far_y(far))
        for b in reversed(self.bits[:-1]):
            n = value.shape[0] // 2
            value = self.add(value[:n], self.hop_y(value[n:], b))
        return value

    def sum_x(self, own, other):
        return self.add(own, self.hop_x(other))

    def gather(self, own):
        mine = [own, self.hop_z(own, 1), self.hop_z(own, 2)]
        mine.append(self.hop_z(mine[2], 1))
        return mine + [self.hop_c(v) for v in mine]

    def scatter_one(self, outs):
        mine = list(outs[:4])
        last, rest = [self.hop_c(v) for v in outs[4:]]
        one, two = second_sum(mine, rest, self.hop_z(first_sum(mine[3], last), 1))
        return [mine[0], rest, one, two]

    def scatter_two(self, left):
        return left[0], left[1], self.hop_z(left[2], 1), self.hop_z(left[3], 2)

    def scatter(self, outs):
        return self.scatter_two(self.scatter_one(outs))


def tables(place):
    half = HEAD_DIM // 2
    freq = THETA ** (-(jnp.arange(half, dtype=F32) * 2.0 / HEAD_DIM))
    angle = place[:, None] * freq[None, :]
    return (jnp.cos(angle), jnp.sin(angle))


def on_device(
    inputs,
    targets,
    seq_ids,
    block_ids,
    attn_gain,
    mlp_gain,
    w_query,
    w_key,
    w_value,
    w_out,
    w_gate,
    w_up,
    w_down,
):
    at = Place()
    inner = at.inner
    full = inputs.shape[1]
    half_span = SPAN // 2
    kw = w_key.shape[1] // 2
    qw = w_query.shape[1] // PARTS
    fw = w_gate.shape[1] // PARTS
    row_f32 = shape((half_span, full), F32)
    row_bf = shape((half_span, full))

    off = jnp.where(seq_ids[0] == at.x, 0, SPAN)
    pos = jnp.stack([off + at.c * half_span, at.z, at.y, at.x, at.c]).astype(jnp.int32)
    spots = [
        (off if xr == 0 else SPAN - off) + (at.c ^ cr) * half_span for xr in range(2) for cr in range(2)
    ]
    spots = jnp.stack(spots).astype(jnp.int32)

    def all_rows(own):
        across = at.hop_x(own)
        return [own, at.hop_c(own), across, at.hop_c(across)]

    rows = 2 * PARTS * half_span
    count = jnp.arange(rows, dtype=jnp.int32)
    zz = at.z ^ ((count // half_span) % PARTS)
    cc = at.c ^ (count // (half_span * PARTS))
    place = ((zz * inner + at.y) * SPAN + cc * half_span + count % half_span).astype(F32)
    cosine, sine = tables(place)

    def listed(w):
        return [v for i in range(2) for k in range(PARTS) for v in w[k][i]]

    def gather_blocks(pair):
        return lax.all_gather(pair, ("y", "x"), axis=0)

    def scatter_blocks(blocks, count):
        blocks = blocks.reshape(-1, blocks.shape[-1])
        got = lax.psum_scatter(blocks, ("y", "x"), scatter_dimension=0, tiled=True)
        n = got.shape[0] // count
        return [got[k * n : (k + 1) * n] for k in range(count)]

    hop_x, hop_z, low_y, far_y = at.hop_x, at.hop_z, at.low_y, at.far_y
    live = Live()
    live.w = [w_gate, w_up, w_down]
    live.rows = [inputs, targets]
    live.qo = pack_attn(at.zs, w_query, w_key, w_value, w_out, attn_gain, mlp_gain, 512)
    live.fence()

    q = live.qo
    z = [q[0]] + [hop_z(q[k], k) for k in range(1, PARTS)]
    live.x_own, live.t_own = own_rows(pos, block_ids.reshape(1, -1), *live.rows)
    live.g = list(pack(at.zs, live.w, [(fw, 1)] * 3, 2 * fw + 512, 2 * fw))
    del live.w, live.rows
    live.g[1] = hop_z(hold([live.g[1]], z[1])[0], 1)
    v = low_y(z[0])
    w = far_y(v)
    live.q0 = (v, w, hop_x(v))
    live.q1 = (low_y(z[1]), low_y(hop_x(z[1])))
    live.z = z[2:]
    live.fence()

    near = gather_blocks(jnp.concatenate(live.g[:2], 0))
    v, w, u = live.q0
    q0 = ((v, w), (u, hop_x(w)))
    v, u = live.q1
    q1 = ((v, far_y(v)), (u, far_y(u)))
    v = low_y(live.z[0])
    w = far_y(v)
    q2 = ((v, w), (hop_x(v), hop_x(w)))
    u, v = low_y(hop_x(live.z[1])), low_y(live.z[1])
    q3 = ((v, far_y(v)), (u, far_y(u)))
    live.x_all = at.gather(live.x_own)
    live.w_qo = listed([q0, q1, q2, q3])
    live.g[2] = hop_z(live.g[2], 2)
    del live.z, live.q0, live.q1
    live.fence()

    live.first, live.query, kv, live.gain, live.row_ids = project(
        pos, live.x_all, cosine, sine, live.w_qo, qw, inner
    )
    live.kvs = [kv]
    live.g[4] = hop_z(live.g[4], 2)
    live.fence()

    g2 = gather_blocks(jnp.concatenate([live.g[2], live.g[4]], 1))

    kvs = live.kvs
    for b in at.bits:
        kvs = kvs + [at.hop_y(v, b) for v in kvs]
    if inner > 2:
        kvs = [jnp.concatenate(kvs, 0)]
    live.kvs = kvs
    mixed_a, mixed_b, live.lse, *live.outs = attend(
        pos, live.query, kvs, live.row_ids, live.w_qo, inner
    )
    live.mixed = (mixed_a, mixed_b)
    live.g[3] = hop_z(live.g[3], 3)
    live.w_near = near
    live.fence()

    live.left = at.scatter_one(live.outs)
    live.g[5] = hop_z(live.g[5], 3)
    v = low_y(live.g[3])
    live.g3 = (v, far_y(v), low_y(hop_x(live.g[3])))
    del live.outs
    live.fence()

    v, w, u = live.g3
    live.g3 = [v, w, u, far_y(u)]
    v = low_y(live.g[5])
    w = far_y(v)
    live.g3 += [v, w, hop_x(v), hop_x(w)]
    del live.g
    live.middle, n_own, live.sum_attn = call(
        after_attn_body,
        [row_f32, row_bf, shape((8, 128), F32)],
        [VM] * 6,
        [VM] * 3,
    )(*at.scatter_two(live.left), live.x_own, live.gain)
    live.n_all = at.gather(n_own)
    live.w_two = g2
    del live.left
    live.fence()

    live.w_ff = [live.w_near, live.w_two, *live.g3]
    del live.w_near, live.w_two, live.g3
    out = feed(pos, live.n_all, live.w_ff, fw, inner)
    live.hidden, live.slope, live.silu = out[:2], out[2:4], out[4:6]
    live.n_all, outs = out[6], out[7:]
    live.d_own, live.layer_own, live.sums = call(
        after_mlp_body,
        [row_bf, row_bf, shape((16, 128), F32)],
        [VM] * 6,
        [VM] * 3,
    )(*at.scatter(outs), live.middle, live.t_own)
    del live.t_own
    live.fence()

    live.d_rows = at.gather(live.d_own)
    live.layer_out = all_rows(live.layer_own)
    del live.layer_own
    live.fence()


    live.grad_d, live.d_rows = down_grad(pos, live.d_rows, live.hidden, inner)
    live.fence()

    d = scatter_blocks(live.grad_d, 4)
    out = feed_back(pos, live.d_rows, live.slope, live.silu, live.w_ff, fw, inner)
    live.d_gu, live.outs = out[:2], out[2:]
    del live.slope, live.silu, live.w_ff, live.d_rows, live.hidden, live.grad_d
    live.fence()

    live.left = at.scatter_one(live.outs)
    del live.outs
    live.far = block_grad(pos, live.n_all, live.d_gu, inner, (2, 3))
    live.fence()

    far = scatter_blocks(live.far, 2)
    live.d_middle, live.a_own, live.grad_gain_two = call(
        after_feed_back_body,
        [row_f32, row_bf, shape((1, full), F32)],
        [VM] * 7,
        [VM] * 3,
    )(*at.scatter_two(live.left), live.middle, live.d_own, live.gain)
    del live.middle, live.d_own, live.left, live.far
    live.near = block_grad(pos, live.n_all, live.d_gu, inner, (0, 1))
    del live.n_all, live.d_gu
    live.fence()

    near = scatter_blocks(live.near, 2)
    live.a_all = at.gather(live.a_own)
    del live.a_own, live.near
    live.fence()

    live.d_query, live.d_kv, live.sent, live.a_all = attend_back(
        pos, live.a_all, live.query, live.kvs, live.row_ids, live.lse, cosine, sine, live.w_qo, inner
    )
    del live.query, live.kvs, live.row_ids, live.lse
    live.d = [d[0], hop_z(d[1], 1), d[2], hop_z(d[3], 3)]
    live.fence()

    d_kv, sent = live.d_kv, live.sent
    if inner > 2:
        sent = jnp.concatenate([d_kv, sent.astype(F32)], 0)
        for b in reversed(at.bits[1:]):
            n = sent.shape[0] // 2
            sent = sent[:n] + at.hop_y(sent[n:].astype(BF), b).astype(F32)
        d_kv, sent = sent[:rows], sent[rows:].astype(BF)
    sent = at.hop_y(sent, at.bits[0])
    live.d_qkv = split_grads(live.d_query, d_kv, sent, cosine, sine)
    live.d[2] = hop_z(live.d[2], 2)
    del live.d_kv, live.sent, live.d_query
    live.fence()

    tails = (live.grad_gain_two, live.sum_attn, live.sums)
    q = attn_grad(pos, live.first, live.a_all, *tails, live.d_qkv, live.mixed, live.w_qo, inner)
    live.q_far, live.q_near = (q[0:2], q[2:4]), q[4]
    live.far3 = hop_z(far[1], 3)
    del live.first, live.a_all, live.mixed
    del live.grad_gain_two, live.sum_attn, live.sums
    live.fence()

    live.left = at.scatter_one(project_back(pos, live.d_qkv, live.w_qo, inner))
    del live.d_qkv, live.w_qo
    q_near, q_far = scatter_blocks(live.q_near, 2), live.q_far
    del live.q_near, live.q_far
    (a, b), (c, d) = q_far
    q_far, last = at.sum_x(a, c), at.sum_x(b, d)
    if inner == 2:
        q_far = at.halves(q_far, at.far_y(last))
    else:
        q_far = jnp.split(at.sum_y(q_far, last), 2)
    far2 = hop_z(far[0], 2)
    live.fence()

    (live.input_own,) = call(
        after_all_body,
        [row_bf],
        [VM] * 7,
        [VM],
    )(*at.scatter_two(live.left), live.x_own, live.d_middle, live.gain)
    del live.left, live.x_own, live.d_middle
    live.q_far, live.far2 = q_far, far2
    (live.g_down,) = unpack(at.zs, live.d, [(0, fw, 1)])
    live.layer_out = spread_rows(spots, live.layer_out)
    del live.d
    live.fence()

    near_own, near_one = hold(near, live.input_own)
    live.g = [near_own, hop_z(near_one, 1), live.far2, live.far3]
    live.input_grad = all_rows(live.input_own)
    del live.far2, live.far3, live.input_own
    live.q = [hop_z(live.q_far[0], 2), hop_z(live.q_far[1], 3)]
    del live.q_far
    live.fence()

    q_near = hold(q_near, live.q[0])
    q = [q_near[0], hop_z(q_near[1], 1), *live.q]
    layer_out, input_grad = live.layer_out, spread_rows(spots, live.input_grad)
    g_gate, g_up = unpack(at.zs, live.g, [(0, fw, 1), (fw, fw, 1)])
    g_down = live.g_down
    takes = [(0, qw, 1), (qw, kw, 2), (qw + kw, kw, 2), (qw + 2 * kw, qw, 1)]
    g_query, g_key, g_value, g_out = unpack(at.zs, q, takes)
    g_key, g_value = g_key.T, g_value.T
    tails = sum(p[:, 384:512].astype(F32) for p in q)
    tails = tails + at.hop_c(tails)
    entries = inputs.shape[0] * at.count * inputs.shape[1]
    rms = jnp.sqrt(tails[0, 98:101] / entries + EPS)
    return (
        layer_out,
        input_grad,
        g_query,
        g_key,
        g_value,
        g_out,
        g_gate,
        g_up,
        g_down,
        tails[:, 96],
        tails[:, 97],
        rms[0],
        rms[1],
        rms[2],
    )


def solution(mesh):
    devices = mesh.devices.reshape(PARTS, -1, 2, mesh.devices.shape[1] // 2)
    seq, mp = ("z", "y"), ("x", "c")
    rows, single, block = P(seq, None), P(seq), P(seq, mp)
    return jax.shard_map(
        on_device,
        mesh=Mesh(devices, AXES),
        in_specs=(rows, rows, single, single, single, single) + (block,) * 7,
        out_specs=(rows, rows) + (block,) * 7 + (single, single, P(), P(), P()),
        check_vma=False,
    )
```
